32 devices in a mesh: blk: 8 (over z, y), group: 4 (over x, core).
Axes of the slice: x: 2, y: 2, z: 4, core: 2. Of those that a mesh axis runs over, the one named last changes fastest.
Arguments:
- vertex_matrix: bfloat16 [32, 1152, 1152], P(('blk', 'group')), may hold values from -0.1875 to 0.1875
- vertex_site: int32 [32, 1152], P(('blk', 'group')), may hold values from 0 to 15
- vertex_time: int32 [32, 1152], P(('blk', 'group')), may hold values from 0 to 1023
- vertex_spin: int32 [32, 1152], P(('blk', 'group')), may hold values from 0 to 1
- free_green: float32 [2, 128], replicated, may hold values from -3 to 3
- plus_table: int32 [32, 128], replicated, may hold values from 0 to 127, each once within a row
- cross_table: int32 [128, 32], P('blk'), may hold values from 0 to 31, each once within a row
Outputs:
- crossed: float32 [2, 128, 32, 128], P(None, 'blk', None, 'group')
The draws below stay inside these ranges and needn't reach their ends.
Inputs may be any that keep to these rules, and one draw needn't show every extreme that they name: `plus_table`: each row is a permutation of 0 to 127. `cross_table`: each row is a permutation of 0 to 31.
All inputs are finite; a program needn't handle non-finite values.
Results may differ from the reference program's by a relative error of at most 0.0078.
Values may be sent and summed in bfloat16 or wider, within the bound.
A program may use at most 64 MiB of HBM per device.

```python
import math
import jax
import jax.numpy as jnp
from jax import lax

LX = 4
NK = 16
NW = 8
W = 128
NV = 1152
NT = 1024
NQ = 32
WALKERS = 32


def place_ends(result, own_key, low, largest):
    longest = result.shape.index(max(result.shape))
    spots = []
    for shift in (0, 1):
        where = [jax.random.randint(jax.random.fold_in(own_key, axis), (), 0, length) for axis, length in enumerate(result.shape)]
        where[longest] = (where[longest] + shift) % result.shape[longest]
        spots.append(tuple(where))
    return result.at[spots[0]].set(low).at[spots[1]].set(largest)


def shard_levels(own_key, dims, pieces, smallest, high):
    factor_of = 1.0
    for dim, shards_of in pieces:
        steps = jax.random.uniform(jax.random.fold_in(jax.random.fold_in(own_key, 6), dim), (shards_of,), jnp.float32, smallest / len(pieces), high / len(pieces))
        factor_of = factor_of * jnp.repeat(jnp.exp(steps), dims[dim] // shards_of).reshape((-1,) + (1,) * (len(dims) - 1 - dim))
    return factor_of


def noise(key, shape, deviation, most, shards=(), kind=jnp.bfloat16):
    entries = jax.random.normal(key, shape, jnp.float32) * deviation
    if len(shards) > 0:
        entries = shard_levels(key, shape, shards, -0.22, 0.18) * entries
    return jnp.clip(entries, min=-most, max=most).astype(kind)


def setup_inputs(seed: int = 0) -> dict:
    seeds = jax.random.split(jax.random.key(seed), 8)
    return {
        "vertex_matrix": noise(seeds[0], (WALKERS, NV, NV), NV ** -0.5, 0.1875, ((0, 32),)),
        "vertex_site": place_ends(jax.random.randint(seeds[1], (WALKERS, NV), 0, NK), jax.random.fold_in(seeds[1], 1), 0, NK - 1).astype(jnp.int32),
        "vertex_time": place_ends(jax.random.randint(seeds[2], (WALKERS, NV), 0, NT), jax.random.fold_in(seeds[2], 1), 0, NT - 1).astype(jnp.int32),
        "vertex_spin": place_ends(jax.random.randint(seeds[3], (WALKERS, NV), 0, 2), jax.random.fold_in(seeds[3], 1), 0, 1).astype(jnp.int32),
        "free_green": noise(seeds[4], (2, W), 0.5, 3.0, (), jnp.float32),
        "plus_table": jax.vmap(lambda own: jax.random.permutation(own, W))(jax.random.split(seeds[5], NQ)).reshape((NQ, W)).astype(jnp.int32),
        "cross_table": jax.vmap(lambda own: jax.random.permutation(own, NQ))(jax.random.split(seeds[6], W)).reshape((W, NQ)).astype(jnp.int32),
    }


def phases(site_ids, time_ids):
    points = jnp.arange(W, dtype=jnp.int32)
    moment = points // NW
    freq_index = points % NW
    kx_part = moment % LX
    ky_part = moment // LX
    rx_part = site_ids % LX
    ry_part = site_ids // LX
    winding = (2 * freq_index + 1)[:, None] * time_ids[None, :] + 2 * NT // LX * (kx_part[:, None] * rx_part[None, :] + ky_part[:, None] * ry_part[None, :])
    winding = winding % (2 * NT)
    return winding.astype(jnp.float32) * (math.pi / NT)

def green_pair(matrix, site_ids, time_ids, spin_ids, free_green):
    angles = phases(site_ids, time_ids)
    cosine = jnp.cos(angles)
    sine_part = jnp.sin(angles)
    spin_up = (spin_ids == 0).astype(jnp.float32)[None, :]
    spin_down = (spin_ids == 1).astype(jnp.float32)[None, :]
    fourier_rows = jnp.concatenate([cosine * spin_up, sine_part * spin_up, cosine * spin_down, sine_part * spin_down], 0).astype(jnp.bfloat16)
    projected = jnp.dot(fourier_rows, matrix, preferred_element_type=jnp.float32).astype(jnp.bfloat16)
    norm_factor = 1.0 / math.sqrt(NV)
    real_free = free_green[0]
    imag_free = free_green[1]
    greens = []
    for spin_index in range(2):
        offset = 2 * W * spin_index
        cosine_rows = fourier_rows[offset:offset + W]
        sine_rows = fourier_rows[offset + W:offset + 2 * W]
        proj_real = projected[offset:offset + W]
        proj_imag = projected[offset + W:offset + 2 * W]
        left_block = jnp.concatenate([jnp.concatenate([proj_real, proj_imag], 1), jnp.concatenate([proj_imag, -proj_real], 1)], 0)
        right_block = jnp.concatenate([cosine_rows, sine_rows], 1)
        kernel = lax.dot_general(left_block, right_block, (((1,), (1,)), ((), ())), preferred_element_type=jnp.float32)
        kernel_real = kernel[:W]
        kernel_imag = kernel[W:]
        half_real = real_free[:, None] * kernel_real - imag_free[:, None] * kernel_imag
        half_imag = real_free[:, None] * kernel_imag + imag_free[:, None] * kernel_real
        green_real = -(half_real * real_free[None, :] - half_imag * imag_free[None, :]) * norm_factor
        green_imag = -(half_real * imag_free[None, :] + half_imag * real_free[None, :]) * norm_factor
        greens.append(jnp.stack([green_real, green_imag], 0))
    green_sum = (greens[0] + greens[1]).astype(jnp.bfloat16)
    return (green_sum, greens[0].astype(jnp.bfloat16), greens[1].astype(jnp.bfloat16))

def pair_terms(green_sum, green_up, green_down, perm_rows):
    summed = green_sum.astype(jnp.float32)
    partner = jnp.swapaxes(summed[:, perm_rows[:, :, None], perm_rows[:, None, :]], 2, 3)
    direct_real = summed[0][None] * partner[0] - summed[1][None] * partner[1]
    direct_imag = summed[0][None] * partner[1] + summed[1][None] * partner[0]
    column_ids = jnp.arange(W, dtype=jnp.int32)[None, :]
    cross_real = jnp.zeros_like(direct_real)
    cross_imag = jnp.zeros_like(direct_imag)
    for spin_green in (green_up, green_down):
        values = spin_green.astype(jnp.float32)
        lead_values = values[:, column_ids, perm_rows]
        trail_values = values[:, perm_rows, column_ids]
        cross_real = cross_real + lead_values[0][:, :, None] * trail_values[0][:, None, :] - lead_values[1][:, :, None] * trail_values[1][:, None, :]
        cross_imag = cross_imag + lead_values[0][:, :, None] * trail_values[1][:, None, :] + lead_values[1][:, :, None] * trail_values[0][:, None, :]
    return jnp.stack([direct_real - cross_real, direct_imag - cross_imag], 0)

def reference(vertex_matrix, vertex_site, vertex_time, vertex_spin, free_green, plus_table, cross_table):

    def accumulate(running, walker):
        matrix, site_ids, time_ids, spin_ids = walker
        green_sum, green_up, green_down = green_pair(matrix, site_ids, time_ids, spin_ids, free_green)
        return (running + pair_terms(green_sum, green_up, green_down, plus_table), None)
    zero_total = jnp.zeros((2, NQ, W, W), jnp.float32)
    transfer, ignored = lax.scan(accumulate, zero_total, (vertex_matrix, vertex_site, vertex_time, vertex_spin))
    row_ids = jnp.arange(W, dtype=jnp.int32)
    return transfer[:, cross_table, row_ids[:, None], :]
```

```python
import functools
import math

import jax
import jax.numpy as jnp
from jax import lax
from jax.experimental import pallas as pl
from jax.experimental.pallas import tpu as pltpu
from jax.sharding import PartitionSpec as P

LX = 4
NW = 8
W = 128
NV = 1152
NT = 1024


def phases(site_ids, time_ids):
    points = jnp.arange(W, dtype=jnp.int32)
    moment = points // NW
    freq_index = points % NW
    kx_part = moment % LX
    ky_part = moment // LX
    rx_part = site_ids % LX
    ry_part = site_ids // LX
    winding = (2 * freq_index + 1)[:, None] * time_ids[None, :] + 2 * NT // LX * (
        kx_part[:, None] * rx_part[None, :] + ky_part[:, None] * ry_part[None, :]
    )
    winding = winding % (2 * NT)
    return winding.astype(jnp.float32) * (math.pi / NT)


def green_pair(matrix, site_ids, time_ids, spin_ids, free_green):
    angles = phases(site_ids, time_ids)
    cosine = jnp.cos(angles)
    sine_part = jnp.sin(angles)
    spin_up = (spin_ids == 0).astype(jnp.float32)[None, :]
    spin_down = (spin_ids == 1).astype(jnp.float32)[None, :]
    fourier_rows = jnp.concatenate(
        [cosine * spin_up, sine_part * spin_up, cosine * spin_down, sine_part * spin_down], 0
    ).astype(jnp.bfloat16)
    projected = jnp.dot(fourier_rows, matrix, preferred_element_type=jnp.float32).astype(
        jnp.bfloat16
    )
    norm_factor = 1.0 / math.sqrt(NV)
    real_free = free_green[0]
    imag_free = free_green[1]
    greens = []
    for spin_index in range(2):
        offset = 2 * W * spin_index
        cosine_rows = fourier_rows[offset : offset + W]
        sine_rows = fourier_rows[offset + W : offset + 2 * W]
        proj_real = projected[offset : offset + W]
        proj_imag = projected[offset + W : offset + 2 * W]
        left_block = jnp.concatenate(
            [
                jnp.concatenate([proj_real, proj_imag], 1),
                jnp.concatenate([proj_imag, -proj_real], 1),
            ],
            0,
        )
        right_block = jnp.concatenate([cosine_rows, sine_rows], 1)
        kernel = lax.dot_general(
            left_block, right_block, (((1,), (1,)), ((), ())), preferred_element_type=jnp.float32
        )
        kernel_real = kernel[:W]
        kernel_imag = kernel[W:]
        half_real = real_free[:, None] * kernel_real - imag_free[:, None] * kernel_imag
        half_imag = real_free[:, None] * kernel_imag + imag_free[:, None] * kernel_real
        green_real = (
            -(half_real * real_free[None, :] - half_imag * imag_free[None, :]) * norm_factor
        )
        green_imag = (
            -(half_real * imag_free[None, :] + half_imag * real_free[None, :]) * norm_factor
        )
        greens.append(jnp.stack([green_real, green_imag], 0))
    green_sum = (greens[0] + greens[1]).astype(jnp.bfloat16)
    return (green_sum, greens[0].astype(jnp.bfloat16), greens[1].astype(jnp.bfloat16))


def direct_terms(sums_piece, perm_row):
    column_ids = jnp.arange(sums_piece.shape[-1], dtype=jnp.int32)
    selector = (perm_row[:, None] == column_ids[None, :]).astype(jnp.bfloat16)
    halfway = jnp.einsum(
        "aj,kcbj->kcab", selector, sums_piece, preferred_element_type=jnp.float32
    ).astype(jnp.bfloat16)
    partner = jnp.einsum("kcaj,bj->kcab", halfway, selector, preferred_element_type=jnp.float32)
    local_copy = sums_piece.astype(jnp.float32)
    real_part = jnp.sum(local_copy[:, 0] * partner[:, 0] - local_copy[:, 1] * partner[:, 1], axis=0)
    imag_part = jnp.sum(local_copy[:, 0] * partner[:, 1] + local_copy[:, 1] * partner[:, 0], axis=0)
    return jnp.stack([real_part, imag_part], 0)


def copy_exchange(up_piece, down_piece, perm_row):
    column_ids = jnp.arange(up_piece.shape[-1], dtype=jnp.int32)
    spin_pieces = jnp.concatenate([up_piece, down_piece], 0)
    lead_values = spin_pieces[:, :, column_ids, perm_row]
    trail_values = spin_pieces[:, :, perm_row, column_ids]
    real_part = jnp.einsum(
        "ka,kb->ab", lead_values[:, 0], trail_values[:, 0], preferred_element_type=jnp.float32
    ) - jnp.einsum(
        "ka,kb->ab", lead_values[:, 1], trail_values[:, 1], preferred_element_type=jnp.float32
    )
    imag_part = jnp.einsum(
        "ka,kb->ab", lead_values[:, 0], trail_values[:, 1], preferred_element_type=jnp.float32
    ) + jnp.einsum(
        "ka,kb->ab", lead_values[:, 1], trail_values[:, 0], preferred_element_type=jnp.float32
    )
    return jnp.stack([real_part, imag_part], 0)


def plain_body(vertex_matrix, vertex_site, vertex_time, vertex_spin, free_green, plus_table, cross_table):
    green_sum, green_up, green_down = green_pair(
        vertex_matrix[0], vertex_site[0], vertex_time[0], vertex_spin[0], free_green
    )
    slices = plus_table.shape[0] // lax.axis_size("blk")
    owned_perms = lax.dynamic_slice_in_dim(plus_table, lax.axis_index("blk") * slices, slices, 0)
    sums_piece = lax.all_gather(green_sum[None], "blk", axis=0, tiled=True)
    up_piece = lax.all_gather(green_up[None], "blk", axis=0, tiled=True)
    down_piece = lax.all_gather(green_down[None], "blk", axis=0, tiled=True)

    def one_slice(perm_row):
        return direct_terms(sums_piece, perm_row) - copy_exchange(up_piece, down_piece, perm_row)

    transfer = jnp.swapaxes(lax.map(one_slice, owned_perms), 0, 1)
    shares = lax.psum_scatter(transfer, "group", scatter_dimension=3, tiled=True)
    regrouped = lax.all_to_all(shares, "blk", split_axis=2, concat_axis=1, tiled=True)
    row_ids = jnp.arange(regrouped.shape[2], dtype=jnp.int32)
    return regrouped[:, cross_table, row_ids[:, None], :]


BF = jnp.bfloat16
F32 = jnp.float32
MESH = pl.DeviceIdType.MESH
INNER = 2
PARTS = 4
CHUNKS = 3


def iota(shape, dim):
    return lax.broadcasted_iota(jnp.int32, shape, dim)


def one_hot(condition):
    return jnp.where(condition, 1.0, 0.0).astype(BF)


def dot(left, right):
    return jnp.dot(left, right, preferred_element_type=F32)


def dot_nt(left, right):
    return lax.dot_general(left, right, (((1,), (1,)), ((), ())), preferred_element_type=F32)


def kernel(
    nblk,
    ngroup,
    site_ref,
    time_ref,
    spin_ref,
    free_ref,
    plus_ref,
    cross_ref,
    matrix_hbm,
    out_ref,
    matrix,
    rows,
    kern,
    st,
    lr,
    lr_send,
    sel_b,
    sel_a,
    sel_out,
    spread,
    prow,
    sb,
    halfway,
    tsend,
    trecv,
    matrix_sem,
    st_send,
    st_recv,
    lr_send_sem,
    lr_recv,
    t_send,
    t_recv,
):
    nz = nblk // INNER
    na = W // nblk
    nb = W // ngroup
    nq = plus_ref.shape[0]
    half = na * nz
    npair = nq // 2
    nchunk = W // na
    nv = site_ref.shape[1]
    piece = nv // CHUNKS
    blk = lax.axis_index("blk")
    grp = lax.axis_index("group")
    zz = blk // INNER
    yy = blk % INNER
    plane = [(dy, dg) for dy in range(INNER) for dg in range(ngroup) if dy + dg > 0]

    def plane_peer(dy, dg):
        return (zz * INNER + (yy + dy) % INNER, (grp + dg) % ngroup)

    def z_peer(dz):
        return (((zz + dz) % nz) * INNER + yy, grp)

    barrier = pltpu.get_barrier_semaphore()
    for dy, dg in plane:
        pl.semaphore_signal(barrier, inc=1, device_id=plane_peer(dy, dg), device_id_type=MESH)
    for dz in range(1, nz):
        pl.semaphore_signal(barrier, inc=1, device_id=z_peer(dz), device_id_type=MESH)

    def matrix_copy(index):
        cols = pl.ds(pl.multiple_of(index * piece, 128), piece)
        return pltpu.make_async_copy(
            matrix_hbm.at[:, cols], matrix.at[:, cols], matrix_sem.at[index]
        )

    for index in range(CHUNKS):
        matrix_copy(index).start()

    site = site_ref[...]
    rx = site % LX
    ry = site // LX
    freq = iota((NW, nv), 0)
    winding = ((2 * freq + 1) * time_ref[...]) % (2 * NT)
    angles = winding.astype(F32) * (math.pi / NT)
    cosine = jnp.cos(angles)
    sine = jnp.sin(angles)
    spin = jnp.broadcast_to(spin_ref[...], (NW, nv))
    up = jnp.where(spin == 0, 1.0, 0.0)
    down = jnp.where(spin == 1, 1.0, 0.0)
    rx = jnp.broadcast_to(rx, (NW, nv))
    ry = jnp.broadcast_to(ry, (NW, nv))
    for first in range(0, W // NW, 2):
        c_rows = []
        s_rows = []
        for k in (first, first + 1):
            turn = ((k % LX) * rx + (k // LX) * ry) % 4
            odd = turn % 2 == 1
            c_sign = jnp.where((turn == 1) | (turn == 2), -1.0, 1.0)
            s_sign = jnp.where(turn >= 2, -1.0, 1.0)
            c_rows.append(jnp.where(odd, sine, cosine) * c_sign)
            s_rows.append(jnp.where(odd, cosine, sine) * s_sign)
        both_up = jnp.concatenate([up, up], 0)
        both_down = jnp.concatenate([down, down], 0)
        c_both = jnp.concatenate(c_rows, 0)
        s_both = jnp.concatenate(s_rows, 0)
        at = first * NW
        rows[pl.ds(at, 2 * NW), :] = (c_both * both_up).astype(BF)
        rows[pl.ds(W + at, 2 * NW), :] = (s_both * both_up).astype(BF)
        rows[pl.ds(2 * W + at, 2 * NW), :] = (c_both * both_down).astype(BF)
        rows[pl.ds(3 * W + at, 2 * NW), :] = (s_both * both_down).astype(BF)

    kern[...] = jnp.zeros_like(kern)

    def project(index, carry):
        matrix_copy(index).wait()
        cols = pl.ds(pl.multiple_of(index * piece, 128), piece)
        projected = dot(rows[...], matrix[:, cols]).astype(BF)
        for s in range(2):
            kern[s] += dot_nt(
                projected[2 * W * s : 2 * W * (s + 1)], rows[pl.ds(2 * W * s, 2 * W), cols]
            )
        return carry

    lax.fori_loop(0, CHUNKS, project, 0)

    ga_re = jnp.broadcast_to(free_ref[0:1, :], (W, W))
    ga_im = jnp.broadcast_to(free_ref[1:2, :], (W, W))
    gb_re, gb_im = ga_re, ga_im
    ga_re = ga_re.T
    ga_im = ga_im.T
    norm_factor = 1.0 / math.sqrt(NV)
    greens = []
    for s in range(2):
        k_re = kern[s, :W, :W] + kern[s, W:, W:]
        k_im = kern[s, W:, :W] - kern[s, :W, W:]
        h_re = ga_re * k_re - ga_im * k_im
        h_im = ga_re * k_im + ga_im * k_re
        greens.append(-(h_re * gb_re - h_im * gb_im) * norm_factor)
        greens.append(-(h_re * gb_im + h_im * gb_re) * norm_factor)
    turned = [g.T for g in greens]
    st[0, :W, :] = (turned[0] + turned[2]).astype(BF)
    st[0, W:, :] = (turned[1] + turned[3]).astype(BF)

    pl.semaphore_wait(barrier, len(plane) + nz - 1)

    def st_copy(slot, dy, dg):
        return pltpu.make_async_remote_copy(
            src_ref=st.at[0],
            dst_ref=st.at[slot],
            send_sem=st_send.at[slot],
            recv_sem=st_recv.at[slot],
            device_id=plane_peer(dy, dg),
            device_id_type=MESH,
        )

    def lr_copy(slot, dy, dg):
        wanted = ((yy + dy) % INNER) * ngroup + (grp + dg) % ngroup
        return pltpu.make_async_remote_copy(
            src_ref=lr_send.at[wanted],
            dst_ref=lr.at[slot],
            send_sem=lr_send_sem.at[slot],
            recv_sem=lr_recv.at[slot],
            device_id=plane_peer(dy, dg),
            device_id_type=MESH,
        )

    for slot, (dy, dg) in enumerate(plane):
        st_copy(slot + 1, dy, dg).start()

    greens = [g.astype(BF).astype(F32) for g in greens]
    turned = [g.astype(BF).astype(F32) for g in turned]
    plus = plus_ref[...].astype(F32)
    plus_turned = jnp.concatenate([plus, jnp.zeros((W - nq, W), F32)], 0).T
    expand = one_hot(iota((W, W), 1) // PARTS == iota((W, W), 0))
    index = dot(plus_turned.astype(BF), expand).astype(jnp.int32)
    lane = iota((W, W), 1)
    part = lane % PARTS

    def choose(values):
        picked = values[0]
        for g in range(1, PARTS):
            picked = jnp.where(part == g, values[g], picked)
        return picked

    lead = choose([jnp.take_along_axis(g, index, axis=1) for g in greens])
    trail = [jnp.take_along_axis(g, index, axis=1) for g in turned]
    trail_re = choose([trail[0], -trail[1], trail[2], -trail[3]]).T
    trail_im = choose([trail[1], trail[0], trail[3], trail[2]]).T
    order = [INNER * z + y for y in range(INNER) for z in range(nz)]
    lead = jnp.concatenate([lead[na * i : na * (i + 1)] for i in order], 0).T

    def shifted(value, by):
        by = by % W
        return value if by == 0 else pltpu.roll(value, by, 1)

    for j in range(ngroup):
        left = jnp.where(
            lane < nb, shifted(trail_re, -nb * j), shifted(trail_im, nb - nb * j)
        )
        for y in range(INNER):
            joined = jnp.where(lane < half, left, shifted(lead, half - half * y))
            lr_send[y * ngroup + j] = joined.astype(BF)
    for slot, (dy, dg) in enumerate(plane):
        lr_copy(slot + 1, dy, dg).start()
    lr[0] = lr_send[yy * ngroup + grp]

    plus_bf = plus.astype(BF)
    my_b = one_hot(iota((nb, W), 1) == iota((nb, W), 0) + nb * grp)
    plus_b = dot_nt(my_b, plus_bf).astype(jnp.int32)
    for q in range(nq):
        column = jnp.broadcast_to(plus_b[:, q : q + 1], (nb, W))
        sel_b[pl.ds(q * nb, nb), :] = one_hot(column == iota((nb, W), 1))
    place = (lane % half) // na * (na * INNER) + na * yy + lane % na
    my_a = one_hot(iota((W, W), 0) == place)
    prow[...] = dot(plus_bf, my_a)

    def pair_selector(pair, carry):
        first = prow[pl.ds(2 * pair, 1), :]
        second = prow[pl.ds(2 * pair + 1, 1), :]
        low = lane < half
        hit = iota((W, W), 0) == jnp.where(
            low, jnp.broadcast_to(first, (W, W)), jnp.broadcast_to(second, (W, W))
        ).astype(jnp.int32)
        sel_a[pair, :W, :] = one_hot(hit & low)
        sel_a[pair, W:, :] = one_hot(hit & (lane >= half))
        return carry

    lax.fori_loop(0, npair, pair_selector, 0)

    width = nz * W
    source = iota((width, W), 0)
    target = (source // na) % nz * W + source // half * na + source % na
    for z in range(nz):
        spread[:, z * W : (z + 1) * W] = one_hot(target == iota((width, W), 1) + z * W)

    same = one_hot(iota((nq, nq), 0) == iota((nq, nq), 1))
    crossing = dot_nt(same, cross_ref[...].astype(F32).astype(BF)).astype(jnp.int32)
    for r in range(na):
        column = jnp.broadcast_to(crossing[:, r : r + 1] * na + r, (nq, nq * na))
        sel_out[pl.ds(r * nq, nq), :] = one_hot(column == iota((nq, nq * na), 1))

    def first_selection(slot, carry):
        @pl.when(slot > 0)
        def _():
            st_copy(slot, 0, 1).wait_recv()

        for c in range(2):
            mine = st[slot, pl.ds(pl.multiple_of(c * W + nb * grp, nb), nb), :]
            sb[slot, c] = dot(mine, my_a)
            chosen = dot_nt(sel_b[...], st[slot, c * W : (c + 1) * W, :]).astype(BF)
            for q in range(nq):
                halfway[q // 2, slot, c, :, pl.ds((q % 2) * W, W)] = chosen[
                    q * nb : (q + 1) * nb
                ]
        return carry

    lax.fori_loop(0, len(plane) + 1, first_selection, 0)

    for slot, (dy, dg) in enumerate(plane):
        lr_copy(slot + 1, dy, dg).wait_recv()

    nw = len(plane) + 1
    four = W // (nw * PARTS)
    depth = four * PARTS

    def t_copy(dz, chunk):
        cols = pl.ds(pl.multiple_of(chunk * W, W), W)
        return pltpu.make_async_remote_copy(
            src_ref=tsend.at[(zz + dz) % nz, :, cols],
            dst_ref=trecv.at[dz, :, cols],
            send_sem=t_send.at[dz, chunk],
            recv_sem=t_recv.at[dz, chunk],
            device_id=z_peer(dz),
            device_id_type=MESH,
        )

    def measure_chunk(chunk, carry):
        totals = []
        for sub in range(nz):
            pair = chunk * nz + sub
            partner = dot(halfway[pair].reshape(nw * 2 * nb, 2 * W), sel_a[pair])
            t_re = jnp.zeros((nb, W), F32)
            t_im = jnp.zeros((nb, W), F32)
            for w in range(nw):
                s_re = sb[w, 0]
                s_im = sb[w, 1]
                p_re = partner[2 * nb * w : 2 * nb * w + nb]
                p_im = partner[2 * nb * w + nb : 2 * nb * (w + 1)]
                t_re = t_re + (s_re * p_re - s_im * p_im)
                t_im = t_im + (s_re * p_im + s_im * p_re)
            pairs = four // 2
            if sub % pairs == 0:
                start = pl.multiple_of((chunk * (nz // pairs) + sub // pairs) * depth, depth)
                stacked = lr[:, pl.ds(start, depth), :].reshape(W, W).astype(F32)
                trailing = stacked.T[:half].astype(BF)
                leading = jnp.where(lane < half, pltpu.roll(stacked, half, 1), stacked)
                row_q = iota((W, W), 0) % depth // PARTS
            masked = jnp.where(row_q == 2 * (sub % pairs) + lane // half, leading, 0.0)
            exchange = dot(trailing, masked.astype(BF))
            totals.append((jnp.concatenate([t_re, t_im], 0) - exchange).astype(BF))
        moved = dot(jnp.concatenate(totals, 1), spread[...]).astype(BF)
        cols = pl.ds(pl.multiple_of(chunk * W, W), W)
        for z in range(nz):
            tsend[z, :, cols] = moved[:, z * W : (z + 1) * W]
        for dz in range(1, nz):
            t_copy(dz, chunk).start()
        return carry

    chunks = nq // nchunk
    lax.fori_loop(0, chunks, measure_chunk, 0)

    out_ref[...] = dot_nt(sel_out[...], tsend[zz])
    for dz in range(1, nz):
        for chunk in range(chunks):
            t_copy(dz, chunk).wait_recv()
        out_ref[...] += dot_nt(sel_out[...], trecv[dz])

    for slot, (dy, dg) in enumerate(plane):
        st_copy(slot + 1, dy, dg).wait_send()
        lr_copy(slot + 1, dy, dg).wait_send()
    for dz in range(1, nz):
        for chunk in range(chunks):
            t_copy(dz, chunk).wait_send()


def kernel_body(
    vertex_matrix, vertex_site, vertex_time, vertex_spin, free_green, plus_table, cross_table
):
    nblk = lax.axis_size("blk")
    ngroup = lax.axis_size("group")
    nv = vertex_matrix.shape[-1]
    nq = plus_table.shape[0]
    nz = nblk // INNER
    na = W // nblk
    nb = W // ngroup
    nw = INNER * ngroup
    npair = nq // 2
    chunks = nq // (W // na)
    vmem = pl.BlockSpec(memory_space=pltpu.VMEM)
    dma = pltpu.SemaphoreType.DMA
    out = pl.pallas_call(
        functools.partial(kernel, nblk, ngroup),
        out_shape=jax.ShapeDtypeStruct((na * nq, 2 * nb), F32),
        in_specs=[vmem] * 6 + [pl.BlockSpec(memory_space=pl.ANY)],
        out_specs=vmem,
        scratch_shapes=[
            pltpu.VMEM((nv, nv), BF),
            pltpu.VMEM((4 * W, nv), BF),
            pltpu.VMEM((2, 2 * W, 2 * W), F32),
            pltpu.VMEM((nw, 2 * W, W), BF),
            pltpu.VMEM((nw, W, W), BF),
            pltpu.VMEM((nw, W, W), BF),
            pltpu.VMEM((nq * nb, W), BF),
            pltpu.VMEM((npair, 2 * W, W), BF),
            pltpu.VMEM((na * nq, nq * na), BF),
            pltpu.VMEM((nz * W, nz * W), BF),
            pltpu.VMEM((nq, W), F32),
            pltpu.VMEM((nw, 2, nb, W), F32),
            pltpu.VMEM((npair, nw, 2, nb, 2 * W), BF),
            pltpu.VMEM((nz, 2 * nb, nq * na), BF),
            pltpu.VMEM((nz, 2 * nb, nq * na), BF),
            dma((CHUNKS,)),
            dma((nw,)),
            dma((nw,)),
            dma((nw,)),
            dma((nw,)),
            dma((nz, chunks)),
            dma((nz, chunks)),
        ],
        compiler_params=pltpu.CompilerParams(
            collective_id=0, has_side_effects=True, vmem_limit_bytes=40 * 1024 * 1024
        ),
    )(
        vertex_site,
        vertex_time,
        vertex_spin,
        free_green,
        plus_table,
        cross_table,
        vertex_matrix[0],
    )
    return out.reshape(na, nq, 2, nb).transpose(2, 0, 1, 3)


def fits(mesh):
    nblk, ngroup = mesh.shape["blk"], mesh.shape["group"]
    if nblk % INNER or W % nblk or W % ngroup:
        return False
    nz, na, nb = nblk // INNER, W // nblk, W // ngroup
    return nz == 4 and 2 * nz * na == W and 4 * nb == W and na % 16 == 0 and nb % 16 == 0


def solution(mesh):
    in_specs = (
        P(("blk", "group"), None, None),
        P(("blk", "group"), None),
        P(("blk", "group"), None),
        P(("blk", "group"), None),
        P(),
        P(),
        P("blk", None),
    )
    out_specs = P(None, "blk", None, "group")

    def chosen(*args):
        matrix, plus = args[0], args[5]
        small = fits(mesh) and PARTS * plus.shape[0] == W and matrix.shape[-1] % (128 * CHUNKS) == 0
        return (kernel_body if small else plain_body)(*args)

    return jax.shard_map(chosen, mesh=mesh, in_specs=in_specs, out_specs=out_specs, check_vma=False)
```

```python
import functools
import math

import jax
import jax.numpy as jnp
from jax import lax
from jax.experimental import pallas as pl
from jax.experimental.pallas import tpu as pltpu
from jax.sharding import PartitionSpec as P

LX = 4
NW = 8
W = 128
NV = 1152
NT = 1024


def phases(site_ids, time_ids):
    points = jnp.arange(W, dtype=jnp.int32)
    moment = points // NW
    freq_index = points % NW
    kx_part = moment % LX
    ky_part = moment // LX
    rx_part = site_ids % LX
    ry_part = site_ids // LX
    winding = (2 * freq_index + 1)[:, None] * time_ids[None, :] + 2 * NT // LX * (
        kx_part[:, None] * rx_part[None, :] + ky_part[:, None] * ry_part[None, :]
    )
    winding = winding % (2 * NT)
    return winding.astype(jnp.float32) * (math.pi / NT)


def green_pair(matrix, site_ids, time_ids, spin_ids, free_green):
    angles = phases(site_ids, time_ids)
    cosine = jnp.cos(angles)
    sine_part = jnp.sin(angles)
    spin_up = (spin_ids == 0).astype(jnp.float32)[None, :]
    spin_down = (spin_ids == 1).astype(jnp.float32)[None, :]
    fourier_rows = jnp.concatenate(
        [cosine * spin_up, sine_part * spin_up, cosine * spin_down, sine_part * spin_down], 0
    ).astype(jnp.bfloat16)
    projected = jnp.dot(fourier_rows, matrix, preferred_element_type=jnp.float32).astype(
        jnp.bfloat16
    )
    norm_factor = 1.0 / math.sqrt(NV)
    real_free = free_green[0]
    imag_free = free_green[1]
    greens = []
    for spin_index in range(2):
        offset = 2 * W * spin_index
        cosine_rows = fourier_rows[offset : offset + W]
        sine_rows = fourier_rows[offset + W : offset + 2 * W]
        proj_real = projected[offset : offset + W]
        proj_imag = projected[offset + W : offset + 2 * W]
        left_block = jnp.concatenate(
            [
                jnp.concatenate([proj_real, proj_imag], 1),
                jnp.concatenate([proj_imag, -proj_real], 1),
            ],
            0,
        )
        right_block = jnp.concatenate([cosine_rows, sine_rows], 1)
        kernel = lax.dot_general(
            left_block, right_block, (((1,), (1,)), ((), ())), preferred_element_type=jnp.float32
        )
        kernel_real = kernel[:W]
        kernel_imag = kernel[W:]
        half_real = real_free[:, None] * kernel_real - imag_free[:, None] * kernel_imag
        half_imag = real_free[:, None] * kernel_imag + imag_free[:, None] * kernel_real
        green_real = (
            -(half_real * real_free[None, :] - half_imag * imag_free[None, :]) * norm_factor
        )
        green_imag = (
            -(half_real * imag_free[None, :] + half_imag * real_free[None, :]) * norm_factor
        )
        greens.append(jnp.stack([green_real, green_imag], 0))
    green_sum = (greens[0] + greens[1]).astype(jnp.bfloat16)
    return (green_sum, greens[0].astype(jnp.bfloat16), greens[1].astype(jnp.bfloat16))


def direct_terms(sums_piece, perm_row):
    column_ids = jnp.arange(sums_piece.shape[-1], dtype=jnp.int32)
    selector = (perm_row[:, None] == column_ids[None, :]).astype(jnp.bfloat16)
    halfway = jnp.einsum(
        "aj,kcbj->kcab", selector, sums_piece, preferred_element_type=jnp.float32
    ).astype(jnp.bfloat16)
    partner = jnp.einsum("kcaj,bj->kcab", halfway, selector, preferred_element_type=jnp.float32)
    local_copy = sums_piece.astype(jnp.float32)
    real_part = jnp.sum(local_copy[:, 0] * partner[:, 0] - local_copy[:, 1] * partner[:, 1], axis=0)
    imag_part = jnp.sum(local_copy[:, 0] * partner[:, 1] + local_copy[:, 1] * partner[:, 0], axis=0)
    return jnp.stack([real_part, imag_part], 0)


def copy_exchange(up_piece, down_piece, perm_row):
    column_ids = jnp.arange(up_piece.shape[-1], dtype=jnp.int32)
    spin_pieces = jnp.concatenate([up_piece, down_piece], 0)
    lead_values = spin_pieces[:, :, column_ids, perm_row]
    trail_values = spin_pieces[:, :, perm_row, column_ids]
    real_part = jnp.einsum(
        "ka,kb->ab", lead_values[:, 0], trail_values[:, 0], preferred_element_type=jnp.float32
    ) - jnp.einsum(
        "ka,kb->ab", lead_values[:, 1], trail_values[:, 1], preferred_element_type=jnp.float32
    )
    imag_part = jnp.einsum(
        "ka,kb->ab", lead_values[:, 0], trail_values[:, 1], preferred_element_type=jnp.float32
    ) + jnp.einsum(
        "ka,kb->ab", lead_values[:, 1], trail_values[:, 0], preferred_element_type=jnp.float32
    )
    return jnp.stack([real_part, imag_part], 0)


def plain_body(vertex_matrix, vertex_site, vertex_time, vertex_spin, free_green, plus_table, cross_table):
    green_sum, green_up, green_down = green_pair(
        vertex_matrix[0], vertex_site[0], vertex_time[0], vertex_spin[0], free_green
    )
    slices = plus_table.shape[0] // lax.axis_size("blk")
    owned_perms = lax.dynamic_slice_in_dim(plus_table, lax.axis_index("blk") * slices, slices, 0)
    sums_piece = lax.all_gather(green_sum[None], "blk", axis=0, tiled=True)
    up_piece = lax.all_gather(green_up[None], "blk", axis=0, tiled=True)
    down_piece = lax.all_gather(green_down[None], "blk", axis=0, tiled=True)

    def one_slice(perm_row):
        return direct_terms(sums_piece, perm_row) - copy_exchange(up_piece, down_piece, perm_row)

    transfer = jnp.swapaxes(lax.map(one_slice, owned_perms), 0, 1)
    shares = lax.psum_scatter(transfer, "group", scatter_dimension=3, tiled=True)
    regrouped = lax.all_to_all(shares, "blk", split_axis=2, concat_axis=1, tiled=True)
    row_ids = jnp.arange(regrouped.shape[2], dtype=jnp.int32)
    return regrouped[:, cross_table, row_ids[:, None], :]


BF = jnp.bfloat16
F32 = jnp.float32
MESH = pl.DeviceIdType.MESH
INNER = 2
PARTS = 4
CHUNKS = 3


def iota(shape, dim):
    return lax.broadcasted_iota(jnp.int32, shape, dim)


def one_hot(condition):
    return jnp.where(condition, 1.0, 0.0).astype(BF)


def dot(left, right):
    return jnp.dot(left, right, preferred_element_type=F32)


def dot_nt(left, right):
    return lax.dot_general(left, right, (((1,), (1,)), ((), ())), preferred_element_type=F32)


def kernel(
    nblk,
    ngroup,
    site_hbm,
    time_hbm,
    spin_hbm,
    free_hbm,
    plus_hbm,
    cross_hbm,
    matrix_hbm,
    out_ref,
    site_ref,
    time_ref,
    spin_ref,
    free_ref,
    plus_ref,
    cross_ref,
    total,
    matrix,
    rows,
    kern,
    st,
    lr,
    lr_send,
    sel_b,
    sel_a,
    sel_out,
    spread,
    prow,
    sb,
    halfway,
    tsend,
    trecv,
    small_sem,
    matrix_sem,
    st_send,
    st_recv,
    lr_send_sem,
    lr_recv,
    t_send,
    t_recv,
):
    small = [
        pltpu.make_async_copy(source, target, small_sem.at[place])
        for place, (source, target) in enumerate(
            [
                (site_hbm, site_ref),
                (time_hbm, time_ref),
                (spin_hbm, spin_ref),
                (free_hbm, free_ref),
                (plus_hbm, plus_ref),
                (cross_hbm, cross_ref),
            ]
        )
    ]
    for copy in small:
        copy.start()

    nz = nblk // INNER
    na = W // nblk
    nb = W // ngroup
    nq = plus_ref.shape[0]
    half = na * nz
    npair = nq // 2
    nchunk = W // na
    nv = site_ref.shape[1]
    piece = nv // CHUNKS
    blk = lax.axis_index("blk")
    grp = lax.axis_index("group")
    zz = blk // INNER
    yy = blk % INNER
    plane = [(dy, dg) for dy in range(INNER) for dg in range(ngroup) if dy + dg > 0]

    def plane_peer(dy, dg):
        return (zz * INNER + (yy + dy) % INNER, (grp + dg) % ngroup)

    def z_peer(dz):
        return (((zz + dz) % nz) * INNER + yy, grp)

    barrier = pltpu.get_barrier_semaphore()
    for dy, dg in plane:
        pl.semaphore_signal(barrier, inc=1, device_id=plane_peer(dy, dg), device_id_type=MESH)
    for dz in range(1, nz):
        pl.semaphore_signal(barrier, inc=1, device_id=z_peer(dz), device_id_type=MESH)

    def matrix_copy(index):
        cols = pl.ds(pl.multiple_of(index * piece, 128), piece)
        return pltpu.make_async_copy(
            matrix_hbm.at[:, cols], matrix.at[:, cols], matrix_sem.at[index]
        )

    for index in range(CHUNKS):
        matrix_copy(index).start()

    for copy in small:
        copy.wait()
    site = site_ref[...]
    rx = site % LX
    ry = site // LX
    freq = iota((NW, nv), 0)
    winding = ((2 * freq + 1) * time_ref[...]) % (2 * NT)
    angles = winding.astype(F32) * (math.pi / NT)
    cosine = jnp.cos(angles)
    sine = jnp.sin(angles)
    spin = jnp.broadcast_to(spin_ref[...], (NW, nv))
    up = jnp.where(spin == 0, 1.0, 0.0)
    down = jnp.where(spin == 1, 1.0, 0.0)
    rx = jnp.broadcast_to(rx, (NW, nv))
    ry = jnp.broadcast_to(ry, (NW, nv))
    for first in range(0, W // NW, 2):
        c_rows = []
        s_rows = []
        for k in (first, first + 1):
            turn = ((k % LX) * rx + (k // LX) * ry) % 4
            odd = turn % 2 == 1
            c_sign = jnp.where((turn == 1) | (turn == 2), -1.0, 1.0)
            s_sign = jnp.where(turn >= 2, -1.0, 1.0)
            c_rows.append(jnp.where(odd, sine, cosine) * c_sign)
            s_rows.append(jnp.where(odd, cosine, sine) * s_sign)
        both_up = jnp.concatenate([up, up], 0)
        both_down = jnp.concatenate([down, down], 0)
        c_both = jnp.concatenate(c_rows, 0)
        s_both = jnp.concatenate(s_rows, 0)
        at = first * NW
        rows[pl.ds(at, 2 * NW), :] = (c_both * both_up).astype(BF)
        rows[pl.ds(W + at, 2 * NW), :] = (s_both * both_up).astype(BF)
        rows[pl.ds(2 * W + at, 2 * NW), :] = (c_both * both_down).astype(BF)
        rows[pl.ds(3 * W + at, 2 * NW), :] = (s_both * both_down).astype(BF)

    kern[...] = jnp.zeros_like(kern)

    def project(index, carry):
        matrix_copy(index).wait()
        cols = pl.ds(pl.multiple_of(index * piece, 128), piece)
        projected = dot(rows[...], matrix[:, cols]).astype(BF)
        for s in range(2):
            kern[s] += dot_nt(
                projected[2 * W * s : 2 * W * (s + 1)], rows[pl.ds(2 * W * s, 2 * W), cols]
            )
        return carry

    lax.fori_loop(0, CHUNKS, project, 0)

    ga_re = jnp.broadcast_to(free_ref[0:1, :], (W, W))
    ga_im = jnp.broadcast_to(free_ref[1:2, :], (W, W))
    gb_re, gb_im = ga_re, ga_im
    ga_re = ga_re.T
    ga_im = ga_im.T
    norm_factor = 1.0 / math.sqrt(NV)
    greens = []
    for s in range(2):
        k_re = kern[s, :W, :W] + kern[s, W:, W:]
        k_im = kern[s, W:, :W] - kern[s, :W, W:]
        h_re = ga_re * k_re - ga_im * k_im
        h_im = ga_re * k_im + ga_im * k_re
        greens.append(-(h_re * gb_re - h_im * gb_im) * norm_factor)
        greens.append(-(h_re * gb_im + h_im * gb_re) * norm_factor)
    turned = [g.T for g in greens]
    st[0, :W, :] = (turned[0] + turned[2]).astype(BF)
    st[0, W:, :] = (turned[1] + turned[3]).astype(BF)

    pl.semaphore_wait(barrier, len(plane) + nz - 1)

    def st_copy(slot, dy, dg):
        return pltpu.make_async_remote_copy(
            src_ref=st.at[0],
            dst_ref=st.at[slot],
            send_sem=st_send.at[slot],
            recv_sem=st_recv.at[slot],
            device_id=plane_peer(dy, dg),
            device_id_type=MESH,
        )

    def lr_copy(slot, dy, dg):
        wanted = ((yy + dy) % INNER) * ngroup + (grp + dg) % ngroup
        return pltpu.make_async_remote_copy(
            src_ref=lr_send.at[wanted],
            dst_ref=lr.at[slot],
            send_sem=lr_send_sem.at[slot],
            recv_sem=lr_recv.at[slot],
            device_id=plane_peer(dy, dg),
            device_id_type=MESH,
        )

    for slot, (dy, dg) in enumerate(plane):
        st_copy(slot + 1, dy, dg).start()

    greens = [g.astype(BF).astype(F32) for g in greens]
    turned = [g.astype(BF).astype(F32) for g in turned]
    plus = plus_ref[...].astype(F32)
    plus_turned = jnp.concatenate([plus, jnp.zeros((W - nq, W), F32)], 0).T
    expand = one_hot(iota((W, W), 1) // PARTS == iota((W, W), 0))
    index = dot(plus_turned.astype(BF), expand).astype(jnp.int32)
    lane = iota((W, W), 1)
    part = lane % PARTS

    def choose(values):
        picked = values[0]
        for g in range(1, PARTS):
            picked = jnp.where(part == g, values[g], picked)
        return picked

    lead = choose([jnp.take_along_axis(g, index, axis=1) for g in greens])
    trail = [jnp.take_along_axis(g, index, axis=1) for g in turned]
    trail_re = choose([trail[0], -trail[1], trail[2], -trail[3]]).T
    trail_im = choose([trail[1], trail[0], trail[3], trail[2]]).T
    order = [INNER * z + y for y in range(INNER) for z in range(nz)]
    lead = jnp.concatenate([lead[na * i : na * (i + 1)] for i in order], 0).T

    def shifted(value, by):
        by = by % W
        return value if by == 0 else pltpu.roll(value, by, 1)

    for j in range(ngroup):
        left = jnp.where(
            lane < nb, shifted(trail_re, -nb * j), shifted(trail_im, nb - nb * j)
        )
        for y in range(INNER):
            joined = jnp.where(lane < half, left, shifted(lead, half - half * y))
            lr_send[y * ngroup + j] = joined.astype(BF)
    for slot, (dy, dg) in enumerate(plane):
        lr_copy(slot + 1, dy, dg).start()
    lr[0] = lr_send[yy * ngroup + grp]

    plus_bf = plus.astype(BF)
    my_b = one_hot(iota((nb, W), 1) == iota((nb, W), 0) + nb * grp)
    plus_b = dot_nt(my_b, plus_bf).astype(jnp.int32)
    for q in range(nq):
        column = jnp.broadcast_to(plus_b[:, q : q + 1], (nb, W))
        sel_b[pl.ds(q * nb, nb), :] = one_hot(column == iota((nb, W), 1))
    place = (lane % half) // na * (na * INNER) + na * yy + lane % na
    my_a = one_hot(iota((W, W), 0) == place)
    prow[...] = dot(plus_bf, my_a)

    def pair_selector(pair, carry):
        first = prow[pl.ds(2 * pair, 1), :]
        second = prow[pl.ds(2 * pair + 1, 1), :]
        low = lane < half
        hit = iota((W, W), 0) == jnp.where(
            low, jnp.broadcast_to(first, (W, W)), jnp.broadcast_to(second, (W, W))
        ).astype(jnp.int32)
        sel_a[pair, :W, :] = one_hot(hit & low)
        sel_a[pair, W:, :] = one_hot(hit & (lane >= half))
        return carry

    lax.fori_loop(0, npair, pair_selector, 0)

    width = nz * W
    source = iota((width, W), 0)
    target = (source // na) % nz * W + source // half * na + source % na
    for z in range(nz):
        spread[:, z * W : (z + 1) * W] = one_hot(target == iota((width, W), 1) + z * W)

    same = one_hot(iota((nq, nq), 0) == iota((nq, nq), 1))
    crossing = dot_nt(same, cross_ref[...].astype(F32).astype(BF)).astype(jnp.int32)
    for r in range(na):
        column = jnp.broadcast_to(crossing[:, r : r + 1] * na + r, (nq, nq * na))
        sel_out[pl.ds(r * nq, nq), :] = one_hot(column == iota((nq, nq * na), 1))

    def first_selection(slot, carry):
        @pl.when(slot > 0)
        def _():
            st_copy(slot, 0, 1).wait_recv()

        for c in range(2):
            mine = st[slot, pl.ds(pl.multiple_of(c * W + nb * grp, nb), nb), :]
            sb[slot, c] = dot(mine, my_a)
            chosen = dot_nt(sel_b[...], st[slot, c * W : (c + 1) * W, :]).astype(BF)
            for q in range(nq):
                halfway[q // 2, slot, c, :, pl.ds((q % 2) * W, W)] = chosen[
                    q * nb : (q + 1) * nb
                ]
        return carry

    lax.fori_loop(0, len(plane) + 1, first_selection, 0)

    for slot, (dy, dg) in enumerate(plane):
        lr_copy(slot + 1, dy, dg).wait_recv()

    nw = len(plane) + 1
    four = W // (nw * PARTS)
    depth = four * PARTS

    def t_copy(dz, chunk):
        cols = pl.ds(pl.multiple_of(chunk * W, W), W)
        return pltpu.make_async_remote_copy(
            src_ref=tsend.at[(zz + dz) % nz, :, cols],
            dst_ref=trecv.at[dz, :, cols],
            send_sem=t_send.at[dz, chunk],
            recv_sem=t_recv.at[dz, chunk],
            device_id=z_peer(dz),
            device_id_type=MESH,
        )

    def measure_chunk(chunk, carry):
        totals = []
        for sub in range(nz):
            pair = chunk * nz + sub
            partner = dot(halfway[pair].reshape(nw * 2 * nb, 2 * W), sel_a[pair])
            t_re = jnp.zeros((nb, W), F32)
            t_im = jnp.zeros((nb, W), F32)
            for w in range(nw):
                s_re = sb[w, 0]
                s_im = sb[w, 1]
                p_re = partner[2 * nb * w : 2 * nb * w + nb]
                p_im = partner[2 * nb * w + nb : 2 * nb * (w + 1)]
                t_re = t_re + (s_re * p_re - s_im * p_im)
                t_im = t_im + (s_re * p_im + s_im * p_re)
            pairs = four // 2
            if sub % pairs == 0:
                start = pl.multiple_of((chunk * (nz // pairs) + sub // pairs) * depth, depth)
                stacked = lr[:, pl.ds(start, depth), :].reshape(W, W).astype(F32)
                trailing = stacked.T[:half].astype(BF)
                leading = jnp.where(lane < half, pltpu.roll(stacked, half, 1), stacked)
                row_q = iota((W, W), 0) % depth // PARTS
            masked = jnp.where(row_q == 2 * (sub % pairs) + lane // half, leading, 0.0)
            exchange = dot(trailing, masked.astype(BF))
            totals.append((jnp.concatenate([t_re, t_im], 0) - exchange).astype(BF))
        moved = dot(jnp.concatenate(totals, 1), spread[...]).astype(BF)
        cols = pl.ds(pl.multiple_of(chunk * W, W), W)
        for z in range(nz):
            tsend[z, :, cols] = moved[:, z * W : (z + 1) * W]
        for dz in range(1, nz):
            t_copy(dz, chunk).start()
        return carry

    chunks = nq // nchunk
    lax.fori_loop(0, chunks, measure_chunk, 0)

    total[...] = dot_nt(sel_out[...], tsend[zz])
    for dz in range(1, nz):
        for chunk in range(chunks):
            t_copy(dz, chunk).wait_recv()
        total[...] += dot_nt(sel_out[...], trecv[dz])
    for c in range(2):
        out_ref[c] = total[:, c * nb : (c + 1) * nb].reshape(na, nq, nb)

    for slot, (dy, dg) in enumerate(plane):
        st_copy(slot + 1, dy, dg).wait_send()
        lr_copy(slot + 1, dy, dg).wait_send()
    for dz in range(1, nz):
        for chunk in range(chunks):
            t_copy(dz, chunk).wait_send()


def kernel_body(
    vertex_matrix, vertex_site, vertex_time, vertex_spin, free_green, plus_table, cross_table
):
    nblk = lax.axis_size("blk")
    ngroup = lax.axis_size("group")
    nv = vertex_matrix.shape[-1]
    nq = plus_table.shape[0]
    nz = nblk // INNER
    na = W // nblk
    nb = W // ngroup
    nw = INNER * ngroup
    npair = nq // 2
    chunks = nq // (W // na)
    vmem = pl.BlockSpec(memory_space=pltpu.VMEM)
    dma = pltpu.SemaphoreType.DMA
    return pl.pallas_call(
        functools.partial(kernel, nblk, ngroup),
        out_shape=jax.ShapeDtypeStruct((2, na, nq, nb), F32),
        in_specs=[pl.BlockSpec(memory_space=pltpu.HBM)] * 7,
        out_specs=vmem,
        scratch_shapes=[
            pltpu.VMEM(vertex_site.shape, jnp.int32),
            pltpu.VMEM(vertex_time.shape, jnp.int32),
            pltpu.VMEM(vertex_spin.shape, jnp.int32),
            pltpu.VMEM(free_green.shape, F32),
            pltpu.VMEM(plus_table.shape, jnp.int32),
            pltpu.VMEM(cross_table.shape, jnp.int32),
            pltpu.VMEM((na * nq, 2 * nb), F32),
            pltpu.VMEM((nv, nv), BF),
            pltpu.VMEM((4 * W, nv), BF),
            pltpu.VMEM((2, 2 * W, 2 * W), F32),
            pltpu.VMEM((nw, 2 * W, W), BF),
            pltpu.VMEM((nw, W, W), BF),
            pltpu.VMEM((nw, W, W), BF),
            pltpu.VMEM((nq * nb, W), BF),
            pltpu.VMEM((npair, 2 * W, W), BF),
            pltpu.VMEM((na * nq, nq * na), BF),
            pltpu.VMEM((nz * W, nz * W), BF),
            pltpu.VMEM((nq, W), F32),
            pltpu.VMEM((nw, 2, nb, W), F32),
            pltpu.VMEM((npair, nw, 2, nb, 2 * W), BF),
            pltpu.VMEM((nz, 2 * nb, nq * na), BF),
            pltpu.VMEM((nz, 2 * nb, nq * na), BF),
            dma((6,)),
            dma((CHUNKS,)),
            dma((nw,)),
            dma((nw,)),
            dma((nw,)),
            dma((nw,)),
            dma((nz, chunks)),
            dma((nz, chunks)),
        ],
        compiler_params=pltpu.CompilerParams(
            collective_id=0, has_side_effects=True, vmem_limit_bytes=63 * 1024 * 1024
        ),
    )(
        vertex_site,
        vertex_time,
        vertex_spin,
        free_green,
        plus_table,
        cross_table,
        vertex_matrix[0],
    )


def fits(mesh):
    nblk, ngroup = mesh.shape["blk"], mesh.shape["group"]
    if nblk % INNER or W % nblk or W % ngroup:
        return False
    nz, na, nb = nblk // INNER, W // nblk, W // ngroup
    return nz == 4 and 2 * nz * na == W and 4 * nb == W and na % 16 == 0 and nb % 16 == 0


def solution(mesh):
    in_specs = (
        P(("blk", "group"), None, None),
        P(("blk", "group"), None),
        P(("blk", "group"), None),
        P(("blk", "group"), None),
        P(),
        P(),
        P("blk", None),
    )
    out_specs = P(None, "blk", None, "group")

    def chosen(*args):
        matrix, plus = args[0], args[5]
        small = fits(mesh) and PARTS * plus.shape[0] == W and matrix.shape[-1] % (128 * CHUNKS) == 0
        return (kernel_body if small else plain_body)(*args)

    return jax.shard_map(chosen, mesh=mesh, in_specs=in_specs, out_specs=out_specs, check_vma=False)
```

```python
import functools
import math

import jax
import jax.numpy as jnp
from jax import lax
from jax.experimental import pallas as pl
from jax.experimental.pallas import tpu as pltpu
from jax.sharding import PartitionSpec as P

LX = 4
NW = 8
W = 128
NV = 1152
NT = 1024


def phases(site_ids, time_ids):
    points = jnp.arange(W, dtype=jnp.int32)
    moment = points // NW
    freq_index = points % NW
    kx_part = moment % LX
    ky_part = moment // LX
    rx_part = site_ids % LX
    ry_part = site_ids // LX
    winding = (2 * freq_index + 1)[:, None] * time_ids[None, :] + 2 * NT // LX * (
        kx_part[:, None] * rx_part[None, :] + ky_part[:, None] * ry_part[None, :]
    )
    winding = winding % (2 * NT)
    return winding.astype(jnp.float32) * (math.pi / NT)


def green_pair(matrix, site_ids, time_ids, spin_ids, free_green):
    angles = phases(site_ids, time_ids)
    cosine = jnp.cos(angles)
    sine_part = jnp.sin(angles)
    spin_up = (spin_ids == 0).astype(jnp.float32)[None, :]
    spin_down = (spin_ids == 1).astype(jnp.float32)[None, :]
    fourier_rows = jnp.concatenate(
        [cosine * spin_up, sine_part * spin_up, cosine * spin_down, sine_part * spin_down], 0
    ).astype(jnp.bfloat16)
    projected = jnp.dot(fourier_rows, matrix, preferred_element_type=jnp.float32).astype(
        jnp.bfloat16
    )
    norm_factor = 1.0 / math.sqrt(NV)
    real_free = free_green[0]
    imag_free = free_green[1]
    greens = []
    for spin_index in range(2):
        offset = 2 * W * spin_index
        cosine_rows = fourier_rows[offset : offset + W]
        sine_rows = fourier_rows[offset + W : offset + 2 * W]
        proj_real = projected[offset : offset + W]
        proj_imag = projected[offset + W : offset + 2 * W]
        left_block = jnp.concatenate(
            [
                jnp.concatenate([proj_real, proj_imag], 1),
                jnp.concatenate([proj_imag, -proj_real], 1),
            ],
            0,
        )
        right_block = jnp.concatenate([cosine_rows, sine_rows], 1)
        kernel = lax.dot_general(
            left_block, right_block, (((1,), (1,)), ((), ())), preferred_element_type=jnp.float32
        )
        kernel_real = kernel[:W]
        kernel_imag = kernel[W:]
        half_real = real_free[:, None] * kernel_real - imag_free[:, None] * kernel_imag
        half_imag = real_free[:, None] * kernel_imag + imag_free[:, None] * kernel_real
        green_real = (
            -(half_real * real_free[None, :] - half_imag * imag_free[None, :]) * norm_factor
        )
        green_imag = (
            -(half_real * imag_free[None, :] + half_imag * real_free[None, :]) * norm_factor
        )
        greens.append(jnp.stack([green_real, green_imag], 0))
    green_sum = (greens[0] + greens[1]).astype(jnp.bfloat16)
    return (green_sum, greens[0].astype(jnp.bfloat16), greens[1].astype(jnp.bfloat16))


def direct_terms(sums_piece, perm_row):
    column_ids = jnp.arange(sums_piece.shape[-1], dtype=jnp.int32)
    selector = (perm_row[:, None] == column_ids[None, :]).astype(jnp.bfloat16)
    halfway = jnp.einsum(
        "aj,kcbj->kcab", selector, sums_piece, preferred_element_type=jnp.float32
    ).astype(jnp.bfloat16)
    partner = jnp.einsum("kcaj,bj->kcab", halfway, selector, preferred_element_type=jnp.float32)
    local_copy = sums_piece.astype(jnp.float32)
    real_part = jnp.sum(local_copy[:, 0] * partner[:, 0] - local_copy[:, 1] * partner[:, 1], axis=0)
    imag_part = jnp.sum(local_copy[:, 0] * partner[:, 1] + local_copy[:, 1] * partner[:, 0], axis=0)
    return jnp.stack([real_part, imag_part], 0)


def copy_exchange(up_piece, down_piece, perm_row):
    column_ids = jnp.arange(up_piece.shape[-1], dtype=jnp.int32)
    spin_pieces = jnp.concatenate([up_piece, down_piece], 0)
    lead_values = spin_pieces[:, :, column_ids, perm_row]
    trail_values = spin_pieces[:, :, perm_row, column_ids]
    real_part = jnp.einsum(
        "ka,kb->ab", lead_values[:, 0], trail_values[:, 0], preferred_element_type=jnp.float32
    ) - jnp.einsum(
        "ka,kb->ab", lead_values[:, 1], trail_values[:, 1], preferred_element_type=jnp.float32
    )
    imag_part = jnp.einsum(
        "ka,kb->ab", lead_values[:, 0], trail_values[:, 1], preferred_element_type=jnp.float32
    ) + jnp.einsum(
        "ka,kb->ab", lead_values[:, 1], trail_values[:, 0], preferred_element_type=jnp.float32
    )
    return jnp.stack([real_part, imag_part], 0)


def plain_body(vertex_matrix, vertex_site, vertex_time, vertex_spin, free_green, plus_table, cross_table):
    green_sum, green_up, green_down = green_pair(
        vertex_matrix[0], vertex_site[0], vertex_time[0], vertex_spin[0], free_green
    )
    slices = plus_table.shape[0] // lax.axis_size("blk")
    owned_perms = lax.dynamic_slice_in_dim(plus_table, lax.axis_index("blk") * slices, slices, 0)
    sums_piece = lax.all_gather(green_sum[None], "blk", axis=0, tiled=True)
    up_piece = lax.all_gather(green_up[None], "blk", axis=0, tiled=True)
    down_piece = lax.all_gather(green_down[None], "blk", axis=0, tiled=True)

    def one_slice(perm_row):
        return direct_terms(sums_piece, perm_row) - copy_exchange(up_piece, down_piece, perm_row)

    transfer = jnp.swapaxes(lax.map(one_slice, owned_perms), 0, 1)
    shares = lax.psum_scatter(transfer, "group", scatter_dimension=3, tiled=True)
    regrouped = lax.all_to_all(shares, "blk", split_axis=2, concat_axis=1, tiled=True)
    row_ids = jnp.arange(regrouped.shape[2], dtype=jnp.int32)
    return regrouped[:, cross_table, row_ids[:, None], :]


BF = jnp.bfloat16
F32 = jnp.float32
MESH = pl.DeviceIdType.MESH
INNER = 2
CORES = 2
PARTS = 4
CHUNKS = 3


def iota(shape, dim):
    return lax.broadcasted_iota(jnp.int32, shape, dim)


def shift_down(value, divisor):
    return value >> (divisor.bit_length() - 1)


def one_hot(condition):
    return jnp.where(condition, 1.0, 0.0).astype(BF)


def dot(left, right):
    return jnp.dot(left, right, preferred_element_type=F32)


def dot_nt(left, right):
    return lax.dot_general(left, right, (((1,), (1,)), ((), ())), preferred_element_type=F32)


def kernel(
    nblk,
    ngroup,
    site_hbm,
    time_hbm,
    spin_hbm,
    free_hbm,
    plus_hbm,
    cross_hbm,
    matrix_hbm,
    out_ref,
    site_ref,
    time_ref,
    spin_ref,
    free_ref,
    plus_ref,
    cross_ref,
    total,
    matrix,
    rows,
    kern,
    st,
    lr,
    lr_send,
    sel_b,
    sel_a,
    sel_out,
    spread,
    prow,
    sb,
    halfway,
    tsend,
    trecv,
    small_sem,
    matrix_sem,
    st_send,
    st_recv,
    lr_send_sem,
    lr_recv,
    t_send,
    t_recv,
):
    small = [
        pltpu.make_async_copy(source, target, small_sem.at[place])
        for place, (source, target) in enumerate(
            [
                (site_hbm, site_ref),
                (time_hbm, time_ref),
                (spin_hbm, spin_ref),
                (free_hbm, free_ref),
                (plus_hbm, plus_ref),
                (cross_hbm, cross_ref),
            ]
        )
    ]
    for copy in small:
        copy.start()

    nz = nblk // INNER
    na = W // nblk
    nb = W // ngroup
    nq = plus_ref.shape[0]
    half = na * nz
    npair = nq // 2
    nchunk = W // na
    nv = site_ref.shape[1]
    piece = nv // CHUNKS
    blk = lax.axis_index("blk")
    grp = lax.axis_index("group")
    zz = blk // INNER
    yy = blk % INNER
    nx = ngroup // CORES
    xx = grp // CORES
    core = grp % CORES
    near = nx * INNER
    plane = list(range(1, CORES * near))

    def plane_peer(slot):
        dc, dy, dx = slot // near, slot // nx % INNER, slot % nx
        return (
            zz * INNER + (yy + dy) % INNER,
            (xx + dx) % nx * CORES + (core + dc) % CORES,
        )

    def z_peer(dz):
        return (((zz + dz) % nz) * INNER + yy, grp)

    barrier = pltpu.get_barrier_semaphore()
    for slot in plane:
        pl.semaphore_signal(barrier, inc=1, device_id=plane_peer(slot), device_id_type=MESH)
    for dz in range(1, nz):
        pl.semaphore_signal(barrier, inc=1, device_id=z_peer(dz), device_id_type=MESH)

    def matrix_copy(index):
        cols = pl.ds(pl.multiple_of(index * piece, 128), piece)
        return pltpu.make_async_copy(
            matrix_hbm.at[:, cols], matrix.at[:, cols], matrix_sem.at[index]
        )

    for index in range(CHUNKS):
        matrix_copy(index).start()

    for copy in small:
        copy.wait()

    quarter = NT // 2
    site = jnp.broadcast_to(site_ref[...], (2 * NW, nv))
    rx = site & (LX - 1)
    ry = shift_down(site, LX)
    ids = iota((2 * NW, nv), 0)
    freq = ids & (NW - 1)
    upper = shift_down(ids, NW)
    winding = (2 * freq + 1) * time_ref[...]
    turns = shift_down(winding + quarter // 2, quarter)
    rest = (winding - turns * quarter).astype(F32) * (math.pi / NT)
    square = rest * rest
    cosine = 1.0 + square * (
        -1 / 2
        + square
        * (1 / 24 + square * (-1 / 720 + square * (1 / 40320 + square * (-1 / 3628800))))
    )
    sine = rest + rest * square * (
        -1 / 6 + square * (1 / 120 + square * (-1 / 5040 + square * (1 / 362880)))
    )
    cosine = cosine.astype(BF)
    sine = sine.astype(BF)

    def unit(amount):
        amount = amount & 3
        real = jnp.where(amount == 0, 1.0, jnp.where(amount == 2, -1.0, 0.0))
        imag = jnp.where(amount == 1, 1.0, jnp.where(amount == 3, -1.0, 0.0))
        return real.astype(BF), imag.astype(BF)

    def turn(value, by):
        return (value[0] * by[0] - value[1] * by[1], value[1] * by[0] + value[0] * by[1])

    spin = jnp.broadcast_to(spin_ref[...], (2 * NW, nv))
    up = one_hot(spin == 0)
    down = one_hot(spin == 1)
    across = [unit((kx + upper) * rx) for kx in range(0, LX, 2)]
    for ky in range(W // NW // LX):
        base = turn((cosine, sine), unit(turns + ky * ry))
        for place, by in enumerate(across):
            c_both, s_both = turn(base, by)
            at = (ky * LX + 2 * place) * NW
            rows[pl.ds(at, 2 * NW), :] = c_both * up
            rows[pl.ds(W + at, 2 * NW), :] = s_both * up
            rows[pl.ds(2 * W + at, 2 * NW), :] = c_both * down
            rows[pl.ds(3 * W + at, 2 * NW), :] = s_both * down

    kern[...] = jnp.zeros_like(kern)

    def project(index, carry):
        matrix_copy(index).wait()
        cols = pl.ds(pl.multiple_of(index * piece, 128), piece)
        projected = dot(rows[...], matrix[:, cols]).astype(BF)
        for s in range(2):
            kern[s] += dot_nt(
                projected[2 * W * s : 2 * W * (s + 1)], rows[pl.ds(2 * W * s, 2 * W), cols]
            )
        return carry

    lax.fori_loop(0, CHUNKS, project, 0)

    ga_re = jnp.broadcast_to(free_ref[0:1, :], (W, W))
    ga_im = jnp.broadcast_to(free_ref[1:2, :], (W, W))
    gb_re, gb_im = ga_re, ga_im
    ga_re = ga_re.T
    ga_im = ga_im.T
    norm_factor = 1.0 / math.sqrt(NV)
    greens = []
    for s in range(2):
        k_re = kern[s, :W, :W] + kern[s, W:, W:]
        k_im = kern[s, W:, :W] - kern[s, :W, W:]
        h_re = ga_re * k_re - ga_im * k_im
        h_im = ga_re * k_im + ga_im * k_re
        greens.append(-(h_re * gb_re - h_im * gb_im) * norm_factor)
        greens.append(-(h_re * gb_im + h_im * gb_re) * norm_factor)
    turned = [g.T for g in greens]
    st[0, :W, :] = (turned[0] + turned[2]).astype(BF)
    st[0, W:, :] = (turned[1] + turned[3]).astype(BF)

    pl.semaphore_wait(barrier, len(plane) + nz - 1)

    def st_copy(source, slot, steps):
        return pltpu.make_async_remote_copy(
            src_ref=st.at[source],
            dst_ref=st.at[slot],
            send_sem=st_send.at[slot],
            recv_sem=st_recv.at[slot],
            device_id=plane_peer(steps),
            device_id_type=MESH,
        )

    def lr_copy(slot):
        peer = plane_peer(slot)
        wanted = peer[0] % INNER * ngroup + peer[1]
        return pltpu.make_async_remote_copy(
            src_ref=lr_send.at[wanted],
            dst_ref=lr.at[slot],
            send_sem=lr_send_sem.at[slot],
            recv_sem=lr_recv.at[slot],
            device_id=peer,
            device_id_type=MESH,
        )

    for slot in range(near - 1, 0, -1):
        st_copy(0, slot, slot).start()
    st_copy(0, near, near).start()

    greens = [g.astype(BF).astype(F32) for g in greens]
    turned = [g.astype(BF).astype(F32) for g in turned]
    plus = plus_ref[...].astype(F32)
    plus_turned = jnp.concatenate([plus, jnp.zeros((W - nq, W), F32)], 0).T
    expand = one_hot(shift_down(iota((W, W), 1), PARTS) == iota((W, W), 0))
    index = dot(plus_turned.astype(BF), expand).astype(jnp.int32)
    lane = iota((W, W), 1)
    part = lane & (PARTS - 1)

    def choose(values):
        picked = values[0]
        for g in range(1, PARTS):
            picked = jnp.where(part == g, values[g], picked)
        return picked

    lead = choose([jnp.take_along_axis(g, index, axis=1) for g in greens])
    trail = [jnp.take_along_axis(g, index, axis=1) for g in turned]
    trail_re = choose([trail[0], -trail[1], trail[2], -trail[3]]).T
    trail_im = choose([trail[1], trail[0], trail[3], trail[2]]).T
    order = [INNER * z + y for y in range(INNER) for z in range(nz)]
    lead = jnp.concatenate([lead[na * i : na * (i + 1)] for i in order], 0).T

    def shifted(value, by):
        by = by % W
        return value if by == 0 else pltpu.roll(value, by, 1)

    for j in range(ngroup):
        left = jnp.where(
            lane < nb, shifted(trail_re, -nb * j), shifted(trail_im, nb - nb * j)
        )
        for y in range(INNER):
            joined = jnp.where(lane < half, left, shifted(lead, half - half * y))
            lr_send[y * ngroup + j] = joined.astype(BF)
    for slot in plane:
        lr_copy(slot).start()
    lr[0] = lr_send[yy * ngroup + grp]

    plus_bf = plus.astype(BF)
    my_b = one_hot(iota((nb, W), 1) == iota((nb, W), 0) + nb * grp)
    plus_b = dot_nt(my_b, plus_bf).astype(jnp.int32)
    for q in range(nq):
        column = jnp.broadcast_to(plus_b[:, q : q + 1], (nb, W))
        sel_b[pl.ds(q * nb, nb), :] = one_hot(column == iota((nb, W), 1))
    place = shift_down(lane & (half - 1), na) * (na * INNER) + na * yy + (lane & (na - 1))
    my_a = one_hot(iota((W, W), 0) == place)
    prow[...] = dot(plus_bf, my_a)

    def pair_selector(pair, carry):
        first = prow[pl.ds(2 * pair, 1), :]
        second = prow[pl.ds(2 * pair + 1, 1), :]
        low = lane < half
        hit = iota((W, W), 0) == jnp.where(
            low, jnp.broadcast_to(first, (W, W)), jnp.broadcast_to(second, (W, W))
        ).astype(jnp.int32)
        sel_a[pair, :W, :] = one_hot(hit & low)
        sel_a[pair, W:, :] = one_hot(hit & (lane >= half))
        return carry

    lax.fori_loop(0, npair, pair_selector, 0)

    width = nz * W
    source = iota((width, W), 0)
    target = (
        (shift_down(source, na) & (nz - 1)) * W
        + shift_down(source, half) * na
        + (source & (na - 1))
    )
    for z in range(nz):
        spread[:, z * W : (z + 1) * W] = one_hot(target == iota((width, W), 1) + z * W)

    same = one_hot(iota((nq, nq), 0) == iota((nq, nq), 1))
    crossing = dot_nt(same, cross_ref[...].astype(F32).astype(BF)).astype(jnp.int32)
    for r in range(na):
        column = jnp.broadcast_to(crossing[:, r : r + 1] * na + r, (nq, nq * na))
        sel_out[pl.ds(r * nq, nq), :] = one_hot(column == iota((nq, nq * na), 1))

    def first_selection(slot):
        for c in range(2):
            mine = st[slot, pl.ds(pl.multiple_of(c * W + nb * grp, nb), nb), :]
            sb[slot, c] = dot(mine, my_a)
            chosen = dot_nt(sel_b[...], st[slot, c * W : (c + 1) * W, :]).astype(BF)
            for q in range(nq):
                halfway[q // 2, slot, c, :, pl.ds((q % 2) * W, W)] = chosen[
                    q * nb : (q + 1) * nb
                ]

    def own_chip(step, carry):
        @pl.when(step > 0)
        def _():
            st_copy(0, near, near).wait_recv()

        first_selection(step * near)
        return carry

    def same_core(step, carry):
        st_copy(0, step, near).wait_recv()
        st_copy(step, near + step, near).start()
        first_selection(step)
        return carry

    def forwarded(step, carry):
        st_copy(0, step, near).wait_recv()
        first_selection(step)
        return carry

    lax.fori_loop(0, CORES, own_chip, 0)
    lax.fori_loop(1, near, same_core, 0)
    lax.fori_loop(near + 1, CORES * near, forwarded, 0)

    for slot in plane:
        lr_copy(slot).wait_recv()

    nw = len(plane) + 1
    four = W // (nw * PARTS)
    depth = four * PARTS

    def t_copy(dz, chunk):
        cols = pl.ds(pl.multiple_of(chunk * W, W), W)
        return pltpu.make_async_remote_copy(
            src_ref=tsend.at[(zz + dz) % nz, :, cols],
            dst_ref=trecv.at[dz, :, cols],
            send_sem=t_send.at[dz, chunk],
            recv_sem=t_recv.at[dz, chunk],
            device_id=z_peer(dz),
            device_id_type=MESH,
        )

    same_q = shift_down(iota((W, W), 0) & (depth - 1), PARTS) - shift_down(lane, half)

    def measure_chunk(chunk, carry):
        totals = []
        for sub in range(nz):
            pair = chunk * nz + sub
            partner = dot(halfway[pair].reshape(nw * 2 * nb, 2 * W), sel_a[pair])
            t_re = jnp.zeros((nb, W), F32)
            t_im = jnp.zeros((nb, W), F32)
            for w in range(nw):
                s_re = sb[w, 0]
                s_im = sb[w, 1]
                p_re = partner[2 * nb * w : 2 * nb * w + nb]
                p_im = partner[2 * nb * w + nb : 2 * nb * (w + 1)]
                t_re = t_re + (s_re * p_re - s_im * p_im)
                t_im = t_im + (s_re * p_im + s_im * p_re)
            pairs = four // 2
            if sub % pairs == 0:
                start = pl.multiple_of((chunk * (nz // pairs) + sub // pairs) * depth, depth)
                stacked = lr[:, pl.ds(start, depth), :].reshape(W, W).astype(F32)
                trailing = stacked.T[:half].astype(BF)
                leading = jnp.where(lane < half, pltpu.roll(stacked, half, 1), stacked)
            masked = jnp.where(same_q == 2 * (sub % pairs), leading, 0.0)
            exchange = dot(trailing, masked.astype(BF))
            totals.append((jnp.concatenate([t_re, t_im], 0) - exchange).astype(BF))
        moved = dot(jnp.concatenate(totals, 1), spread[...]).astype(BF)
        cols = pl.ds(pl.multiple_of(chunk * W, W), W)
        for z in range(nz):
            tsend[z, :, cols] = moved[:, z * W : (z + 1) * W]
        for dz in range(1, nz):
            t_copy(dz, chunk).start()
        return carry

    chunks = nq // nchunk
    lax.fori_loop(0, chunks, measure_chunk, 0)

    total[...] = dot_nt(sel_out[...], tsend[zz])
    for dz in range(1, nz):
        for chunk in range(chunks):
            t_copy(dz, chunk).wait_recv()
        total[...] += dot_nt(sel_out[...], trecv[dz])
    for c in range(2):
        out_ref[c] = total[:, c * nb : (c + 1) * nb].reshape(na, nq, nb)

    for slot in plane:
        st_copy(0, slot, near).wait_send()
        lr_copy(slot).wait_send()
    for dz in range(1, nz):
        for chunk in range(chunks):
            t_copy(dz, chunk).wait_send()


def kernel_body(
    vertex_matrix, vertex_site, vertex_time, vertex_spin, free_green, plus_table, cross_table
):
    nblk = lax.axis_size("blk")
    ngroup = lax.axis_size("group")
    nv = vertex_matrix.shape[-1]
    nq = plus_table.shape[0]
    nz = nblk // INNER
    na = W // nblk
    nb = W // ngroup
    nw = INNER * ngroup
    npair = nq // 2
    chunks = nq // (W // na)
    vmem = pl.BlockSpec(memory_space=pltpu.VMEM)
    dma = pltpu.SemaphoreType.DMA
    return pl.pallas_call(
        functools.partial(kernel, nblk, ngroup),
        out_shape=jax.ShapeDtypeStruct((2, na, nq, nb), F32),
        in_specs=[pl.BlockSpec(memory_space=pltpu.HBM)] * 7,
        out_specs=vmem,
        scratch_shapes=[
            pltpu.VMEM(vertex_site.shape, jnp.int32),
            pltpu.VMEM(vertex_time.shape, jnp.int32),
            pltpu.VMEM(vertex_spin.shape, jnp.int32),
            pltpu.VMEM(free_green.shape, F32),
            pltpu.VMEM(plus_table.shape, jnp.int32),
            pltpu.VMEM(cross_table.shape, jnp.int32),
            pltpu.VMEM((na * nq, 2 * nb), F32),
            pltpu.VMEM((nv, nv), BF),
            pltpu.VMEM((4 * W, nv), BF),
            pltpu.VMEM((2, 2 * W, 2 * W), F32),
            pltpu.VMEM((nw, 2 * W, W), BF),
            pltpu.VMEM((nw, W, W), BF),
            pltpu.VMEM((nw, W, W), BF),
            pltpu.VMEM((nq * nb, W), BF),
            pltpu.VMEM((npair, 2 * W, W), BF),
            pltpu.VMEM((na * nq, nq * na), BF),
            pltpu.VMEM((nz * W, nz * W), BF),
            pltpu.VMEM((nq, W), F32),
            pltpu.VMEM((nw, 2, nb, W), F32),
            pltpu.VMEM((npair, nw, 2, nb, 2 * W), BF),
            pltpu.VMEM((nz, 2 * nb, nq * na), BF),
            pltpu.VMEM((nz, 2 * nb, nq * na), BF),
            dma((6,)),
            dma((CHUNKS,)),
            dma((nw,)),
            dma((nw,)),
            dma((nw,)),
            dma((nw,)),
            dma((nz, chunks)),
            dma((nz, chunks)),
        ],
        compiler_params=pltpu.CompilerParams(
            collective_id=0, has_side_effects=True, vmem_limit_bytes=63 * 1024 * 1024
        ),
    )(
        vertex_site,
        vertex_time,
        vertex_spin,
        free_green,
        plus_table,
        cross_table,
        vertex_matrix[0],
    )


def fits(mesh):
    nblk, ngroup = mesh.shape["blk"], mesh.shape["group"]
    if nblk % INNER or W % nblk or W % ngroup:
        return False
    nz, na, nb = nblk // INNER, W // nblk, W // ngroup
    return nz == 4 and ngroup % CORES == 0 and 2 * nz * na == W and 4 * nb == W and na % 16 == 0 and nb % 16 == 0


def solution(mesh):
    in_specs = (
        P(("blk", "group"), None, None),
        P(("blk", "group"), None),
        P(("blk", "group"), None),
        P(("blk", "group"), None),
        P(),
        P(),
        P("blk", None),
    )
    out_specs = P(None, "blk", None, "group")

    def chosen(*args):
        matrix, plus = args[0], args[5]
        small = fits(mesh) and PARTS * plus.shape[0] == W and matrix.shape[-1] % (128 * CHUNKS) == 0
        return (kernel_body if small else plain_body)(*args)

    return jax.shard_map(chosen, mesh=mesh, in_specs=in_specs, out_specs=out_specs, check_vma=False)
```

```python
import functools
import math

import jax
import jax.numpy as jnp
from jax import lax
from jax.experimental import pallas as pl
from jax.experimental.pallas import tpu as pltpu
from jax.sharding import PartitionSpec as P

LX = 4
NW = 8
W = 128
NV = 1152
NT = 1024


def phases(site_ids, time_ids):
    points = jnp.arange(W, dtype=jnp.int32)
    moment = points // NW
    freq_index = points % NW
    kx_part = moment % LX
    ky_part = moment // LX
    rx_part = site_ids % LX
    ry_part = site_ids // LX
    winding = (2 * freq_index + 1)[:, None] * time_ids[None, :] + 2 * NT // LX * (
        kx_part[:, None] * rx_part[None, :] + ky_part[:, None] * ry_part[None, :]
    )
    winding = winding % (2 * NT)
    return winding.astype(jnp.float32) * (math.pi / NT)


def green_pair(matrix, site_ids, time_ids, spin_ids, free_green):
    angles = phases(site_ids, time_ids)
    cosine = jnp.cos(angles)
    sine_part = jnp.sin(angles)
    spin_up = (spin_ids == 0).astype(jnp.float32)[None, :]
    spin_down = (spin_ids == 1).astype(jnp.float32)[None, :]
    fourier_rows = jnp.concatenate(
        [cosine * spin_up, sine_part * spin_up, cosine * spin_down, sine_part * spin_down], 0
    ).astype(jnp.bfloat16)
    projected = jnp.dot(fourier_rows, matrix, preferred_element_type=jnp.float32).astype(
        jnp.bfloat16
    )
    norm_factor = 1.0 / math.sqrt(NV)
    real_free = free_green[0]
    imag_free = free_green[1]
    greens = []
    for spin_index in range(2):
        offset = 2 * W * spin_index
        cosine_rows = fourier_rows[offset : offset + W]
        sine_rows = fourier_rows[offset + W : offset + 2 * W]
        proj_real = projected[offset : offset + W]
        proj_imag = projected[offset + W : offset + 2 * W]
        left_block = jnp.concatenate(
            [
                jnp.concatenate([proj_real, proj_imag], 1),
                jnp.concatenate([proj_imag, -proj_real], 1),
            ],
            0,
        )
        right_block = jnp.concatenate([cosine_rows, sine_rows], 1)
        kernel = lax.dot_general(
            left_block, right_block, (((1,), (1,)), ((), ())), preferred_element_type=jnp.float32
        )
        kernel_real = kernel[:W]
        kernel_imag = kernel[W:]
        half_real = real_free[:, None] * kernel_real - imag_free[:, None] * kernel_imag
        half_imag = real_free[:, None] * kernel_imag + imag_free[:, None] * kernel_real
        green_real = (
            -(half_real * real_free[None, :] - half_imag * imag_free[None, :]) * norm_factor
        )
        green_imag = (
            -(half_real * imag_free[None, :] + half_imag * real_free[None, :]) * norm_factor
        )
        greens.append(jnp.stack([green_real, green_imag], 0))
    green_sum = (greens[0] + greens[1]).astype(jnp.bfloat16)
    return (green_sum, greens[0].astype(jnp.bfloat16), greens[1].astype(jnp.bfloat16))


def direct_terms(sums_piece, perm_row):
    column_ids = jnp.arange(sums_piece.shape[-1], dtype=jnp.int32)
    selector = (perm_row[:, None] == column_ids[None, :]).astype(jnp.bfloat16)
    halfway = jnp.einsum(
        "aj,kcbj->kcab", selector, sums_piece, preferred_element_type=jnp.float32
    ).astype(jnp.bfloat16)
    partner = jnp.einsum("kcaj,bj->kcab", halfway, selector, preferred_element_type=jnp.float32)
    local_copy = sums_piece.astype(jnp.float32)
    real_part = jnp.sum(local_copy[:, 0] * partner[:, 0] - local_copy[:, 1] * partner[:, 1], axis=0)
    imag_part = jnp.sum(local_copy[:, 0] * partner[:, 1] + local_copy[:, 1] * partner[:, 0], axis=0)
    return jnp.stack([real_part, imag_part], 0)


def copy_exchange(up_piece, down_piece, perm_row):
    column_ids = jnp.arange(up_piece.shape[-1], dtype=jnp.int32)
    spin_pieces = jnp.concatenate([up_piece, down_piece], 0)
    lead_values = spin_pieces[:, :, column_ids, perm_row]
    trail_values = spin_pieces[:, :, perm_row, column_ids]
    real_part = jnp.einsum(
        "ka,kb->ab", lead_values[:, 0], trail_values[:, 0], preferred_element_type=jnp.float32
    ) - jnp.einsum(
        "ka,kb->ab", lead_values[:, 1], trail_values[:, 1], preferred_element_type=jnp.float32
    )
    imag_part = jnp.einsum(
        "ka,kb->ab", lead_values[:, 0], trail_values[:, 1], preferred_element_type=jnp.float32
    ) + jnp.einsum(
        "ka,kb->ab", lead_values[:, 1], trail_values[:, 0], preferred_element_type=jnp.float32
    )
    return jnp.stack([real_part, imag_part], 0)


def plain_body(vertex_matrix, vertex_site, vertex_time, vertex_spin, free_green, plus_table, cross_table):
    green_sum, green_up, green_down = green_pair(
        vertex_matrix[0], vertex_site[0], vertex_time[0], vertex_spin[0], free_green
    )
    slices = plus_table.shape[0] // lax.axis_size("blk")
    owned_perms = lax.dynamic_slice_in_dim(plus_table, lax.axis_index("blk") * slices, slices, 0)
    sums_piece = lax.all_gather(green_sum[None], "blk", axis=0, tiled=True)
    up_piece = lax.all_gather(green_up[None], "blk", axis=0, tiled=True)
    down_piece = lax.all_gather(green_down[None], "blk", axis=0, tiled=True)

    def one_slice(perm_row):
        return direct_terms(sums_piece, perm_row) - copy_exchange(up_piece, down_piece, perm_row)

    transfer = jnp.swapaxes(lax.map(one_slice, owned_perms), 0, 1)
    shares = lax.psum_scatter(transfer, "group", scatter_dimension=3, tiled=True)
    regrouped = lax.all_to_all(shares, "blk", split_axis=2, concat_axis=1, tiled=True)
    row_ids = jnp.arange(regrouped.shape[2], dtype=jnp.int32)
    return regrouped[:, cross_table, row_ids[:, None], :]


BF = jnp.bfloat16
F32 = jnp.float32
MESH = pl.DeviceIdType.MESH
INNER = 2
CORES = 2
VMEM_BYTES = 64 * 1024 * 1024
PARTS = 4
CHUNKS = 3


def iota(shape, dim):
    return lax.broadcasted_iota(jnp.int32, shape, dim)


def shift_down(value, divisor):
    return value >> (divisor.bit_length() - 1)


def one_hot(condition):
    return jnp.where(condition, 1.0, 0.0).astype(BF)


def dot(left, right):
    return jnp.dot(left, right, preferred_element_type=F32)


def dot_nt(left, right):
    return lax.dot_general(left, right, (((1,), (1,)), ((), ())), preferred_element_type=F32)


def kernel(
    nblk,
    ngroup,
    site_hbm,
    time_hbm,
    spin_hbm,
    free_hbm,
    plus_hbm,
    cross_hbm,
    matrix_hbm,
    out_ref,
    site_ref,
    time_ref,
    spin_ref,
    free_ref,
    plus_ref,
    cross_ref,
    matrix,
    rows,
    kern,
    st,
    lr,
    lr_send,
    sel_b,
    sel_a,
    sel_out,
    prow,
    sb,
    halfway,
    tsend,
    trecv,
    small_sem,
    matrix_sem,
    st_send,
    st_recv,
    lr_send_sem,
    lr_recv,
    t_send,
    t_recv,
):
    small = [
        pltpu.make_async_copy(source, target, small_sem.at[place])
        for place, (source, target) in enumerate(
            [
                (site_hbm, site_ref),
                (time_hbm, time_ref),
                (spin_hbm, spin_ref),
                (free_hbm, free_ref),
                (plus_hbm, plus_ref),
                (cross_hbm, cross_ref),
            ]
        )
    ]
    for copy in small:
        copy.start()

    nz = nblk // INNER
    na = W // nblk
    nb = W // ngroup
    nq = plus_ref.shape[0]
    half = na * nz
    npair = nq // 2
    nchunk = W // na
    nv = site_ref.shape[1]
    piece = nv // CHUNKS
    blk = lax.axis_index("blk")
    grp = lax.axis_index("group")
    zz = blk // INNER
    yy = blk % INNER
    nx = ngroup // CORES
    xx = grp // CORES
    core = grp % CORES
    near = nx * INNER
    plane = list(range(1, CORES * near))

    def plane_peer(slot):
        dc, dy, dx = slot // near, slot // nx % INNER, slot % nx
        return (
            zz * INNER + (yy + dy) % INNER,
            (xx + dx) % nx * CORES + (core + dc) % CORES,
        )

    def z_peer(dz):
        return (((zz + dz) % nz) * INNER + yy, grp)

    barrier = pltpu.get_barrier_semaphore()
    for slot in plane:
        pl.semaphore_signal(barrier, inc=1, device_id=plane_peer(slot), device_id_type=MESH)
    for dz in range(1, nz):
        pl.semaphore_signal(barrier, inc=1, device_id=z_peer(dz), device_id_type=MESH)

    def matrix_copy(index):
        cols = pl.ds(pl.multiple_of(index * piece, 128), piece)
        return pltpu.make_async_copy(
            matrix_hbm.at[:, cols], matrix.at[:, cols], matrix_sem.at[index]
        )

    for index in range(CHUNKS):
        matrix_copy(index).start()

    for copy in small:
        copy.wait()

    quarter = NT // 2
    site = jnp.broadcast_to(site_ref[...], (2 * NW, nv))
    rx = site & (LX - 1)
    ry = shift_down(site, LX)
    ids = iota((2 * NW, nv), 0)
    freq = ids & (NW - 1)
    upper = shift_down(ids, NW)
    winding = (2 * freq + 1) * time_ref[...]
    turns = shift_down(winding + quarter // 2, quarter)
    rest = (winding - turns * quarter).astype(F32) * (math.pi / NT)
    square = rest * rest
    cosine = 1.0 + square * (
        -1 / 2
        + square
        * (1 / 24 + square * (-1 / 720 + square * (1 / 40320 + square * (-1 / 3628800))))
    )
    sine = rest + rest * square * (
        -1 / 6 + square * (1 / 120 + square * (-1 / 5040 + square * (1 / 362880)))
    )
    cosine = cosine.astype(BF)
    sine = sine.astype(BF)

    def unit(amount):
        amount = amount & 3
        real = jnp.where(amount == 0, 1.0, jnp.where(amount == 2, -1.0, 0.0))
        imag = jnp.where(amount == 1, 1.0, jnp.where(amount == 3, -1.0, 0.0))
        return real.astype(BF), imag.astype(BF)

    def turn(value, by):
        return (value[0] * by[0] - value[1] * by[1], value[1] * by[0] + value[0] * by[1])

    spin = jnp.broadcast_to(spin_ref[...], (2 * NW, nv))
    up = one_hot(spin == 0)
    down = one_hot(spin == 1)
    across = [unit((kx + upper) * rx) for kx in range(0, LX, 2)]
    for ky in range(W // NW // LX):
        base = turn((cosine, sine), unit(turns + ky * ry))
        for place, by in enumerate(across):
            c_both, s_both = turn(base, by)
            at = (ky * LX + 2 * place) * NW
            rows[pl.ds(at, 2 * NW), :] = c_both * up
            rows[pl.ds(W + at, 2 * NW), :] = s_both * up
            rows[pl.ds(2 * W + at, 2 * NW), :] = c_both * down
            rows[pl.ds(3 * W + at, 2 * NW), :] = s_both * down

    kern[...] = jnp.zeros_like(kern)

    def project(index, carry):
        matrix_copy(index).wait()
        cols = pl.ds(pl.multiple_of(index * piece, 128), piece)
        projected = dot(rows[...], matrix[:, cols]).astype(BF)
        for s in range(2):
            kern[s] += dot_nt(
                projected[2 * W * s : 2 * W * (s + 1)], rows[pl.ds(2 * W * s, 2 * W), cols]
            )
        return carry

    lax.fori_loop(0, CHUNKS, project, 0)

    ga_re = jnp.broadcast_to(free_ref[0:1, :], (W, W))
    ga_im = jnp.broadcast_to(free_ref[1:2, :], (W, W))
    gb_re, gb_im = ga_re, ga_im
    ga_re = ga_re.T
    ga_im = ga_im.T
    norm_factor = 1.0 / math.sqrt(NV)
    greens = []
    for s in range(2):
        k_re = kern[s, :W, :W] + kern[s, W:, W:]
        k_im = kern[s, W:, :W] - kern[s, :W, W:]
        h_re = ga_re * k_re - ga_im * k_im
        h_im = ga_re * k_im + ga_im * k_re
        greens.append(-(h_re * gb_re - h_im * gb_im) * norm_factor)
        greens.append(-(h_re * gb_im + h_im * gb_re) * norm_factor)
    turned = [g.T for g in greens]
    st[0, :W, :] = (turned[0] + turned[2]).astype(BF)
    st[0, W:, :] = (turned[1] + turned[3]).astype(BF)

    pl.semaphore_wait(barrier, len(plane) + nz - 1)

    def st_copy(source, slot, steps):
        return pltpu.make_async_remote_copy(
            src_ref=st.at[source],
            dst_ref=st.at[slot],
            send_sem=st_send.at[slot],
            recv_sem=st_recv.at[slot],
            device_id=plane_peer(steps),
            device_id_type=MESH,
        )

    def lr_copy(source, slot, steps):
        return pltpu.make_async_remote_copy(
            src_ref=source,
            dst_ref=lr.at[slot],
            send_sem=lr_send_sem.at[slot],
            recv_sem=lr_recv.at[slot],
            device_id=plane_peer(steps),
            device_id_type=MESH,
        )

    def lr_for(slot):
        dy, dx = slot // nx % INNER, slot % nx
        return lr_send.at[(yy + dy) % INNER * nx + (xx + dx) % nx]

    for slot in range(near - 1, 0, -1):
        st_copy(0, slot, slot).start()
    st_copy(0, near, near).start()

    greens = [g.astype(BF).astype(F32) for g in greens]
    turned = [g.astype(BF).astype(F32) for g in turned]
    plus = plus_ref[...].astype(F32)
    plus_turned = jnp.concatenate([plus, jnp.zeros((W - nq, W), F32)], 0).T
    expand = one_hot(shift_down(iota((W, W), 1), PARTS) == iota((W, W), 0))
    index = dot(plus_turned.astype(BF), expand).astype(jnp.int32)
    lane = iota((W, W), 1)
    part = lane & (PARTS - 1)

    def choose(values):
        picked = values[0]
        for g in range(1, PARTS):
            picked = jnp.where(part == g, values[g], picked)
        return picked

    lead = choose([jnp.take_along_axis(g, index, axis=1) for g in greens])
    trail = [jnp.take_along_axis(g, index, axis=1) for g in turned]
    trail = choose(trail).T
    order = [INNER * z + y for y in range(INNER) for z in range(nz)]
    lead = jnp.concatenate([lead[na * i : na * (i + 1)] for i in order], 0).T

    def shifted(value, by):
        by = by % W
        return value if by == 0 else pltpu.roll(value, by, 1)

    for x in range(nx):
        left = shifted(trail, -half * x)
        for y in range(INNER):
            joined = jnp.where(lane < half, left, shifted(lead, half - half * y))
            lr_send[y * nx + x] = joined.astype(BF)
    for slot in range(near - 1, 0, -1):
        lr_copy(lr_for(slot), slot, slot).start()
    lr_copy(lr_for(near), near, near).start()
    lr[0] = lr_send[yy * nx + xx]

    plus_bf = plus.astype(BF)
    my_b = one_hot(iota((nb, W), 1) == iota((nb, W), 0) + nb * grp)
    plus_b = dot_nt(my_b, plus_bf).astype(jnp.int32)
    for q in range(nq):
        column = jnp.broadcast_to(plus_b[:, q : q + 1], (nb, W))
        sel_b[pl.ds(q * nb, nb), :] = one_hot(column == iota((nb, W), 1))
    place = shift_down(lane & (half - 1), na) * (na * INNER) + na * yy + (lane & (na - 1))
    my_a = one_hot(iota((W, W), 0) == place)
    prow[...] = dot(plus_bf, my_a)

    def pair_selector(pair, carry):
        first = prow[pl.ds(2 * pair, 1), :]
        second = prow[pl.ds(2 * pair + 1, 1), :]
        low = lane < half
        hit = iota((W, W), 0) == jnp.where(
            low, jnp.broadcast_to(first, (W, W)), jnp.broadcast_to(second, (W, W))
        ).astype(jnp.int32)
        sel_a[pair, :W, :] = one_hot(hit & low)
        sel_a[pair, W:, :] = one_hot(hit & (lane >= half))
        return carry

    lax.fori_loop(0, npair, pair_selector, 0)

    same = one_hot(iota((nq, nq), 0) == iota((nq, nq), 1))
    crossing = dot_nt(same, cross_ref[...].astype(F32).astype(BF)).astype(jnp.int32)
    crossing = (
        shift_down(crossing, nchunk) * W
        + (crossing & 1) * half
        + (shift_down(crossing, 2) & (nz - 1)) * na
    )
    for r in range(na):
        column = jnp.broadcast_to(crossing[:, r : r + 1] + r, (nq, nq * na))
        sel_out[pl.ds(r * nq, nq), :] = one_hot(column == iota((nq, nq * na), 1))

    def first_selection(slot):
        for c in range(2):
            mine = st[slot, pl.ds(pl.multiple_of(c * W + nb * grp, nb), nb), :]
            sb[slot, c] = dot(mine, my_a)
            chosen = dot_nt(sel_b[...], st[slot, c * W : (c + 1) * W, :]).astype(BF)
            for q in range(nq):
                halfway[q // 2, slot, c, :, pl.ds((q % 2) * W, W)] = chosen[
                    q * nb : (q + 1) * nb
                ]

    def own_chip(step, carry):
        @pl.when(step > 0)
        def _():
            st_copy(0, near, near).wait_recv()

        first_selection(step * near)
        return carry

    def same_core(step, carry):
        st_copy(0, step, near).wait_recv()
        st_copy(step, near + step, near).start()
        first_selection(step)
        return carry

    def forwarded(step, carry):
        st_copy(0, step, near).wait_recv()
        first_selection(step)
        return carry

    lax.fori_loop(0, CORES, own_chip, 0)
    lax.fori_loop(1, near, same_core, 0)
    for slot in range(1, near):
        lr_copy(lr.at[0], slot, near).wait_recv()
        lr_copy(lr.at[slot], near + slot, near).start()
    lax.fori_loop(near + 1, CORES * near, forwarded, 0)

    for slot in range(near, CORES * near):
        lr_copy(lr.at[0], slot, near).wait_recv()

    nw = len(plane) + 1
    four = W // (nw * PARTS)
    depth = four * PARTS

    def t_copy(dz, chunk):
        cols = pl.ds(pl.multiple_of(chunk * W, W), W)
        return pltpu.make_async_remote_copy(
            src_ref=tsend.at[(zz + dz) % nz, :, cols],
            dst_ref=trecv.at[dz, :, cols],
            send_sem=t_send.at[dz, chunk],
            recv_sem=t_recv.at[dz, chunk],
            device_id=z_peer(dz),
            device_id_type=MESH,
        )

    same_q = shift_down(iota((W, W), 0) & (depth - 1), PARTS) - shift_down(lane, half)

    def measure_chunk(chunk, carry):
        totals = []
        for sub in range(nz):
            pair = chunk * nz + sub
            partner = dot(halfway[pair].reshape(nw * 2 * nb, 2 * W), sel_a[pair])
            t_re = jnp.zeros((nb, W), F32)
            t_im = jnp.zeros((nb, W), F32)
            for w in range(nw):
                s_re = sb[w, 0]
                s_im = sb[w, 1]
                p_re = partner[2 * nb * w : 2 * nb * w + nb]
                p_im = partner[2 * nb * w + nb : 2 * nb * (w + 1)]
                t_re = t_re + (s_re * p_re - s_im * p_im)
                t_im = t_im + (s_re * p_im + s_im * p_re)
            pairs = four // 2
            if sub % pairs == 0:
                start = pl.multiple_of((chunk * (nz // pairs) + sub // pairs) * depth, depth)
                stacked = lr[:, pl.ds(start, depth), :].reshape(W, W).astype(F32)
                turned_back = stacked.T
                mine = jnp.where(core == 0, turned_back[:nb], turned_back[nb : 2 * nb])
                odd = (iota((nb, W), 1) & 1) == 1
                trailing = jnp.concatenate(
                    [
                        jnp.where(odd, -mine, mine),
                        jnp.where(odd, pltpu.roll(mine, 1, 1), pltpu.roll(mine, W - 1, 1)),
                    ],
                    0,
                ).astype(BF)
                leading = jnp.where(lane < half, pltpu.roll(stacked, half, 1), stacked)
            masked = jnp.where(same_q == 2 * (sub % pairs), leading, 0.0)
            exchange = dot(trailing, masked.astype(BF))
            totals.append(jnp.concatenate([t_re, t_im], 0) - exchange)
        spot = shift_down(iota((2 * nb, W), 1), na) & (nz - 1)
        cols = pl.ds(pl.multiple_of(chunk * W, W), W)
        for z in range(nz):
            moved = shifted(totals[0], -na * z)
            for sub in range(1, nz):
                moved = jnp.where(spot == sub, shifted(totals[sub], na * (sub - z)), moved)
            tsend[z, :, cols] = moved.astype(BF)
        for dz in range(1, nz):
            t_copy(dz, chunk).start()
        return carry

    chunks = nq // nchunk
    lax.fori_loop(0, chunks, measure_chunk, 0)

    total = dot_nt(tsend[zz], sel_out[...])
    for dz in range(1, nz):
        for chunk in range(chunks):
            t_copy(dz, chunk).wait_recv()
        total = total + dot_nt(trecv[dz], sel_out[...])
    out_ref[...] = total

    for slot in plane:
        st_copy(0, slot, near).wait_send()
        lr_copy(lr.at[0], slot, near).wait_send()
    for dz in range(1, nz):
        for chunk in range(chunks):
            t_copy(dz, chunk).wait_send()


def kernel_body(
    vertex_matrix, vertex_site, vertex_time, vertex_spin, free_green, plus_table, cross_table
):
    nblk = lax.axis_size("blk")
    ngroup = lax.axis_size("group")
    nv = vertex_matrix.shape[-1]
    nq = plus_table.shape[0]
    nz = nblk // INNER
    na = W // nblk
    nb = W // ngroup
    nw = INNER * ngroup
    npair = nq // 2
    chunks = nq // (W // na)
    vmem = pl.BlockSpec(memory_space=pltpu.VMEM)
    dma = pltpu.SemaphoreType.DMA
    out = pl.pallas_call(
        functools.partial(kernel, nblk, ngroup),
        out_shape=jax.ShapeDtypeStruct((2 * nb, na * nq), F32),
        in_specs=[pl.BlockSpec(memory_space=pltpu.HBM)] * 7,
        out_specs=vmem,
        scratch_shapes=[
            pltpu.VMEM(vertex_site.shape, jnp.int32),
            pltpu.VMEM(vertex_time.shape, jnp.int32),
            pltpu.VMEM(vertex_spin.shape, jnp.int32),
            pltpu.VMEM(free_green.shape, F32),
            pltpu.VMEM(plus_table.shape, jnp.int32),
            pltpu.VMEM(cross_table.shape, jnp.int32),
            pltpu.VMEM((nv, nv), BF),
            pltpu.VMEM((4 * W, nv), BF),
            pltpu.VMEM((2, 2 * W, 2 * W), F32),
            pltpu.VMEM((nw, 2 * W, W), BF),
            pltpu.VMEM((nw, W, W), BF),
            pltpu.VMEM((nw // CORES, W, W), BF),
            pltpu.VMEM((nq * nb, W), BF),
            pltpu.VMEM((npair, 2 * W, W), BF),
            pltpu.VMEM((na * nq, nq * na), BF),
            pltpu.VMEM((nq, W), F32),
            pltpu.VMEM((nw, 2, nb, W), F32),
            pltpu.VMEM((npair, nw, 2, nb, 2 * W), BF),
            pltpu.VMEM((nz, 2 * nb, nq * na), BF),
            pltpu.VMEM((nz, 2 * nb, nq * na), BF),
            dma((6,)),
            dma((CHUNKS,)),
            dma((nw,)),
            dma((nw,)),
            dma((nw,)),
            dma((nw,)),
            dma((nz, chunks)),
            dma((nz, chunks)),
        ],
        compiler_params=pltpu.CompilerParams(
            collective_id=0, has_side_effects=True, vmem_limit_bytes=VMEM_BYTES - 1024 * 1024
        ),
    )(
        vertex_site,
        vertex_time,
        vertex_spin,
        free_green,
        plus_table,
        cross_table,
        vertex_matrix[0],
    )
    return out.reshape(2, nb, na, nq).transpose(0, 2, 3, 1)


def fits(mesh):
    nblk, ngroup = mesh.shape["blk"], mesh.shape["group"]
    if nblk % INNER or W % nblk or W % ngroup:
        return False
    nz, na, nb = nblk // INNER, W // nblk, W // ngroup
    return nz == 4 and ngroup % CORES == 0 and 2 * nz * na == W and 4 * nb == W and na % 16 == 0 and nb % 16 == 0


def solution(mesh):
    in_specs = (
        P(("blk", "group"), None, None),
        P(("blk", "group"), None),
        P(("blk", "group"), None),
        P(("blk", "group"), None),
        P(),
        P(),
        P("blk", None),
    )
    out_specs = P(None, "blk", None, "group")

    def chosen(*args):
        matrix, plus = args[0], args[5]
        small = fits(mesh) and PARTS * plus.shape[0] == W and matrix.shape[-1] % (128 * CHUNKS) == 0
        return (kernel_body if small else plain_body)(*args)

    return jax.shard_map(chosen, mesh=mesh, in_specs=in_specs, out_specs=out_specs, check_vma=False)
```

```python
import functools
import math

import jax
import jax.numpy as jnp
from jax import lax
from jax.experimental import pallas as pl
from jax.experimental.pallas import tpu as pltpu
from jax.sharding import PartitionSpec as P

LX = 4
NW = 8
W = 128
NV = 1152
NT = 1024


def phases(site_ids, time_ids):
    points = jnp.arange(W, dtype=jnp.int32)
    moment = points // NW
    freq_index = points % NW
    kx_part = moment % LX
    ky_part = moment // LX
    rx_part = site_ids % LX
    ry_part = site_ids // LX
    winding = (2 * freq_index + 1)[:, None] * time_ids[None, :] + 2 * NT // LX * (
        kx_part[:, None] * rx_part[None, :] + ky_part[:, None] * ry_part[None, :]
    )
    winding = winding % (2 * NT)
    return winding.astype(jnp.float32) * (math.pi / NT)


def green_pair(matrix, site_ids, time_ids, spin_ids, free_green):
    angles = phases(site_ids, time_ids)
    cosine = jnp.cos(angles)
    sine_part = jnp.sin(angles)
    spin_up = (spin_ids == 0).astype(jnp.float32)[None, :]
    spin_down = (spin_ids == 1).astype(jnp.float32)[None, :]
    fourier_rows = jnp.concatenate(
        [cosine * spin_up, sine_part * spin_up, cosine * spin_down, sine_part * spin_down], 0
    ).astype(jnp.bfloat16)
    projected = jnp.dot(fourier_rows, matrix, preferred_element_type=jnp.float32).astype(
        jnp.bfloat16
    )
    norm_factor = 1.0 / math.sqrt(NV)
    real_free = free_green[0]
    imag_free = free_green[1]
    greens = []
    for spin_index in range(2):
        offset = 2 * W * spin_index
        cosine_rows = fourier_rows[offset : offset + W]
        sine_rows = fourier_rows[offset + W : offset + 2 * W]
        proj_real = projected[offset : offset + W]
        proj_imag = projected[offset + W : offset + 2 * W]
        left_block = jnp.concatenate(
            [
                jnp.concatenate([proj_real, proj_imag], 1),
                jnp.concatenate([proj_imag, -proj_real], 1),
            ],
            0,
        )
        right_block = jnp.concatenate([cosine_rows, sine_rows], 1)
        kernel = lax.dot_general(
            left_block, right_block, (((1,), (1,)), ((), ())), preferred_element_type=jnp.float32
        )
        kernel_real = kernel[:W]
        kernel_imag = kernel[W:]
        half_real = real_free[:, None] * kernel_real - imag_free[:, None] * kernel_imag
        half_imag = real_free[:, None] * kernel_imag + imag_free[:, None] * kernel_real
        green_real = (
            -(half_real * real_free[None, :] - half_imag * imag_free[None, :]) * norm_factor
        )
        green_imag = (
            -(half_real * imag_free[None, :] + half_imag * real_free[None, :]) * norm_factor
        )
        greens.append(jnp.stack([green_real, green_imag], 0))
    green_sum = (greens[0] + greens[1]).astype(jnp.bfloat16)
    return (green_sum, greens[0].astype(jnp.bfloat16), greens[1].astype(jnp.bfloat16))


def direct_terms(sums_piece, perm_row):
    column_ids = jnp.arange(sums_piece.shape[-1], dtype=jnp.int32)
    selector = (perm_row[:, None] == column_ids[None, :]).astype(jnp.bfloat16)
    halfway = jnp.einsum(
        "aj,kcbj->kcab", selector, sums_piece, preferred_element_type=jnp.float32
    ).astype(jnp.bfloat16)
    partner = jnp.einsum("kcaj,bj->kcab", halfway, selector, preferred_element_type=jnp.float32)
    local_copy = sums_piece.astype(jnp.float32)
    real_part = jnp.sum(local_copy[:, 0] * partner[:, 0] - local_copy[:, 1] * partner[:, 1], axis=0)
    imag_part = jnp.sum(local_copy[:, 0] * partner[:, 1] + local_copy[:, 1] * partner[:, 0], axis=0)
    return jnp.stack([real_part, imag_part], 0)


def copy_exchange(up_piece, down_piece, perm_row):
    column_ids = jnp.arange(up_piece.shape[-1], dtype=jnp.int32)
    spin_pieces = jnp.concatenate([up_piece, down_piece], 0)
    lead_values = spin_pieces[:, :, column_ids, perm_row]
    trail_values = spin_pieces[:, :, perm_row, column_ids]
    real_part = jnp.einsum(
        "ka,kb->ab", lead_values[:, 0], trail_values[:, 0], preferred_element_type=jnp.float32
    ) - jnp.einsum(
        "ka,kb->ab", lead_values[:, 1], trail_values[:, 1], preferred_element_type=jnp.float32
    )
    imag_part = jnp.einsum(
        "ka,kb->ab", lead_values[:, 0], trail_values[:, 1], preferred_element_type=jnp.float32
    ) + jnp.einsum(
        "ka,kb->ab", lead_values[:, 1], trail_values[:, 0], preferred_element_type=jnp.float32
    )
    return jnp.stack([real_part, imag_part], 0)


def plain_body(vertex_matrix, vertex_site, vertex_time, vertex_spin, free_green, plus_table, cross_table):
    green_sum, green_up, green_down = green_pair(
        vertex_matrix[0], vertex_site[0], vertex_time[0], vertex_spin[0], free_green
    )
    slices = plus_table.shape[0] // lax.axis_size("blk")
    owned_perms = lax.dynamic_slice_in_dim(plus_table, lax.axis_index("blk") * slices, slices, 0)
    sums_piece = lax.all_gather(green_sum[None], "blk", axis=0, tiled=True)
    up_piece = lax.all_gather(green_up[None], "blk", axis=0, tiled=True)
    down_piece = lax.all_gather(green_down[None], "blk", axis=0, tiled=True)

    def one_slice(perm_row):
        return direct_terms(sums_piece, perm_row) - copy_exchange(up_piece, down_piece, perm_row)

    transfer = jnp.swapaxes(lax.map(one_slice, owned_perms), 0, 1)
    shares = lax.psum_scatter(transfer, "group", scatter_dimension=3, tiled=True)
    regrouped = lax.all_to_all(shares, "blk", split_axis=2, concat_axis=1, tiled=True)
    row_ids = jnp.arange(regrouped.shape[2], dtype=jnp.int32)
    return regrouped[:, cross_table, row_ids[:, None], :]


BF = jnp.bfloat16
F32 = jnp.float32
MESH = pl.DeviceIdType.MESH
INNER = 2
CORES = 2
VMEM_BYTES = 64 * 1024 * 1024
PARTS = 4
PIECE = 256


def iota(shape, dim):
    return lax.broadcasted_iota(jnp.int32, shape, dim)


def shift_down(value, divisor):
    return value >> (divisor.bit_length() - 1)


def one_hot(condition):
    return jnp.where(condition, 1.0, 0.0).astype(BF)


def dot(left, right):
    return jnp.dot(left, right, preferred_element_type=F32)


def dot_nt(left, right):
    return lax.dot_general(left, right, (((1,), (1,)), ((), ())), preferred_element_type=F32)


def kernel(
    nblk,
    ngroup,
    site_hbm,
    time_hbm,
    spin_hbm,
    free_hbm,
    plus_hbm,
    cross_hbm,
    matrix_hbm,
    out_ref,
    site_ref,
    time_ref,
    spin_ref,
    free_ref,
    plus_ref,
    cross_ref,
    matrix,
    rows,
    kern,
    st,
    lr,
    lr_send,
    sel_b,
    sel_a,
    sel_out,
    prow,
    sb,
    halfway,
    tsend,
    trecv,
    small_sem,
    matrix_sem,
    st_send,
    st_recv,
    lr_send_sem,
    lr_recv,
    t_send,
    t_recv,
):
    small = [
        pltpu.make_async_copy(source, target, small_sem.at[place])
        for place, (source, target) in enumerate(
            [
                (site_hbm, site_ref),
                (time_hbm, time_ref),
                (spin_hbm, spin_ref),
                (free_hbm, free_ref),
                (plus_hbm, plus_ref),
                (cross_hbm, cross_ref),
            ]
        )
    ]
    for copy in small:
        copy.start()

    nz = nblk // INNER
    na = W // nblk
    nb = W // ngroup
    nq = plus_ref.shape[0]
    half = na * nz
    npair = nq // 2
    nchunk = W // na
    nv = site_ref.shape[1]
    pieces = nv // PIECE
    tail = nv % PIECE
    blk = lax.axis_index("blk")
    grp = lax.axis_index("group")
    zz = blk // INNER
    yy = blk % INNER
    nx = ngroup // CORES
    xx = grp // CORES
    core = grp % CORES
    near = nx * INNER
    plane = list(range(1, CORES * near))

    def plane_peer(slot):
        dc, dy, dx = slot // near, slot // nx % INNER, slot % nx
        return (
            zz * INNER + (yy + dy) % INNER,
            (xx + dx) % nx * CORES + (core + dc) % CORES,
        )

    def z_peer(dz):
        return (((zz + dz) % nz) * INNER + yy, grp)

    def matrix_copy(index, width):
        cols = pl.ds(index * PIECE, width)
        return pltpu.make_async_copy(
            matrix_hbm.at[:, cols], matrix.at[:, cols], matrix_sem.at[index]
        )


    for index in range(pieces):
        matrix_copy(index, PIECE).start()
    if tail:
        matrix_copy(pieces, tail).start()

    barrier = pltpu.get_barrier_semaphore()
    for slot in plane:
        pl.semaphore_signal(barrier, inc=1, device_id=plane_peer(slot), device_id_type=MESH)
    for dz in range(1, nz):
        pl.semaphore_signal(barrier, inc=1, device_id=z_peer(dz), device_id_type=MESH)

    for copy in small:
        copy.wait()

    quarter = NT // 2
    site = jnp.broadcast_to(site_ref[...], (2 * NW, nv))
    rx = site & (LX - 1)
    ry = shift_down(site, LX)
    ids = iota((2 * NW, nv), 0)
    freq = ids & (NW - 1)
    upper = shift_down(ids, NW)
    winding = (2 * freq + 1) * time_ref[...]
    turns = shift_down(winding + quarter // 2, quarter)
    rest = (winding - turns * quarter).astype(F32) * (math.pi / NT)
    square = rest * rest
    cosine = 1.0 + square * (
        -1 / 2
        + square
        * (1 / 24 + square * (-1 / 720 + square * (1 / 40320 + square * (-1 / 3628800))))
    )
    sine = rest + rest * square * (
        -1 / 6 + square * (1 / 120 + square * (-1 / 5040 + square * (1 / 362880)))
    )
    cosine = cosine.astype(BF)
    sine = sine.astype(BF)

    def unit(amount):
        amount = amount & 3
        real = jnp.where(amount == 0, 1.0, jnp.where(amount == 2, -1.0, 0.0))
        imag = jnp.where(amount == 1, 1.0, jnp.where(amount == 3, -1.0, 0.0))
        return real.astype(BF), imag.astype(BF)

    def turn(value, by):
        return (value[0] * by[0] - value[1] * by[1], value[1] * by[0] + value[0] * by[1])

    spin = jnp.broadcast_to(spin_ref[...], (2 * NW, nv))
    up = one_hot(spin == 0)
    down = one_hot(spin == 1)
    across = [unit((kx + upper) * rx) for kx in range(0, LX, 2)]
    for ky in range(W // NW // LX):
        base = turn((cosine, sine), unit(turns + ky * ry))
        for place, by in enumerate(across):
            c_both, s_both = turn(base, by)
            at = (ky * LX + 2 * place) * NW
            rows[pl.ds(at, 2 * NW), :] = c_both * up
            rows[pl.ds(W + at, 2 * NW), :] = s_both * up
            rows[pl.ds(2 * W + at, 2 * NW), :] = c_both * down
            rows[pl.ds(3 * W + at, 2 * NW), :] = s_both * down

    kern[...] = jnp.zeros_like(kern)

    def project(index, width):
        matrix_copy(index, width).wait()
        start = index * PIECE
        cols = pl.ds(start if isinstance(start, int) else pl.multiple_of(start, PIECE), width)
        projected = dot(rows[...], matrix[:, cols]).astype(BF)
        for s in range(2):
            kern[s] += dot_nt(
                projected[2 * W * s : 2 * W * (s + 1)], rows[pl.ds(2 * W * s, 2 * W), cols]
            )

    def project_piece(index, carry):
        project(index, PIECE)
        return carry

    lax.fori_loop(0, pieces, project_piece, 0)
    if tail:
        project(pieces, tail)

    ga_re = jnp.broadcast_to(free_ref[0:1, :], (W, W))
    ga_im = jnp.broadcast_to(free_ref[1:2, :], (W, W))
    gb_re, gb_im = ga_re, ga_im
    ga_re = ga_re.T
    ga_im = ga_im.T
    norm_factor = 1.0 / math.sqrt(NV)
    greens = []
    for s in range(2):
        k_re = kern[s, :W, :W] + kern[s, W:, W:]
        k_im = kern[s, W:, :W] - kern[s, :W, W:]
        h_re = ga_re * k_re - ga_im * k_im
        h_im = ga_re * k_im + ga_im * k_re
        greens.append(-(h_re * gb_re - h_im * gb_im) * norm_factor)
        greens.append(-(h_re * gb_im + h_im * gb_re) * norm_factor)
    turned = [g.T for g in greens]
    st[0, :W, :] = (turned[0] + turned[2]).astype(BF)
    st[0, W:, :] = (turned[1] + turned[3]).astype(BF)

    pl.semaphore_wait(barrier, len(plane) + nz - 1)

    def st_copy(source, slot, steps):
        return pltpu.make_async_remote_copy(
            src_ref=st.at[source],
            dst_ref=st.at[slot],
            send_sem=st_send.at[slot],
            recv_sem=st_recv.at[slot],
            device_id=plane_peer(steps),
            device_id_type=MESH,
        )

    def lr_copy(source, slot, steps):
        return pltpu.make_async_remote_copy(
            src_ref=source,
            dst_ref=lr.at[slot],
            send_sem=lr_send_sem.at[slot],
            recv_sem=lr_recv.at[slot],
            device_id=plane_peer(steps),
            device_id_type=MESH,
        )

    def lr_for(slot):
        dy, dx = slot // nx % INNER, slot % nx
        return lr_send.at[(yy + dy) % INNER * nx + (xx + dx) % nx]

    for slot in range(near - 1, 0, -1):
        st_copy(0, slot, slot).start()
    st_copy(0, near, near).start()

    greens = [g.astype(BF).astype(F32) for g in greens]
    turned = [g.astype(BF).astype(F32) for g in turned]
    plus = plus_ref[...].astype(F32)
    plus_turned = jnp.concatenate([plus, jnp.zeros((W - nq, W), F32)], 0).T
    expand = one_hot(shift_down(iota((W, W), 1), PARTS) == iota((W, W), 0))
    index = dot(plus_turned.astype(BF), expand).astype(jnp.int32)
    lane = iota((W, W), 1)
    part = lane & (PARTS - 1)

    def choose(values):
        picked = values[0]
        for g in range(1, PARTS):
            picked = jnp.where(part == g, values[g], picked)
        return picked

    lead = choose([jnp.take_along_axis(g, index, axis=1) for g in greens])
    trail = [jnp.take_along_axis(g, index, axis=1) for g in turned]
    trail = choose(trail).T
    order = [INNER * z + y for y in range(INNER) for z in range(nz)]
    lead = jnp.concatenate([lead[na * i : na * (i + 1)] for i in order], 0).T

    def shifted(value, by):
        by = by % W
        return value if by == 0 else pltpu.roll(value, by, 1)

    for x in range(nx):
        left = shifted(trail, -half * x)
        for y in range(INNER):
            joined = jnp.where(lane < half, left, shifted(lead, half - half * y))
            lr_send[y * nx + x] = joined.astype(BF)
    for slot in range(near - 1, 0, -1):
        lr_copy(lr_for(slot), slot, slot).start()
    lr_copy(lr_for(near), near, near).start()
    lr[0] = lr_send[yy * nx + xx]

    plus_bf = plus.astype(BF)
    my_b = one_hot(iota((nb, W), 1) == iota((nb, W), 0) + nb * grp)
    plus_b = dot_nt(my_b, plus_bf).astype(jnp.int32)
    for q in range(nq):
        column = jnp.broadcast_to(plus_b[:, q : q + 1], (nb, W))
        sel_b[pl.ds(q * nb, nb), :] = one_hot(column == iota((nb, W), 1))
    place = shift_down(lane & (half - 1), na) * (na * INNER) + na * yy + (lane & (na - 1))
    my_a = one_hot(iota((W, W), 0) == place)
    prow[...] = dot(plus_bf, my_a)

    def pair_selector(pair, carry):
        first = prow[pl.ds(2 * pair, 1), :]
        second = prow[pl.ds(2 * pair + 1, 1), :]
        low = lane < half
        hit = iota((W, W), 0) == jnp.where(
            low, jnp.broadcast_to(first, (W, W)), jnp.broadcast_to(second, (W, W))
        ).astype(jnp.int32)
        sel_a[pair, :W, :] = one_hot(hit & low)
        sel_a[pair, W:, :] = one_hot(hit & (lane >= half))
        return carry

    lax.fori_loop(0, npair, pair_selector, 0)

    same = one_hot(iota((nq, nq), 0) == iota((nq, nq), 1))
    crossing = dot_nt(same, cross_ref[...].astype(F32).astype(BF)).astype(jnp.int32)
    crossing = (
        shift_down(crossing, nchunk) * W
        + (crossing & 1) * half
        + (shift_down(crossing, 2) & (nz - 1)) * na
    )
    for r in range(na):
        column = jnp.broadcast_to(crossing[:, r : r + 1] + r, (nq, nq * na))
        sel_out[pl.ds(r * nq, nq), :] = one_hot(column == iota((nq, nq * na), 1))

    def take_rows(slot):
        for c in range(2):
            mine = st[slot, pl.ds(pl.multiple_of(c * W + nb * grp, nb), nb), :]
            sb[slot, c] = dot(mine, my_a)

    def select(slot, pair, count):
        picks = sel_b[pl.ds(pl.multiple_of(pair * 2 * nb, 2 * nb), count * nb), :]
        picked = dot_nt(picks, st[slot]).astype(BF)
        for q in range(count):
            for c in range(2):
                halfway[pair + q // 2, slot, c, :, pl.ds((q % 2) * W, W)] = picked[
                    q * nb : (q + 1) * nb, c * W : (c + 1) * W
                ]

    def first_selection(slot):
        take_rows(slot)
        for chunk in range(nq // nchunk):
            select(slot, chunk * nchunk // 2, nchunk)

    def own_chip(step, carry):
        @pl.when(step > 0)
        def _():
            st_copy(0, near, near).wait_recv()

        first_selection(step * near)
        return carry

    def same_core(step, carry):
        st_copy(0, step, near).wait_recv()
        st_copy(step, near + step, near).start()
        first_selection(step)
        return carry

    def forwarded(step, carry):
        st_copy(0, step, near).wait_recv()
        take_rows(step)
        return carry

    lax.fori_loop(0, CORES, own_chip, 0)
    lax.fori_loop(1, near, same_core, 0)
    for slot in range(1, near):
        lr_copy(lr.at[0], slot, near).wait_recv()
        lr_copy(lr.at[slot], near + slot, near).start()
    lax.fori_loop(near + 1, CORES * near, forwarded, 0)

    for slot in range(near, CORES * near):
        lr_copy(lr.at[0], slot, near).wait_recv()

    nw = len(plane) + 1
    four = W // (nw * PARTS)
    depth = four * PARTS

    def t_copy(dz, chunk):
        cols = pl.ds(pl.multiple_of(chunk * W, W), W)
        return pltpu.make_async_remote_copy(
            src_ref=tsend.at[(zz + dz) % nz, :, cols],
            dst_ref=trecv.at[dz, :, cols],
            send_sem=t_send.at[dz, chunk],
            recv_sem=t_recv.at[dz, chunk],
            device_id=z_peer(dz),
            device_id_type=MESH,
        )

    same_q = shift_down(iota((W, W), 0) & (depth - 1), PARTS) - shift_down(lane, half)

    def measure_chunk(chunk, carry):
        totals = []
        for slot in range(near + 1, CORES * near):
            select(slot, chunk * nchunk // 2, nchunk)
        for sub in range(nz):
            pair = chunk * nz + sub
            partner = dot(halfway[pair].reshape(nw * 2 * nb, 2 * W), sel_a[pair])
            t_re = jnp.zeros((nb, W), F32)
            t_im = jnp.zeros((nb, W), F32)
            for w in range(nw):
                s_re = sb[w, 0]
                s_im = sb[w, 1]
                p_re = partner[2 * nb * w : 2 * nb * w + nb]
                p_im = partner[2 * nb * w + nb : 2 * nb * (w + 1)]
                t_re = t_re + (s_re * p_re - s_im * p_im)
                t_im = t_im + (s_re * p_im + s_im * p_re)
            pairs = four // 2
            if sub % pairs == 0:
                start = pl.multiple_of((chunk * (nz // pairs) + sub // pairs) * depth, depth)
                stacked = lr[:, pl.ds(start, depth), :].reshape(W, W).astype(F32)
                turned_back = stacked.T
                mine = jnp.where(core == 0, turned_back[:nb], turned_back[nb : 2 * nb])
                odd = (iota((nb, W), 1) & 1) == 1
                trailing = jnp.concatenate(
                    [
                        jnp.where(odd, -mine, mine),
                        jnp.where(odd, pltpu.roll(mine, 1, 1), pltpu.roll(mine, W - 1, 1)),
                    ],
                    0,
                ).astype(BF)
                leading = jnp.where(lane < half, pltpu.roll(stacked, half, 1), stacked)
                masked = jnp.concatenate(
                    [jnp.where(same_q == 2 * i, leading, 0.0) for i in range(pairs)], 1
                )
                exchange = dot(trailing, masked.astype(BF))
            at = sub % pairs * W
            totals.append(jnp.concatenate([t_re, t_im], 0) - exchange[:, at : at + W])
        spot = shift_down(iota((2 * nb, W), 1), na) & (nz - 1)
        cols = pl.ds(pl.multiple_of(chunk * W, W), W)
        for z in range(nz):
            moved = shifted(totals[0], -na * z)
            for sub in range(1, nz):
                moved = jnp.where(spot == sub, shifted(totals[sub], na * (sub - z)), moved)
            tsend[z, :, cols] = moved.astype(BF)
        for dz in range(1, nz):
            t_copy(dz, chunk).start()
        return carry

    chunks = nq // nchunk
    lax.fori_loop(0, chunks, measure_chunk, 0)

    total = dot_nt(tsend[zz], sel_out[...])
    for dz in range(1, nz):
        for chunk in range(chunks):
            t_copy(dz, chunk).wait_recv()
        total = total + dot_nt(trecv[dz], sel_out[...])
    out_ref[...] = total

    for slot in plane:
        st_copy(0, slot, near).wait_send()
        lr_copy(lr.at[0], slot, near).wait_send()
    for dz in range(1, nz):
        for chunk in range(chunks):
            t_copy(dz, chunk).wait_send()


def order_result(dense_ref, out_ref):
    parts, na, nq, nb = out_ref.shape
    for c in range(parts):
        out_ref[c] = dense_ref[c * nb : (c + 1) * nb, :].T.reshape(na, nq, nb)


def kernel_body(
    vertex_matrix, vertex_site, vertex_time, vertex_spin, free_green, plus_table, cross_table
):
    nblk = lax.axis_size("blk")
    ngroup = lax.axis_size("group")
    nv = vertex_matrix.shape[-1]
    nq = plus_table.shape[0]
    nz = nblk // INNER
    na = W // nblk
    nb = W // ngroup
    nw = INNER * ngroup
    npair = nq // 2
    chunks = nq // (W // na)
    vmem = pl.BlockSpec(memory_space=pltpu.VMEM)
    dma = pltpu.SemaphoreType.DMA
    out = pl.pallas_call(
        functools.partial(kernel, nblk, ngroup),
        out_shape=jax.ShapeDtypeStruct((2 * nb, na * nq), F32),
        in_specs=[pl.BlockSpec(memory_space=pltpu.HBM)] * 7,
        out_specs=vmem,
        scratch_shapes=[
            pltpu.VMEM(vertex_site.shape, jnp.int32),
            pltpu.VMEM(vertex_time.shape, jnp.int32),
            pltpu.VMEM(vertex_spin.shape, jnp.int32),
            pltpu.VMEM(free_green.shape, F32),
            pltpu.VMEM(plus_table.shape, jnp.int32),
            pltpu.VMEM(cross_table.shape, jnp.int32),
            pltpu.VMEM((nv, nv), BF),
            pltpu.VMEM((4 * W, nv), BF),
            pltpu.VMEM((2, 2 * W, 2 * W), F32),
            pltpu.VMEM((nw, 2 * W, W), BF),
            pltpu.VMEM((nw, W, W), BF),
            pltpu.VMEM((nw // CORES, W, W), BF),
            pltpu.VMEM((nq * nb, W), BF),
            pltpu.VMEM((npair, 2 * W, W), BF),
            pltpu.VMEM((na * nq, nq * na), BF),
            pltpu.VMEM((nq, W), F32),
            pltpu.VMEM((nw, 2, nb, W), F32),
            pltpu.VMEM((npair, nw, 2, nb, 2 * W), BF),
            pltpu.VMEM((nz, 2 * nb, nq * na), BF),
            pltpu.VMEM((nz, 2 * nb, nq * na), BF),
            dma((6,)),
            dma((nv // PIECE + 1,)),
            dma((nw,)),
            dma((nw,)),
            dma((nw,)),
            dma((nw,)),
            dma((nz, chunks)),
            dma((nz, chunks)),
        ],
        compiler_params=pltpu.CompilerParams(
            collective_id=0, has_side_effects=True, vmem_limit_bytes=VMEM_BYTES - 1024 * 1024
        ),
    )(
        vertex_site,
        vertex_time,
        vertex_spin,
        free_green,
        plus_table,
        cross_table,
        vertex_matrix[0],
    )
    return pl.pallas_call(
        order_result,
        out_shape=jax.ShapeDtypeStruct((2, na, nq, nb), F32),
        in_specs=[vmem],
        out_specs=vmem,
        compiler_params=pltpu.CompilerParams(vmem_limit_bytes=VMEM_BYTES - 1024 * 1024),
    )(out)


def fits(mesh):
    nblk, ngroup = mesh.shape["blk"], mesh.shape["group"]
    if nblk % INNER or W % nblk or W % ngroup:
        return False
    nz, na, nb = nblk // INNER, W // nblk, W // ngroup
    return nz == 4 and ngroup % CORES == 0 and 2 * nz * na == W and 4 * nb == W and na % 16 == 0 and nb % 16 == 0


def solution(mesh):
    in_specs = (
        P(("blk", "group"), None, None),
        P(("blk", "group"), None),
        P(("blk", "group"), None),
        P(("blk", "group"), None),
        P(),
        P(),
        P("blk", None),
    )
    out_specs = P(None, "blk", None, "group")

    def chosen(*args):
        matrix, plus = args[0], args[5]
        small = fits(mesh) and PARTS * plus.shape[0] == W and matrix.shape[-1] % 128 == 0
        return (kernel_body if small else plain_body)(*args)

    return jax.shard_map(chosen, mesh=mesh, in_specs=in_specs, out_specs=out_specs, check_vma=False)
```

```python
import functools
import math

import jax
import jax.numpy as jnp
from jax import lax
from jax.experimental import pallas as pl
from jax.experimental.pallas import tpu as pltpu
from jax.sharding import PartitionSpec as P

LX = 4
NW = 8
W = 128
NV = 1152
NT = 1024


def phases(site_ids, time_ids):
    points = jnp.arange(W, dtype=jnp.int32)
    moment = points // NW
    freq_index = points % NW
    kx_part = moment % LX
    ky_part = moment // LX
    rx_part = site_ids % LX
    ry_part = site_ids // LX
    winding = (2 * freq_index + 1)[:, None] * time_ids[None, :] + 2 * NT // LX * (
        kx_part[:, None] * rx_part[None, :] + ky_part[:, None] * ry_part[None, :]
    )
    winding = winding % (2 * NT)
    return winding.astype(jnp.float32) * (math.pi / NT)


def green_pair(matrix, site_ids, time_ids, spin_ids, free_green):
    angles = phases(site_ids, time_ids)
    cosine = jnp.cos(angles)
    sine_part = jnp.sin(angles)
    spin_up = (spin_ids == 0).astype(jnp.float32)[None, :]
    spin_down = (spin_ids == 1).astype(jnp.float32)[None, :]
    fourier_rows = jnp.concatenate(
        [cosine * spin_up, sine_part * spin_up, cosine * spin_down, sine_part * spin_down], 0
    ).astype(jnp.bfloat16)
    projected = jnp.dot(fourier_rows, matrix, preferred_element_type=jnp.float32).astype(
        jnp.bfloat16
    )
    norm_factor = 1.0 / math.sqrt(NV)
    real_free = free_green[0]
    imag_free = free_green[1]
    greens = []
    for spin_index in range(2):
        offset = 2 * W * spin_index
        cosine_rows = fourier_rows[offset : offset + W]
        sine_rows = fourier_rows[offset + W : offset + 2 * W]
        proj_real = projected[offset : offset + W]
        proj_imag = projected[offset + W : offset + 2 * W]
        left_block = jnp.concatenate(
            [
                jnp.concatenate([proj_real, proj_imag], 1),
                jnp.concatenate([proj_imag, -proj_real], 1),
            ],
            0,
        )
        right_block = jnp.concatenate([cosine_rows, sine_rows], 1)
        kernel = lax.dot_general(
            left_block, right_block, (((1,), (1,)), ((), ())), preferred_element_type=jnp.float32
        )
        kernel_real = kernel[:W]
        kernel_imag = kernel[W:]
        half_real = real_free[:, None] * kernel_real - imag_free[:, None] * kernel_imag
        half_imag = real_free[:, None] * kernel_imag + imag_free[:, None] * kernel_real
        green_real = (
            -(half_real * real_free[None, :] - half_imag * imag_free[None, :]) * norm_factor
        )
        green_imag = (
            -(half_real * imag_free[None, :] + half_imag * real_free[None, :]) * norm_factor
        )
        greens.append(jnp.stack([green_real, green_imag], 0))
    green_sum = (greens[0] + greens[1]).astype(jnp.bfloat16)
    return (green_sum, greens[0].astype(jnp.bfloat16), greens[1].astype(jnp.bfloat16))


def direct_terms(sums_piece, perm_row):
    column_ids = jnp.arange(sums_piece.shape[-1], dtype=jnp.int32)
    selector = (perm_row[:, None] == column_ids[None, :]).astype(jnp.bfloat16)
    halfway = jnp.einsum(
        "aj,kcbj->kcab", selector, sums_piece, preferred_element_type=jnp.float32
    ).astype(jnp.bfloat16)
    partner = jnp.einsum("kcaj,bj->kcab", halfway, selector, preferred_element_type=jnp.float32)
    local_copy = sums_piece.astype(jnp.float32)
    real_part = jnp.sum(local_copy[:, 0] * partner[:, 0] - local_copy[:, 1] * partner[:, 1], axis=0)
    imag_part = jnp.sum(local_copy[:, 0] * partner[:, 1] + local_copy[:, 1] * partner[:, 0], axis=0)
    return jnp.stack([real_part, imag_part], 0)


def copy_exchange(up_piece, down_piece, perm_row):
    column_ids = jnp.arange(up_piece.shape[-1], dtype=jnp.int32)
    spin_pieces = jnp.concatenate([up_piece, down_piece], 0)
    lead_values = spin_pieces[:, :, column_ids, perm_row]
    trail_values = spin_pieces[:, :, perm_row, column_ids]
    real_part = jnp.einsum(
        "ka,kb->ab", lead_values[:, 0], trail_values[:, 0], preferred_element_type=jnp.float32
    ) - jnp.einsum(
        "ka,kb->ab", lead_values[:, 1], trail_values[:, 1], preferred_element_type=jnp.float32
    )
    imag_part = jnp.einsum(
        "ka,kb->ab", lead_values[:, 0], trail_values[:, 1], preferred_element_type=jnp.float32
    ) + jnp.einsum(
        "ka,kb->ab", lead_values[:, 1], trail_values[:, 0], preferred_element_type=jnp.float32
    )
    return jnp.stack([real_part, imag_part], 0)


def plain_body(vertex_matrix, vertex_site, vertex_time, vertex_spin, free_green, plus_table, cross_table):
    green_sum, green_up, green_down = green_pair(
        vertex_matrix[0], vertex_site[0], vertex_time[0], vertex_spin[0], free_green
    )
    slices = plus_table.shape[0] // lax.axis_size("blk")
    owned_perms = lax.dynamic_slice_in_dim(plus_table, lax.axis_index("blk") * slices, slices, 0)
    sums_piece = lax.all_gather(green_sum[None], "blk", axis=0, tiled=True)
    up_piece = lax.all_gather(green_up[None], "blk", axis=0, tiled=True)
    down_piece = lax.all_gather(green_down[None], "blk", axis=0, tiled=True)

    def one_slice(perm_row):
        return direct_terms(sums_piece, perm_row) - copy_exchange(up_piece, down_piece, perm_row)

    transfer = jnp.swapaxes(lax.map(one_slice, owned_perms), 0, 1)
    shares = lax.psum_scatter(transfer, "group", scatter_dimension=3, tiled=True)
    regrouped = lax.all_to_all(shares, "blk", split_axis=2, concat_axis=1, tiled=True)
    row_ids = jnp.arange(regrouped.shape[2], dtype=jnp.int32)
    return regrouped[:, cross_table, row_ids[:, None], :]


BF = jnp.bfloat16
F32 = jnp.float32
MESH = pl.DeviceIdType.MESH
INNER = 2
CORES = 2
VMEM_BYTES = 64 * 1024 * 1024
PARTS = 4
PIECE = 256


def iota(shape, dim):
    return lax.broadcasted_iota(jnp.int32, shape, dim)


def shift_down(value, divisor):
    return value >> (divisor.bit_length() - 1)


def one_hot(condition):
    return jnp.where(condition, 1.0, 0.0).astype(BF)


def dot(left, right):
    return jnp.dot(left, right, preferred_element_type=F32)


def dot_nt(left, right):
    return lax.dot_general(left, right, (((1,), (1,)), ((), ())), preferred_element_type=F32)


def kernel(
    nblk,
    ngroup,
    site_hbm,
    time_hbm,
    spin_hbm,
    free_hbm,
    plus_hbm,
    cross_hbm,
    matrix_hbm,
    out_ref,
    site_ref,
    time_ref,
    spin_ref,
    free_ref,
    plus_ref,
    cross_ref,
    matrix,
    rows,
    kern,
    st,
    lr,
    lr_send,
    sel_b,
    sel_a,
    sel_out,
    prow,
    sb,
    halfway,
    tsend,
    trecv,
    small_sem,
    matrix_sem,
    st_send,
    st_recv,
    lr_send_sem,
    lr_recv,
    t_send,
    t_recv,
):
    small = [
        pltpu.make_async_copy(source, target, small_sem.at[place])
        for place, (source, target) in enumerate(
            [
                (site_hbm, site_ref),
                (time_hbm, time_ref),
                (spin_hbm, spin_ref),
                (free_hbm, free_ref),
                (plus_hbm, plus_ref),
                (cross_hbm, cross_ref),
            ]
        )
    ]
    for copy in small:
        copy.start()

    nz = nblk // INNER
    na = W // nblk
    nb = W // ngroup
    nq = plus_ref.shape[0]
    half = na * nz
    npair = nq // 2
    nchunk = W // na
    nv = site_ref.shape[1]
    pieces = nv // PIECE
    tail = nv % PIECE
    blk = lax.axis_index("blk")
    grp = lax.axis_index("group")
    zz = blk // INNER
    yy = blk % INNER
    nx = ngroup // CORES
    xx = grp // CORES
    core = grp % CORES
    near = nx * INNER
    plane = list(range(1, CORES * near))

    def plane_peer(slot):
        dc, dy, dx = slot // near, slot // nx % INNER, slot % nx
        return (
            zz * INNER + (yy + dy) % INNER,
            (xx + dx) % nx * CORES + (core + dc) % CORES,
        )

    def z_peer(dz):
        return (((zz + dz) % nz) * INNER + yy, grp)

    def matrix_copy(index, width):
        cols = pl.ds(index * PIECE, width)
        return pltpu.make_async_copy(
            matrix_hbm.at[:, cols], matrix.at[:, cols], matrix_sem.at[index]
        )


    for index in range(pieces):
        matrix_copy(index, PIECE).start()
    if tail:
        matrix_copy(pieces, tail).start()

    barrier = pltpu.get_barrier_semaphore()
    for slot in plane:
        pl.semaphore_signal(barrier, inc=1, device_id=plane_peer(slot), device_id_type=MESH)
    for dz in range(1, nz):
        pl.semaphore_signal(barrier, inc=1, device_id=z_peer(dz), device_id_type=MESH)

    for copy in small:
        copy.wait()

    quarter = NT // 2
    site = jnp.broadcast_to(site_ref[...], (2 * NW, nv))
    rx = site & (LX - 1)
    ry = shift_down(site, LX)
    ids = iota((2 * NW, nv), 0)
    freq = ids & (NW - 1)
    upper = shift_down(ids, NW)
    winding = (2 * freq + 1) * time_ref[...]
    turns = shift_down(winding + quarter // 2, quarter)
    rest = (winding - turns * quarter).astype(F32) * (math.pi / NT)
    square = rest * rest
    cosine = 1.0 + square * (
        -1 / 2
        + square
        * (1 / 24 + square * (-1 / 720 + square * (1 / 40320 + square * (-1 / 3628800))))
    )
    sine = rest + rest * square * (
        -1 / 6 + square * (1 / 120 + square * (-1 / 5040 + square * (1 / 362880)))
    )
    cosine = cosine.astype(BF)
    sine = sine.astype(BF)

    def unit(amount):
        amount = amount & 3
        real = jnp.where(amount == 0, 1.0, jnp.where(amount == 2, -1.0, 0.0))
        imag = jnp.where(amount == 1, 1.0, jnp.where(amount == 3, -1.0, 0.0))
        return real.astype(BF), imag.astype(BF)

    def turn(value, by):
        return (value[0] * by[0] - value[1] * by[1], value[1] * by[0] + value[0] * by[1])

    spin = jnp.broadcast_to(spin_ref[...], (2 * NW, nv))
    up = one_hot(spin == 0)
    down = one_hot(spin == 1)
    across = [unit((kx + upper) * rx) for kx in range(0, LX, 2)]
    for ky in range(W // NW // LX):
        base = turn((cosine, sine), unit(turns + ky * ry))
        for place, by in enumerate(across):
            c_both, s_both = turn(base, by)
            at = (ky * LX + 2 * place) * NW
            rows[pl.ds(at, 2 * NW), :] = c_both * up
            rows[pl.ds(W + at, 2 * NW), :] = s_both * up
            rows[pl.ds(2 * W + at, 2 * NW), :] = c_both * down
            rows[pl.ds(3 * W + at, 2 * NW), :] = s_both * down

    lane = iota((W, W), 1)
    plus = plus_ref[...].astype(F32)
    plus = jnp.concatenate([plus, jnp.zeros((W - nq, W), F32)], 0)
    expand = one_hot(shift_down(lane, PARTS) == iota((W, W), 0))
    index = dot(plus.T.astype(BF), expand).astype(jnp.int32)
    plus = plus.astype(BF)
    my_b = one_hot(iota((nb, W), 1) == iota((nb, W), 0) + nb * grp)
    plus_b = dot_nt(my_b, plus).astype(jnp.int32)
    place = shift_down(lane & (half - 1), na) * (na * INNER) + na * yy + (lane & (na - 1))
    my_a = one_hot(iota((W, W), 0) == place)
    prow[...] = dot(plus[:nq], my_a)
    same = one_hot(iota((nq, nq), 0) == iota((nq, nq), 1))
    cross = jnp.concatenate([cross_ref[...].astype(F32), jnp.zeros((W - na, nq), F32)], 0)
    crossing = dot_nt(same, cross.astype(BF)).astype(jnp.int32)
    crossing = (
        shift_down(crossing, nchunk) * W
        + (crossing & 1) * half
        + (shift_down(crossing, 2) & (nz - 1)) * na
        + iota((nq, W), 1)
    )

    def selectors(step):
        share = nq // pieces
        columns = pltpu.roll(plus_b, (W - step * share) % W, 1)
        for i in range(share):
            column = jnp.broadcast_to(columns[:, i : i + 1], (nb, W))
            at = pl.multiple_of((step * share + i) * nb, nb)
            sel_b[pl.ds(at, nb), :] = one_hot(column == iota((nb, W), 1))
        low = lane < half
        for i in range(share // 2):
            pair = step * (share // 2) + i
            first = prow[pl.ds(2 * pair, 1), :]
            second = prow[pl.ds(2 * pair + 1, 1), :]
            hit = iota((W, W), 0) == jnp.where(
                low, jnp.broadcast_to(first, (W, W)), jnp.broadcast_to(second, (W, W))
            ).astype(jnp.int32)
            sel_a[pair, :W, :] = one_hot(hit & low)
            sel_a[pair, W:, :] = one_hot(hit & (lane >= half))
        share = na // pieces
        columns = pltpu.roll(crossing, (W - step * share) % W, 1)
        for i in range(share):
            column = jnp.broadcast_to(columns[:, i : i + 1], (nq, nq * na))
            at = pl.multiple_of((step * share + i) * nq, nq)
            sel_out[pl.ds(at, nq), :] = one_hot(column == iota((nq, nq * na), 1))

    kern[...] = jnp.zeros_like(kern)

    def project(index, width):
        matrix_copy(index, width).wait()
        start = index * PIECE
        cols = pl.ds(start if isinstance(start, int) else pl.multiple_of(start, PIECE), width)
        projected = dot(rows[...], matrix[:, cols]).astype(BF)
        for s in range(2):
            kern[s] += dot_nt(
                projected[2 * W * s : 2 * W * (s + 1)], rows[pl.ds(2 * W * s, 2 * W), cols]
            )

    def project_piece(index, carry):
        project(index, PIECE)
        selectors(index)
        return carry

    lax.fori_loop(0, pieces, project_piece, 0)
    if tail:
        project(pieces, tail)

    ga_re = jnp.broadcast_to(free_ref[0:1, :], (W, W))
    ga_im = jnp.broadcast_to(free_ref[1:2, :], (W, W))
    gb_re, gb_im = ga_re, ga_im
    ga_re = ga_re.T
    ga_im = ga_im.T
    norm_factor = 1.0 / math.sqrt(NV)
    greens = []
    for s in range(2):
        k_re = kern[s, :W, :W] + kern[s, W:, W:]
        k_im = kern[s, W:, :W] - kern[s, :W, W:]
        h_re = ga_re * k_re - ga_im * k_im
        h_im = ga_re * k_im + ga_im * k_re
        greens.append(-(h_re * gb_re - h_im * gb_im) * norm_factor)
        greens.append(-(h_re * gb_im + h_im * gb_re) * norm_factor)
    turned = [g.T for g in greens]
    st[0, :W, :] = (turned[0] + turned[2]).astype(BF)
    st[0, W:, :] = (turned[1] + turned[3]).astype(BF)

    pl.semaphore_wait(barrier, len(plane) + nz - 1)

    def st_copy(source, slot, steps):
        return pltpu.make_async_remote_copy(
            src_ref=st.at[source],
            dst_ref=st.at[slot],
            send_sem=st_send.at[slot],
            recv_sem=st_recv.at[slot],
            device_id=plane_peer(steps),
            device_id_type=MESH,
        )

    def lr_copy(source, slot, steps):
        return pltpu.make_async_remote_copy(
            src_ref=source,
            dst_ref=lr.at[slot],
            send_sem=lr_send_sem.at[slot],
            recv_sem=lr_recv.at[slot],
            device_id=plane_peer(steps),
            device_id_type=MESH,
        )

    def lr_for(slot):
        dy, dx = slot // nx % INNER, slot % nx
        return lr_send.at[(yy + dy) % INNER * nx + (xx + dx) % nx]

    for slot in range(near - 1, 0, -1):
        st_copy(0, slot, slot).start()
    st_copy(0, near, near).start()

    greens = [g.astype(BF).astype(F32) for g in greens]
    turned = [g.astype(BF).astype(F32) for g in turned]
    part = lane & (PARTS - 1)

    def choose(values):
        picked = values[0]
        for g in range(1, PARTS):
            picked = jnp.where(part == g, values[g], picked)
        return picked

    lead = choose([jnp.take_along_axis(g, index, axis=1) for g in greens])
    trail = [jnp.take_along_axis(g, index, axis=1) for g in turned]
    trail = choose(trail).T
    order = [INNER * z + y for y in range(INNER) for z in range(nz)]
    lead = jnp.concatenate([lead[na * i : na * (i + 1)] for i in order], 0).T

    def shifted(value, by):
        by = by % W
        return value if by == 0 else pltpu.roll(value, by, 1)

    for x in range(nx):
        left = shifted(trail, -half * x)
        for y in range(INNER):
            joined = jnp.where(lane < half, left, shifted(lead, half - half * y))
            lr_send[y * nx + x] = joined.astype(BF)
    for slot in range(near - 1, 0, -1):
        lr_copy(lr_for(slot), slot, slot).start()
    lr_copy(lr_for(near), near, near).start()
    lr[0] = lr_send[yy * nx + xx]

    def take_rows(slot):
        for c in range(2):
            mine = st[slot, pl.ds(pl.multiple_of(c * W + nb * grp, nb), nb), :]
            sb[slot, c] = dot(mine, my_a)

    def select(slot, pair, count):
        picks = sel_b[pl.ds(pair * 2 * nb, count * nb), :]
        picked = dot_nt(picks, st[slot]).astype(BF)
        for q in range(count):
            for c in range(2):
                halfway[pair + q // 2, slot, c, :, pl.ds((q % 2) * W, W)] = picked[
                    q * nb : (q + 1) * nb, c * W : (c + 1) * W
                ]

    def first_selection(slot):
        take_rows(slot)
        select(slot, 0, nq)

    def own_chip(step, carry):
        @pl.when(step > 0)
        def _():
            st_copy(0, near, near).wait_recv()

        first_selection(step * near)
        return carry

    def same_core(step, carry):
        st_copy(0, step, near).wait_recv()
        st_copy(step, near + step, near).start()
        first_selection(step)
        return carry

    def forwarded(step, carry):
        st_copy(0, step, near).wait_recv()
        first_selection(step)
        return carry

    lax.fori_loop(0, CORES, own_chip, 0)
    lax.fori_loop(1, near, same_core, 0)
    for slot in range(1, near):
        lr_copy(lr.at[0], slot, near).wait_recv()
        lr_copy(lr.at[slot], near + slot, near).start()
    lax.fori_loop(near + 1, CORES * near, forwarded, 0)

    for slot in range(near, CORES * near):
        lr_copy(lr.at[0], slot, near).wait_recv()

    nw = len(plane) + 1
    four = W // (nw * PARTS)
    depth = four * PARTS

    def t_copy(dz, chunk):
        cols = pl.ds(pl.multiple_of(chunk * W, W), W)
        return pltpu.make_async_remote_copy(
            src_ref=tsend.at[(zz + dz) % nz, :, cols],
            dst_ref=trecv.at[dz, :, cols],
            send_sem=t_send.at[dz, chunk],
            recv_sem=t_recv.at[dz, chunk],
            device_id=z_peer(dz),
            device_id_type=MESH,
        )

    same_q = shift_down(iota((W, W), 0) & (depth - 1), PARTS) - shift_down(lane, half)

    def measure_chunk(chunk, carry):
        totals = []
        for sub in range(nz):
            pair = chunk * nz + sub
            partner = dot(halfway[pair].reshape(nw * 2 * nb, 2 * W), sel_a[pair])
            t_re = jnp.zeros((nb, W), F32)
            t_im = jnp.zeros((nb, W), F32)
            for w in range(nw):
                s_re = sb[w, 0]
                s_im = sb[w, 1]
                p_re = partner[2 * nb * w : 2 * nb * w + nb]
                p_im = partner[2 * nb * w + nb : 2 * nb * (w + 1)]
                t_re = t_re + (s_re * p_re - s_im * p_im)
                t_im = t_im + (s_re * p_im + s_im * p_re)
            pairs = four // 2
            if sub % pairs == 0:
                start = pl.multiple_of((chunk * (nz // pairs) + sub // pairs) * depth, depth)
                stacked = lr[:, pl.ds(start, depth), :].reshape(W, W).astype(F32)
                turned_back = stacked.T
                mine = jnp.where(core == 0, turned_back[:nb], turned_back[nb : 2 * nb])
                odd = (iota((nb, W), 1) & 1) == 1
                trailing = jnp.concatenate(
                    [
                        jnp.where(odd, -mine, mine),
                        jnp.where(odd, pltpu.roll(mine, 1, 1), pltpu.roll(mine, W - 1, 1)),
                    ],
                    0,
                ).astype(BF)
                leading = jnp.where(lane < half, pltpu.roll(stacked, half, 1), stacked)
                masked = jnp.concatenate(
                    [jnp.where(same_q == 2 * i, leading, 0.0) for i in range(pairs)], 1
                )
                exchange = dot(trailing, masked.astype(BF))
            at = sub % pairs * W
            totals.append(jnp.concatenate([t_re, t_im], 0) - exchange[:, at : at + W])
        spot = shift_down(iota((2 * nb, W), 1), na) & (nz - 1)
        cols = pl.ds(pl.multiple_of(chunk * W, W), W)
        for z in range(nz):
            moved = shifted(totals[0], -na * z)
            for sub in range(1, nz):
                moved = jnp.where(spot == sub, shifted(totals[sub], na * (sub - z)), moved)
            tsend[z, :, cols] = moved.astype(BF)
        for dz in range(1, nz):
            t_copy(dz, chunk).start()
        return carry

    chunks = nq // nchunk
    lax.fori_loop(0, chunks, measure_chunk, 0)

    total = dot_nt(tsend[zz], sel_out[...])
    for dz in range(1, nz):
        for chunk in range(chunks):
            t_copy(dz, chunk).wait_recv()
        total = total + dot_nt(trecv[dz], sel_out[...])
    out_ref[...] = total

    for slot in plane:
        st_copy(0, slot, near).wait_send()
        lr_copy(lr.at[0], slot, near).wait_send()
    for dz in range(1, nz):
        for chunk in range(chunks):
            t_copy(dz, chunk).wait_send()


def order_result(dense_ref, out_ref):
    parts, na, nq, nb = out_ref.shape
    for c in range(parts):
        out_ref[c] = dense_ref[c * nb : (c + 1) * nb, :].T.reshape(na, nq, nb)


def kernel_body(
    vertex_matrix, vertex_site, vertex_time, vertex_spin, free_green, plus_table, cross_table
):
    nblk = lax.axis_size("blk")
    ngroup = lax.axis_size("group")
    nv = vertex_matrix.shape[-1]
    nq = plus_table.shape[0]
    nz = nblk // INNER
    na = W // nblk
    nb = W // ngroup
    nw = INNER * ngroup
    npair = nq // 2
    chunks = nq // (W // na)
    vmem = pl.BlockSpec(memory_space=pltpu.VMEM)
    dma = pltpu.SemaphoreType.DMA
    out = pl.pallas_call(
        functools.partial(kernel, nblk, ngroup),
        out_shape=jax.ShapeDtypeStruct((2 * nb, na * nq), F32),
        in_specs=[pl.BlockSpec(memory_space=pltpu.HBM)] * 7,
        out_specs=vmem,
        scratch_shapes=[
            pltpu.VMEM(vertex_site.shape, jnp.int32),
            pltpu.VMEM(vertex_time.shape, jnp.int32),
            pltpu.VMEM(vertex_spin.shape, jnp.int32),
            pltpu.VMEM(free_green.shape, F32),
            pltpu.VMEM(plus_table.shape, jnp.int32),
            pltpu.VMEM(cross_table.shape, jnp.int32),
            pltpu.VMEM((nv, nv), BF),
            pltpu.VMEM((4 * W, nv), BF),
            pltpu.VMEM((2, 2 * W, 2 * W), F32),
            pltpu.VMEM((nw, 2 * W, W), BF),
            pltpu.VMEM((nw, W, W), BF),
            pltpu.VMEM((nw // CORES, W, W), BF),
            pltpu.VMEM((nq * nb, W), BF),
            pltpu.VMEM((npair, 2 * W, W), BF),
            pltpu.VMEM((na * nq, nq * na), BF),
            pltpu.VMEM((nq, W), F32),
            pltpu.VMEM((nw, 2, nb, W), F32),
            pltpu.VMEM((npair, nw, 2, nb, 2 * W), BF),
            pltpu.VMEM((nz, 2 * nb, nq * na), BF),
            pltpu.VMEM((nz, 2 * nb, nq * na), BF),
            dma((6,)),
            dma((nv // PIECE + 1,)),
            dma((nw,)),
            dma((nw,)),
            dma((nw,)),
            dma((nw,)),
            dma((nz, chunks)),
            dma((nz, chunks)),
        ],
        compiler_params=pltpu.CompilerParams(
            collective_id=0, has_side_effects=True, vmem_limit_bytes=VMEM_BYTES - 1024 * 1024
        ),
    )(
        vertex_site,
        vertex_time,
        vertex_spin,
        free_green,
        plus_table,
        cross_table,
        vertex_matrix[0],
    )
    return pl.pallas_call(
        order_result,
        out_shape=jax.ShapeDtypeStruct((2, na, nq, nb), F32),
        in_specs=[vmem],
        out_specs=vmem,
        compiler_params=pltpu.CompilerParams(vmem_limit_bytes=VMEM_BYTES - 1024 * 1024),
    )(out)


def fits(mesh):
    nblk, ngroup = mesh.shape["blk"], mesh.shape["group"]
    if nblk % INNER or W % nblk or W % ngroup:
        return False
    nz, na, nb = nblk // INNER, W // nblk, W // ngroup
    return nz == 4 and ngroup % CORES == 0 and 2 * nz * na == W and 4 * nb == W and na % 16 == 0 and nb % 16 == 0


def solution(mesh):
    in_specs = (
        P(("blk", "group"), None, None),
        P(("blk", "group"), None),
        P(("blk", "group"), None),
        P(("blk", "group"), None),
        P(),
        P(),
        P("blk", None),
    )
    out_specs = P(None, "blk", None, "group")

    def chosen(*args):
        matrix, plus = args[0], args[5]
        pieces = matrix.shape[-1] // PIECE
        small = fits(mesh) and pieces and plus.shape[0] // 2 % pieces == 0 == W // mesh.shape["blk"] % pieces and PARTS * plus.shape[0] == W and matrix.shape[-1] % 128 == 0
        return (kernel_body if small else plain_body)(*args)

    return jax.shard_map(chosen, mesh=mesh, in_specs=in_specs, out_specs=out_specs, check_vma=False)
```

```python
import functools
import math

import jax
import jax.numpy as jnp
from jax import lax
from jax.experimental import pallas as pl
from jax.experimental.pallas import tpu as pltpu
from jax.sharding import PartitionSpec as P

LX = 4
NW = 8
W = 128
NV = 1152
NT = 1024


def phases(site_ids, time_ids):
    points = jnp.arange(W, dtype=jnp.int32)
    moment = points // NW
    freq_index = points % NW
    kx_part = moment % LX
    ky_part = moment // LX
    rx_part = site_ids % LX
    ry_part = site_ids // LX
    winding = (2 * freq_index + 1)[:, None] * time_ids[None, :] + 2 * NT // LX * (
        kx_part[:, None] * rx_part[None, :] + ky_part[:, None] * ry_part[None, :]
    )
    winding = winding % (2 * NT)
    return winding.astype(jnp.float32) * (math.pi / NT)


def green_pair(matrix, site_ids, time_ids, spin_ids, free_green):
    angles = phases(site_ids, time_ids)
    cosine = jnp.cos(angles)
    sine_part = jnp.sin(angles)
    spin_up = (spin_ids == 0).astype(jnp.float32)[None, :]
    spin_down = (spin_ids == 1).astype(jnp.float32)[None, :]
    fourier_rows = jnp.concatenate(
        [cosine * spin_up, sine_part * spin_up, cosine * spin_down, sine_part * spin_down], 0
    ).astype(jnp.bfloat16)
    projected = jnp.dot(fourier_rows, matrix, preferred_element_type=jnp.float32).astype(
        jnp.bfloat16
    )
    norm_factor = 1.0 / math.sqrt(NV)
    real_free = free_green[0]
    imag_free = free_green[1]
    greens = []
    for spin_index in range(2):
        offset = 2 * W * spin_index
        cosine_rows = fourier_rows[offset : offset + W]
        sine_rows = fourier_rows[offset + W : offset + 2 * W]
        proj_real = projected[offset : offset + W]
        proj_imag = projected[offset + W : offset + 2 * W]
        left_block = jnp.concatenate(
            [
                jnp.concatenate([proj_real, proj_imag], 1),
                jnp.concatenate([proj_imag, -proj_real], 1),
            ],
            0,
        )
        right_block = jnp.concatenate([cosine_rows, sine_rows], 1)
        kernel = lax.dot_general(
            left_block, right_block, (((1,), (1,)), ((), ())), preferred_element_type=jnp.float32
        )
        kernel_real = kernel[:W]
        kernel_imag = kernel[W:]
        half_real = real_free[:, None] * kernel_real - imag_free[:, None] * kernel_imag
        half_imag = real_free[:, None] * kernel_imag + imag_free[:, None] * kernel_real
        green_real = (
            -(half_real * real_free[None, :] - half_imag * imag_free[None, :]) * norm_factor
        )
        green_imag = (
            -(half_real * imag_free[None, :] + half_imag * real_free[None, :]) * norm_factor
        )
        greens.append(jnp.stack([green_real, green_imag], 0))
    green_sum = (greens[0] + greens[1]).astype(jnp.bfloat16)
    return (green_sum, greens[0].astype(jnp.bfloat16), greens[1].astype(jnp.bfloat16))


def direct_terms(sums_piece, perm_row):
    column_ids = jnp.arange(sums_piece.shape[-1], dtype=jnp.int32)
    selector = (perm_row[:, None] == column_ids[None, :]).astype(jnp.bfloat16)
    halfway = jnp.einsum(
        "aj,kcbj->kcab", selector, sums_piece, preferred_element_type=jnp.float32
    ).astype(jnp.bfloat16)
    partner = jnp.einsum("kcaj,bj->kcab", halfway, selector, preferred_element_type=jnp.float32)
    local_copy = sums_piece.astype(jnp.float32)
    real_part = jnp.sum(local_copy[:, 0] * partner[:, 0] - local_copy[:, 1] * partner[:, 1], axis=0)
    imag_part = jnp.sum(local_copy[:, 0] * partner[:, 1] + local_copy[:, 1] * partner[:, 0], axis=0)
    return jnp.stack([real_part, imag_part], 0)


def copy_exchange(up_piece, down_piece, perm_row):
    column_ids = jnp.arange(up_piece.shape[-1], dtype=jnp.int32)
    spin_pieces = jnp.concatenate([up_piece, down_piece], 0)
    lead_values = spin_pieces[:, :, column_ids, perm_row]
    trail_values = spin_pieces[:, :, perm_row, column_ids]
    real_part = jnp.einsum(
        "ka,kb->ab", lead_values[:, 0], trail_values[:, 0], preferred_element_type=jnp.float32
    ) - jnp.einsum(
        "ka,kb->ab", lead_values[:, 1], trail_values[:, 1], preferred_element_type=jnp.float32
    )
    imag_part = jnp.einsum(
        "ka,kb->ab", lead_values[:, 0], trail_values[:, 1], preferred_element_type=jnp.float32
    ) + jnp.einsum(
        "ka,kb->ab", lead_values[:, 1], trail_values[:, 0], preferred_element_type=jnp.float32
    )
    return jnp.stack([real_part, imag_part], 0)


def plain_body(vertex_matrix, vertex_site, vertex_time, vertex_spin, free_green, plus_table, cross_table):
    green_sum, green_up, green_down = green_pair(
        vertex_matrix[0], vertex_site[0], vertex_time[0], vertex_spin[0], free_green
    )
    slices = plus_table.shape[0] // lax.axis_size("blk")
    owned_perms = lax.dynamic_slice_in_dim(plus_table, lax.axis_index("blk") * slices, slices, 0)
    sums_piece = lax.all_gather(green_sum[None], "blk", axis=0, tiled=True)
    up_piece = lax.all_gather(green_up[None], "blk", axis=0, tiled=True)
    down_piece = lax.all_gather(green_down[None], "blk", axis=0, tiled=True)

    def one_slice(perm_row):
        return direct_terms(sums_piece, perm_row) - copy_exchange(up_piece, down_piece, perm_row)

    transfer = jnp.swapaxes(lax.map(one_slice, owned_perms), 0, 1)
    shares = lax.psum_scatter(transfer, "group", scatter_dimension=3, tiled=True)
    regrouped = lax.all_to_all(shares, "blk", split_axis=2, concat_axis=1, tiled=True)
    row_ids = jnp.arange(regrouped.shape[2], dtype=jnp.int32)
    return regrouped[:, cross_table, row_ids[:, None], :]


BF = jnp.bfloat16
F32 = jnp.float32
MESH = pl.DeviceIdType.MESH
INNER = 2
CORES = 2
VMEM_BYTES = 64 * 1024 * 1024
PARTS = 4


def iota(shape, dim):
    return lax.broadcasted_iota(jnp.int32, shape, dim)


def shift_down(value, divisor):
    return value >> (divisor.bit_length() - 1)


def one_hot(condition):
    return jnp.where(condition, 1.0, 0.0).astype(BF)


def dot(left, right):
    return jnp.dot(left, right, preferred_element_type=F32)


def dot_nt(left, right):
    return lax.dot_general(left, right, (((1,), (1,)), ((), ())), preferred_element_type=F32)


def kernel(
    nblk,
    ngroup,
    site_hbm,
    time_hbm,
    spin_hbm,
    free_hbm,
    plus_hbm,
    cross_hbm,
    matrix_hbm,
    out_ref,
    site_ref,
    time_ref,
    spin_ref,
    free_ref,
    plus_ref,
    cross_ref,
    matrix,
    rows,
    st,
    lr,
    lr_send,
    sel_b,
    sel_a,
    sel_out,
    prow,
    sb,
    halfway,
    tsend,
    trecv,
    small_sem,
    matrix_sem,
    st_send,
    st_recv,
    lr_send_sem,
    lr_recv,
    t_send,
    t_recv,
):
    small = [
        pltpu.make_async_copy(source, target, small_sem.at[place])
        for place, (source, target) in enumerate(
            [
                (site_hbm, site_ref),
                (time_hbm, time_ref),
                (spin_hbm, spin_ref),
                (free_hbm, free_ref),
                (plus_hbm, plus_ref),
                (cross_hbm, cross_ref),
            ]
        )
    ]
    for copy in small:
        copy.start()
    matrix_copy = pltpu.make_async_copy(matrix_hbm, matrix, matrix_sem)
    matrix_copy.start()

    nz = nblk // INNER
    na = W // nblk
    nb = W // ngroup
    nq = plus_ref.shape[0]
    half = na * nz
    npair = nq // 2
    nchunk = W // na
    nv = site_ref.shape[1]
    blk = lax.axis_index("blk")
    grp = lax.axis_index("group")
    zz = blk // INNER
    yy = blk % INNER
    nx = ngroup // CORES
    xx = grp // CORES
    core = grp % CORES
    near = nx * INNER
    plane = list(range(1, CORES * near))

    def plane_peer(slot):
        dc, dy, dx = slot // near, slot // nx % INNER, slot % nx
        return (
            zz * INNER + (yy + dy) % INNER,
            (xx + dx) % nx * CORES + (core + dc) % CORES,
        )

    def z_peer(dz):
        return (((zz + dz) % nz) * INNER + yy, grp)

    barrier = pltpu.get_barrier_semaphore()
    for slot in plane:
        pl.semaphore_signal(barrier, inc=1, device_id=plane_peer(slot), device_id_type=MESH)
    for dz in range(1, nz):
        pl.semaphore_signal(barrier, inc=1, device_id=z_peer(dz), device_id_type=MESH)

    for copy in small:
        copy.wait()

    quarter = NT // 2
    site = jnp.broadcast_to(site_ref[...], (2 * NW, nv))
    rx = site & (LX - 1)
    ry = shift_down(site, LX)
    ids = iota((2 * NW, nv), 0)
    freq = ids & (NW - 1)
    upper = shift_down(ids, NW)
    winding = (2 * freq + 1) * time_ref[...]
    turns = shift_down(winding + quarter // 2, quarter)
    rest = (winding - turns * quarter).astype(F32) * (math.pi / NT)
    square = rest * rest
    cosine = 1.0 + square * (
        -1 / 2
        + square
        * (1 / 24 + square * (-1 / 720 + square * (1 / 40320 + square * (-1 / 3628800))))
    )
    sine = rest + rest * square * (
        -1 / 6 + square * (1 / 120 + square * (-1 / 5040 + square * (1 / 362880)))
    )
    cosine = cosine.astype(BF)
    sine = sine.astype(BF)

    def unit(amount):
        amount = amount & 3
        real = jnp.where(amount == 0, 1.0, jnp.where(amount == 2, -1.0, 0.0))
        imag = jnp.where(amount == 1, 1.0, jnp.where(amount == 3, -1.0, 0.0))
        return real.astype(BF), imag.astype(BF)

    def turn(value, by):
        return (value[0] * by[0] - value[1] * by[1], value[1] * by[0] + value[0] * by[1])

    spin = jnp.broadcast_to(spin_ref[...], (2 * NW, nv))
    up = one_hot(spin == 0)
    down = one_hot(spin == 1)
    across = [unit((kx + upper) * rx) for kx in range(0, LX, 2)]
    for ky in range(W // NW // LX):
        base = turn((cosine, sine), unit(turns + ky * ry))
        for place, by in enumerate(across):
            c_both, s_both = turn(base, by)
            at = (ky * LX + 2 * place) * NW
            rows[pl.ds(at, 2 * NW), :] = c_both * up
            rows[pl.ds(W + at, 2 * NW), :] = s_both * up
            rows[pl.ds(2 * W + at, 2 * NW), :] = c_both * down
            rows[pl.ds(3 * W + at, 2 * NW), :] = s_both * down

    matrix_copy.wait()
    projected = dot(rows[...], matrix[...]).astype(BF)
    kern = [
        dot_nt(projected[2 * W * s : 2 * W * (s + 1)], rows[2 * W * s : 2 * W * (s + 1), :])
        for s in range(2)
    ]

    ga_re = jnp.broadcast_to(free_ref[0:1, :], (W, W))
    ga_im = jnp.broadcast_to(free_ref[1:2, :], (W, W))
    gb_re, gb_im = ga_re, ga_im
    ga_re = ga_re.T
    ga_im = ga_im.T
    norm_factor = 1.0 / math.sqrt(NV)
    greens = []
    for s in range(2):
        k_re = kern[s][:W, :W] + kern[s][W:, W:]
        k_im = kern[s][W:, :W] - kern[s][:W, W:]
        h_re = ga_re * k_re - ga_im * k_im
        h_im = ga_re * k_im + ga_im * k_re
        greens.append(-(h_re * gb_re - h_im * gb_im) * norm_factor)
        greens.append(-(h_re * gb_im + h_im * gb_re) * norm_factor)
    turned = [g.T for g in greens]
    st[0, :W, :] = (turned[0] + turned[2]).astype(BF)
    st[0, W:, :] = (turned[1] + turned[3]).astype(BF)

    pl.semaphore_wait(barrier, len(plane) + nz - 1)

    def st_copy(source, slot, steps):
        return pltpu.make_async_remote_copy(
            src_ref=st.at[source],
            dst_ref=st.at[slot],
            send_sem=st_send.at[slot],
            recv_sem=st_recv.at[slot],
            device_id=plane_peer(steps),
            device_id_type=MESH,
        )

    def lr_copy(source, slot, steps):
        return pltpu.make_async_remote_copy(
            src_ref=source,
            dst_ref=lr.at[slot],
            send_sem=lr_send_sem.at[slot],
            recv_sem=lr_recv.at[slot],
            device_id=plane_peer(steps),
            device_id_type=MESH,
        )

    def lr_for(slot):
        dy, dx = slot // nx % INNER, slot % nx
        return lr_send.at[(yy + dy) % INNER * nx + (xx + dx) % nx]

    for slot in range(near - 1, 0, -1):
        st_copy(0, slot, slot).start()
    st_copy(0, near, near).start()

    greens = [g.astype(BF).astype(F32) for g in greens]
    turned = [g.astype(BF).astype(F32) for g in turned]
    plus = plus_ref[...].astype(F32)
    plus_turned = jnp.concatenate([plus, jnp.zeros((W - nq, W), F32)], 0).T
    expand = one_hot(shift_down(iota((W, W), 1), PARTS) == iota((W, W), 0))
    index = dot(plus_turned.astype(BF), expand).astype(jnp.int32)
    lane = iota((W, W), 1)
    part = lane & (PARTS - 1)

    def choose(values):
        picked = values[0]
        for g in range(1, PARTS):
            picked = jnp.where(part == g, values[g], picked)
        return picked

    lead = choose([jnp.take_along_axis(g, index, axis=1) for g in greens])
    trail = [jnp.take_along_axis(g, index, axis=1) for g in turned]
    trail = choose(trail).T
    order = [INNER * z + y for y in range(INNER) for z in range(nz)]
    lead = jnp.concatenate([lead[na * i : na * (i + 1)] for i in order], 0).T

    def shifted(value, by):
        by = by % W
        return value if by == 0 else pltpu.roll(value, by, 1)

    for x in range(nx):
        left = shifted(trail, -half * x)
        for y in range(INNER):
            joined = jnp.where(lane < half, left, shifted(lead, half - half * y))
            lr_send[y * nx + x] = joined.astype(BF)
    for slot in range(near - 1, 0, -1):
        lr_copy(lr_for(slot), slot, slot).start()
    lr_copy(lr_for(near), near, near).start()
    lr[0] = lr_send[yy * nx + xx]

    plus_bf = plus.astype(BF)
    my_b = one_hot(iota((nb, W), 1) == iota((nb, W), 0) + nb * grp)
    plus_b = dot_nt(my_b, plus_bf).astype(jnp.int32)
    for q in range(nq):
        column = jnp.broadcast_to(plus_b[:, q : q + 1], (nb, W))
        sel_b[pl.ds(q * nb, nb), :] = one_hot(column == iota((nb, W), 1))
    place = shift_down(lane & (half - 1), na) * (na * INNER) + na * yy + (lane & (na - 1))
    my_a = one_hot(iota((W, W), 0) == place)
    prow[...] = dot(plus_bf, my_a)

    def pair_selector(pair, carry):
        first = prow[pl.ds(2 * pair, 1), :]
        second = prow[pl.ds(2 * pair + 1, 1), :]
        low = lane < half
        hit = iota((W, W), 0) == jnp.where(
            low, jnp.broadcast_to(first, (W, W)), jnp.broadcast_to(second, (W, W))
        ).astype(jnp.int32)
        sel_a[pair, :W, :] = one_hot(hit & low)
        sel_a[pair, W:, :] = one_hot(hit & (lane >= half))
        return carry

    lax.fori_loop(0, npair, pair_selector, 0)

    same = one_hot(iota((nq, nq), 0) == iota((nq, nq), 1))
    crossing = dot_nt(same, cross_ref[...].astype(F32).astype(BF)).astype(jnp.int32)
    crossing = (
        shift_down(crossing, nchunk) * W
        + (crossing & 1) * half
        + (shift_down(crossing, 2) & (nz - 1)) * na
    )
    for r in range(na):
        column = jnp.broadcast_to(crossing[:, r : r + 1] + r, (nq, nq * na))
        sel_out[pl.ds(r * nq, nq), :] = one_hot(column == iota((nq, nq * na), 1))

    def first_selection(slot):
        for c in range(2):
            mine = st[slot, pl.ds(pl.multiple_of(c * W + nb * grp, nb), nb), :]
            sb[slot, c] = dot(mine, my_a)
            chosen = dot_nt(sel_b[...], st[slot, c * W : (c + 1) * W, :]).astype(BF)
            for q in range(nq):
                halfway[q // 2, slot, c, :, pl.ds((q % 2) * W, W)] = chosen[
                    q * nb : (q + 1) * nb
                ]

    def own_chip(step, carry):
        @pl.when(step > 0)
        def _():
            st_copy(0, near, near).wait_recv()

        first_selection(step * near)
        return carry

    def same_core(step, carry):
        st_copy(0, step, near).wait_recv()
        st_copy(step, near + step, near).start()
        return carry

    def peers(step, carry):
        first_selection(step)
        return carry

    def forwarded(step, carry):
        st_copy(0, step, near).wait_recv()
        first_selection(step)
        return carry

    lax.fori_loop(0, CORES, own_chip, 0)
    lax.fori_loop(1, near, same_core, 0)
    lax.fori_loop(1, near, peers, 0)
    for slot in range(1, near):
        lr_copy(lr.at[0], slot, near).wait_recv()
        lr_copy(lr.at[slot], near + slot, near).start()
    lax.fori_loop(near + 1, CORES * near, forwarded, 0)

    for slot in range(near, CORES * near):
        lr_copy(lr.at[0], slot, near).wait_recv()

    nw = len(plane) + 1
    four = W // (nw * PARTS)
    depth = four * PARTS

    def t_copy(dz, chunk):
        cols = pl.ds(pl.multiple_of(chunk * W, W), W)
        return pltpu.make_async_remote_copy(
            src_ref=tsend.at[(zz + dz) % nz, :, cols],
            dst_ref=trecv.at[dz, :, cols],
            send_sem=t_send.at[dz, chunk],
            recv_sem=t_recv.at[dz, chunk],
            device_id=z_peer(dz),
            device_id_type=MESH,
        )

    same_q = shift_down(iota((W, W), 0) & (depth - 1), PARTS) - shift_down(lane, half)

    def measure_chunk(chunk, carry):
        totals = []
        for sub in range(nz):
            pair = chunk * nz + sub
            partner = dot(halfway[pair].reshape(nw * 2 * nb, 2 * W), sel_a[pair])
            t_re = jnp.zeros((nb, W), F32)
            t_im = jnp.zeros((nb, W), F32)
            for w in range(nw):
                s_re = sb[w, 0]
                s_im = sb[w, 1]
                p_re = partner[2 * nb * w : 2 * nb * w + nb]
                p_im = partner[2 * nb * w + nb : 2 * nb * (w + 1)]
                t_re = t_re + (s_re * p_re - s_im * p_im)
                t_im = t_im + (s_re * p_im + s_im * p_re)
            pairs = four // 2
            if sub % pairs == 0:
                start = pl.multiple_of((chunk * (nz // pairs) + sub // pairs) * depth, depth)
                stacked = lr[:, pl.ds(start, depth), :].reshape(W, W).astype(F32)
                turned_back = stacked.T
                mine = jnp.where(core == 0, turned_back[:nb], turned_back[nb : 2 * nb])
                odd = (iota((nb, W), 1) & 1) == 1
                trailing = jnp.concatenate(
                    [
                        jnp.where(odd, -mine, mine),
                        jnp.where(odd, pltpu.roll(mine, 1, 1), pltpu.roll(mine, W - 1, 1)),
                    ],
                    0,
                ).astype(BF)
                leading = jnp.where(lane < half, pltpu.roll(stacked, half, 1), stacked)
            masked = jnp.where(same_q == 2 * (sub % pairs), leading, 0.0)
            exchange = dot(trailing, masked.astype(BF))
            totals.append(jnp.concatenate([t_re, t_im], 0) - exchange)
        spot = shift_down(iota((2 * nb, W), 1), na) & (nz - 1)
        cols = pl.ds(pl.multiple_of(chunk * W, W), W)
        for z in range(nz):
            moved = shifted(totals[0], -na * z)
            for sub in range(1, nz):
                moved = jnp.where(spot == sub, shifted(totals[sub], na * (sub - z)), moved)
            tsend[z, :, cols] = moved.astype(BF)
        for dz in range(1, nz):
            t_copy(dz, chunk).start()
        return carry

    chunks = nq // nchunk
    lax.fori_loop(0, chunks, measure_chunk, 0)

    total = dot_nt(tsend[zz], sel_out[...])
    for dz in range(1, nz):
        for chunk in range(chunks):
            t_copy(dz, chunk).wait_recv()
        total = total + dot_nt(trecv[dz], sel_out[...])
    out_ref[...] = total

    for slot in plane:
        st_copy(0, slot, near).wait_send()
        lr_copy(lr.at[0], slot, near).wait_send()
    for dz in range(1, nz):
        for chunk in range(chunks):
            t_copy(dz, chunk).wait_send()


def order_result(dense_ref, out_ref):
    parts, na, nq, nb = out_ref.shape
    for c in range(parts):
        out_ref[c] = dense_ref[c * nb : (c + 1) * nb, :].T.reshape(na, nq, nb)


def kernel_body(
    vertex_matrix, vertex_site, vertex_time, vertex_spin, free_green, plus_table, cross_table
):
    nblk = lax.axis_size("blk")
    ngroup = lax.axis_size("group")
    nv = vertex_matrix.shape[-1]
    nq = plus_table.shape[0]
    nz = nblk // INNER
    na = W // nblk
    nb = W // ngroup
    nw = INNER * ngroup
    npair = nq // 2
    chunks = nq // (W // na)
    vmem = pl.BlockSpec(memory_space=pltpu.VMEM)
    dma = pltpu.SemaphoreType.DMA
    out = pl.pallas_call(
        functools.partial(kernel, nblk, ngroup),
        out_shape=jax.ShapeDtypeStruct((2 * nb, na * nq), F32),
        in_specs=[pl.BlockSpec(memory_space=pltpu.HBM)] * 7,
        out_specs=vmem,
        scratch_shapes=[
            pltpu.VMEM(vertex_site.shape, jnp.int32),
            pltpu.VMEM(vertex_time.shape, jnp.int32),
            pltpu.VMEM(vertex_spin.shape, jnp.int32),
            pltpu.VMEM(free_green.shape, F32),
            pltpu.VMEM(plus_table.shape, jnp.int32),
            pltpu.VMEM(cross_table.shape, jnp.int32),
            pltpu.VMEM((nv, nv), BF),
            pltpu.VMEM((4 * W, nv), BF),
            pltpu.VMEM((nw, 2 * W, W), BF),
            pltpu.VMEM((nw, W, W), BF),
            pltpu.VMEM((nw // CORES, W, W), BF),
            pltpu.VMEM((nq * nb, W), BF),
            pltpu.VMEM((npair, 2 * W, W), BF),
            pltpu.VMEM((na * nq, nq * na), BF),
            pltpu.VMEM((nq, W), F32),
            pltpu.VMEM((nw, 2, nb, W), F32),
            pltpu.VMEM((npair, nw, 2, nb, 2 * W), BF),
            pltpu.VMEM((nz, 2 * nb, nq * na), BF),
            pltpu.VMEM((nz, 2 * nb, nq * na), BF),
            dma((6,)),
            dma,
            dma((nw,)),
            dma((nw,)),
            dma((nw,)),
            dma((nw,)),
            dma((nz, chunks)),
            dma((nz, chunks)),
        ],
        compiler_params=pltpu.CompilerParams(
            collective_id=0, has_side_effects=True, vmem_limit_bytes=VMEM_BYTES - 1024 * 1024
        ),
    )(
        vertex_site,
        vertex_time,
        vertex_spin,
        free_green,
        plus_table,
        cross_table,
        vertex_matrix[0],
    )
    return pl.pallas_call(
        order_result,
        out_shape=jax.ShapeDtypeStruct((2, na, nq, nb), F32),
        in_specs=[vmem],
        out_specs=vmem,
        compiler_params=pltpu.CompilerParams(vmem_limit_bytes=VMEM_BYTES - 1024 * 1024),
    )(out)


def fits(mesh):
    nblk, ngroup = mesh.shape["blk"], mesh.shape["group"]
    if nblk % INNER or W % nblk or W % ngroup:
        return False
    nz, na, nb = nblk // INNER, W // nblk, W // ngroup
    return nz == 4 and ngroup % CORES == 0 and 2 * nz * na == W and 4 * nb == W and na % 16 == 0 and nb % 16 == 0


def solution(mesh):
    in_specs = (
        P(("blk", "group"), None, None),
        P(("blk", "group"), None),
        P(("blk", "group"), None),
        P(("blk", "group"), None),
        P(),
        P(),
        P("blk", None),
    )
    out_specs = P(None, "blk", None, "group")

    def chosen(*args):
        matrix, plus = args[0], args[5]
        small = fits(mesh) and PARTS * plus.shape[0] == W and matrix.shape[-1] % 128 == 0
        return (kernel_body if small else plain_body)(*args)

    return jax.shard_map(chosen, mesh=mesh, in_specs=in_specs, out_specs=out_specs, check_vma=False)
```

```python
import functools
import math

import jax
import jax.numpy as jnp
from jax import lax
from jax.experimental import pallas as pl
from jax.experimental.pallas import tpu as pltpu
from jax.sharding import PartitionSpec as P

LX = 4
NW = 8
W = 128
NV = 1152
NT = 1024


def phases(site_ids, time_ids):
    points = jnp.arange(W, dtype=jnp.int32)
    moment = points // NW
    freq_index = points % NW
    kx_part = moment % LX
    ky_part = moment // LX
    rx_part = site_ids % LX
    ry_part = site_ids // LX
    winding = (2 * freq_index + 1)[:, None] * time_ids[None, :] + 2 * NT // LX * (
        kx_part[:, None] * rx_part[None, :] + ky_part[:, None] * ry_part[None, :]
    )
    winding = winding % (2 * NT)
    return winding.astype(jnp.float32) * (math.pi / NT)


def green_pair(matrix, site_ids, time_ids, spin_ids, free_green):
    angles = phases(site_ids, time_ids)
    cosine = jnp.cos(angles)
    sine_part = jnp.sin(angles)
    spin_up = (spin_ids == 0).astype(jnp.float32)[None, :]
    spin_down = (spin_ids == 1).astype(jnp.float32)[None, :]
    fourier_rows = jnp.concatenate(
        [cosine * spin_up, sine_part * spin_up, cosine * spin_down, sine_part * spin_down], 0
    ).astype(jnp.bfloat16)
    projected = jnp.dot(fourier_rows, matrix, preferred_element_type=jnp.float32).astype(
        jnp.bfloat16
    )
    norm_factor = 1.0 / math.sqrt(NV)
    real_free = free_green[0]
    imag_free = free_green[1]
    greens = []
    for spin_index in range(2):
        offset = 2 * W * spin_index
        cosine_rows = fourier_rows[offset : offset + W]
        sine_rows = fourier_rows[offset + W : offset + 2 * W]
        proj_real = projected[offset : offset + W]
        proj_imag = projected[offset + W : offset + 2 * W]
        left_block = jnp.concatenate(
            [
                jnp.concatenate([proj_real, proj_imag], 1),
                jnp.concatenate([proj_imag, -proj_real], 1),
            ],
            0,
        )
        right_block = jnp.concatenate([cosine_rows, sine_rows], 1)
        kernel = lax.dot_general(
            left_block, right_block, (((1,), (1,)), ((), ())), preferred_element_type=jnp.float32
        )
        kernel_real = kernel[:W]
        kernel_imag = kernel[W:]
        half_real = real_free[:, None] * kernel_real - imag_free[:, None] * kernel_imag
        half_imag = real_free[:, None] * kernel_imag + imag_free[:, None] * kernel_real
        green_real = (
            -(half_real * real_free[None, :] - half_imag * imag_free[None, :]) * norm_factor
        )
        green_imag = (
            -(half_real * imag_free[None, :] + half_imag * real_free[None, :]) * norm_factor
        )
        greens.append(jnp.stack([green_real, green_imag], 0))
    green_sum = (greens[0] + greens[1]).astype(jnp.bfloat16)
    return (green_sum, greens[0].astype(jnp.bfloat16), greens[1].astype(jnp.bfloat16))


def direct_terms(sums_piece, perm_row):
    column_ids = jnp.arange(sums_piece.shape[-1], dtype=jnp.int32)
    selector = (perm_row[:, None] == column_ids[None, :]).astype(jnp.bfloat16)
    halfway = jnp.einsum(
        "aj,kcbj->kcab", selector, sums_piece, preferred_element_type=jnp.float32
    ).astype(jnp.bfloat16)
    partner = jnp.einsum("kcaj,bj->kcab", halfway, selector, preferred_element_type=jnp.float32)
    local_copy = sums_piece.astype(jnp.float32)
    real_part = jnp.sum(local_copy[:, 0] * partner[:, 0] - local_copy[:, 1] * partner[:, 1], axis=0)
    imag_part = jnp.sum(local_copy[:, 0] * partner[:, 1] + local_copy[:, 1] * partner[:, 0], axis=0)
    return jnp.stack([real_part, imag_part], 0)


def copy_exchange(up_piece, down_piece, perm_row):
    column_ids = jnp.arange(up_piece.shape[-1], dtype=jnp.int32)
    spin_pieces = jnp.concatenate([up_piece, down_piece], 0)
    lead_values = spin_pieces[:, :, column_ids, perm_row]
    trail_values = spin_pieces[:, :, perm_row, column_ids]
    real_part = jnp.einsum(
        "ka,kb->ab", lead_values[:, 0], trail_values[:, 0], preferred_element_type=jnp.float32
    ) - jnp.einsum(
        "ka,kb->ab", lead_values[:, 1], trail_values[:, 1], preferred_element_type=jnp.float32
    )
    imag_part = jnp.einsum(
        "ka,kb->ab", lead_values[:, 0], trail_values[:, 1], preferred_element_type=jnp.float32
    ) + jnp.einsum(
        "ka,kb->ab", lead_values[:, 1], trail_values[:, 0], preferred_element_type=jnp.float32
    )
    return jnp.stack([real_part, imag_part], 0)


def plain_body(vertex_matrix, vertex_site, vertex_time, vertex_spin, free_green, plus_table, cross_table):
    green_sum, green_up, green_down = green_pair(
        vertex_matrix[0], vertex_site[0], vertex_time[0], vertex_spin[0], free_green
    )
    slices = plus_table.shape[0] // lax.axis_size("blk")
    owned_perms = lax.dynamic_slice_in_dim(plus_table, lax.axis_index("blk") * slices, slices, 0)
    sums_piece = lax.all_gather(green_sum[None], "blk", axis=0, tiled=True)
    up_piece = lax.all_gather(green_up[None], "blk", axis=0, tiled=True)
    down_piece = lax.all_gather(green_down[None], "blk", axis=0, tiled=True)

    def one_slice(perm_row):
        return direct_terms(sums_piece, perm_row) - copy_exchange(up_piece, down_piece, perm_row)

    transfer = jnp.swapaxes(lax.map(one_slice, owned_perms), 0, 1)
    shares = lax.psum_scatter(transfer, "group", scatter_dimension=3, tiled=True)
    regrouped = lax.all_to_all(shares, "blk", split_axis=2, concat_axis=1, tiled=True)
    row_ids = jnp.arange(regrouped.shape[2], dtype=jnp.int32)
    return regrouped[:, cross_table, row_ids[:, None], :]


BF = jnp.bfloat16
F32 = jnp.float32
MESH = pl.DeviceIdType.MESH
INNER = 2
CORES = 2
VMEM_BYTES = 64 * 1024 * 1024
PARTS = 4


def iota(shape, dim):
    return lax.broadcasted_iota(jnp.int32, shape, dim)


def shift_down(value, divisor):
    return value >> (divisor.bit_length() - 1)


def one_hot(condition):
    return jnp.where(condition, 1.0, 0.0).astype(BF)


def dot(left, right):
    return jnp.dot(left, right, preferred_element_type=F32)


def dot_nt(left, right):
    return lax.dot_general(left, right, (((1,), (1,)), ((), ())), preferred_element_type=F32)


def kernel(
    nblk,
    ngroup,
    site_hbm,
    time_hbm,
    spin_hbm,
    free_hbm,
    plus_hbm,
    cross_hbm,
    matrix_hbm,
    out_ref,
    site_ref,
    time_ref,
    spin_ref,
    free_ref,
    plus_ref,
    cross_ref,
    matrix,
    rows,
    st,
    lr,
    lr_send,
    sel_b,
    sel_a,
    sel_out,
    prow,
    sb,
    halfway,
    tsend,
    trecv,
    small_sem,
    matrix_sem,
    st_send,
    st_recv,
    lr_send_sem,
    lr_recv,
    t_send,
    t_recv,
):
    small = [
        pltpu.make_async_copy(source, target, small_sem.at[place])
        for place, (source, target) in enumerate(
            [
                (site_hbm, site_ref),
                (time_hbm, time_ref),
                (spin_hbm, spin_ref),
                (free_hbm, free_ref),
                (plus_hbm, plus_ref),
                (cross_hbm, cross_ref),
            ]
        )
    ]
    for copy in small:
        copy.start()
    matrix_copy = pltpu.make_async_copy(matrix_hbm, matrix, matrix_sem)
    matrix_copy.start()

    nz = nblk // INNER
    na = W // nblk
    nb = W // ngroup
    nq = plus_ref.shape[0]
    half = na * nz
    npair = nq // 2
    nchunk = W // na
    nv = site_ref.shape[1]
    blk = lax.axis_index("blk")
    grp = lax.axis_index("group")
    zz = blk // INNER
    yy = blk % INNER
    nx = ngroup // CORES
    xx = grp // CORES
    core = grp % CORES
    near = nx * INNER
    plane = list(range(1, CORES * near))

    def plane_peer(slot):
        dc, dy, dx = slot // near, slot // nx % INNER, slot % nx
        return (
            zz * INNER + (yy + dy) % INNER,
            (xx + dx) % nx * CORES + (core + dc) % CORES,
        )

    def z_peer(dz):
        return (((zz + dz) % nz) * INNER + yy, grp)

    barrier = pltpu.get_barrier_semaphore()
    for slot in plane:
        pl.semaphore_signal(barrier, inc=1, device_id=plane_peer(slot), device_id_type=MESH)
    for dz in range(1, nz):
        pl.semaphore_signal(barrier, inc=1, device_id=z_peer(dz), device_id_type=MESH)

    for copy in small:
        copy.wait()

    quarter = NT // 2
    site = jnp.broadcast_to(site_ref[...], (2 * NW, nv))
    rx = site & (LX - 1)
    ry = shift_down(site, LX)
    ids = iota((2 * NW, nv), 0)
    freq = ids & (NW - 1)
    upper = shift_down(ids, NW)
    winding = (2 * freq + 1) * time_ref[...]
    turns = shift_down(winding + quarter // 2, quarter)
    rest = (winding - turns * quarter).astype(F32) * (math.pi / NT)
    square = rest * rest
    cosine = 1.0 + square * (
        -1 / 2
        + square
        * (1 / 24 + square * (-1 / 720 + square * (1 / 40320 + square * (-1 / 3628800))))
    )
    sine = rest + rest * square * (
        -1 / 6 + square * (1 / 120 + square * (-1 / 5040 + square * (1 / 362880)))
    )
    cosine = cosine.astype(BF)
    sine = sine.astype(BF)

    def unit(amount):
        amount = amount & 3
        real = jnp.where(amount == 0, 1.0, jnp.where(amount == 2, -1.0, 0.0))
        imag = jnp.where(amount == 1, 1.0, jnp.where(amount == 3, -1.0, 0.0))
        return real.astype(BF), imag.astype(BF)

    def turn(value, by):
        return (value[0] * by[0] - value[1] * by[1], value[1] * by[0] + value[0] * by[1])

    spin = jnp.broadcast_to(spin_ref[...], (2 * NW, nv))
    up = one_hot(spin == 0)
    down = one_hot(spin == 1)
    across = [unit((kx + upper) * rx) for kx in range(0, LX, 2)]
    for ky in range(W // NW // LX):
        base = turn((cosine, sine), unit(turns + ky * ry))
        for place, by in enumerate(across):
            c_both, s_both = turn(base, by)
            at = (ky * LX + 2 * place) * NW
            rows[pl.ds(at, 2 * NW), :] = c_both * up
            rows[pl.ds(W + at, 2 * NW), :] = s_both * up
            rows[pl.ds(2 * W + at, 2 * NW), :] = c_both * down
            rows[pl.ds(3 * W + at, 2 * NW), :] = s_both * down

    matrix_copy.wait()
    projected = dot(rows[...], matrix[...]).astype(BF)
    kern = [
        dot_nt(projected[2 * W * s : 2 * W * (s + 1)], rows[2 * W * s : 2 * W * (s + 1), :])
        for s in range(2)
    ]

    ga_re = jnp.broadcast_to(free_ref[0:1, :], (W, W))
    ga_im = jnp.broadcast_to(free_ref[1:2, :], (W, W))
    gb_re, gb_im = ga_re, ga_im
    ga_re = ga_re.T
    ga_im = ga_im.T
    norm_factor = 1.0 / math.sqrt(NV)
    greens = []
    for s in range(2):
        k_re = kern[s][:W, :W] + kern[s][W:, W:]
        k_im = kern[s][W:, :W] - kern[s][:W, W:]
        h_re = ga_re * k_re - ga_im * k_im
        h_im = ga_re * k_im + ga_im * k_re
        greens.append(-(h_re * gb_re - h_im * gb_im) * norm_factor)
        greens.append(-(h_re * gb_im + h_im * gb_re) * norm_factor)
    turned = [g.T for g in greens]
    st[0, :W, :] = (turned[0] + turned[2]).astype(BF)
    st[0, W:, :] = (turned[1] + turned[3]).astype(BF)

    pl.semaphore_wait(barrier, len(plane) + nz - 1)

    def st_copy(source, slot, steps):
        return pltpu.make_async_remote_copy(
            src_ref=st.at[source],
            dst_ref=st.at[slot],
            send_sem=st_send.at[slot],
            recv_sem=st_recv.at[slot],
            device_id=plane_peer(steps),
            device_id_type=MESH,
        )

    def lr_copy(source, slot, steps):
        return pltpu.make_async_remote_copy(
            src_ref=source,
            dst_ref=lr.at[slot],
            send_sem=lr_send_sem.at[slot],
            recv_sem=lr_recv.at[slot],
            device_id=plane_peer(steps),
            device_id_type=MESH,
        )

    def lr_for(slot):
        dy, dx = slot // nx % INNER, slot % nx
        return lr_send.at[(yy + dy) % INNER * nx + (xx + dx) % nx]

    for slot in range(near - 1, 0, -1):
        st_copy(0, slot, slot).start()
    st_copy(0, near, near).start()

    greens = [g.astype(BF).astype(F32) for g in greens]
    turned = [g.astype(BF).astype(F32) for g in turned]
    plus = plus_ref[...].astype(F32)
    plus_turned = jnp.concatenate([plus, jnp.zeros((W - nq, W), F32)], 0).T
    expand = one_hot(shift_down(iota((W, W), 1), PARTS) == iota((W, W), 0))
    index = dot(plus_turned.astype(BF), expand).astype(jnp.int32)
    lane = iota((W, W), 1)
    part = lane & (PARTS - 1)

    def choose(values):
        picked = values[0]
        for g in range(1, PARTS):
            picked = jnp.where(part == g, values[g], picked)
        return picked

    lead = choose([jnp.take_along_axis(g, index, axis=1) for g in greens])
    trail = [jnp.take_along_axis(g, index, axis=1) for g in turned]
    trail = choose(trail).T
    order = [INNER * z + y for y in range(INNER) for z in range(nz)]
    lead = jnp.concatenate([lead[na * i : na * (i + 1)] for i in order], 0).T

    def shifted(value, by):
        by = by % W
        return value if by == 0 else pltpu.roll(value, by, 1)

    for x in range(nx):
        left = shifted(trail, -half * x)
        for y in range(INNER):
            joined = jnp.where(lane < half, left, shifted(lead, half - half * y))
            lr_send[y * nx + x] = joined.astype(BF)
    for slot in range(near - 1, 0, -1):
        lr_copy(lr_for(slot), slot, slot).start()
    lr_copy(lr_for(near), near, near).start()
    lr[0] = lr_send[yy * nx + xx]

    plus_bf = plus.astype(BF)
    my_b = one_hot(iota((nb, W), 1) == iota((nb, W), 0) + nb * grp)
    plus_b = dot_nt(my_b, plus_bf).astype(jnp.int32)
    for q in range(nq):
        column = jnp.broadcast_to(plus_b[:, q : q + 1], (nb, W))
        sel_b[pl.ds(q * nb, nb), :] = one_hot(column == iota((nb, W), 1))
    place = shift_down(lane & (half - 1), na) * (na * INNER) + na * yy + (lane & (na - 1))
    my_a = one_hot(iota((W, W), 0) == place)
    prow[...] = dot(plus_bf, my_a)

    def pair_selector(pair, carry):
        first = prow[pl.ds(2 * pair, 1), :]
        second = prow[pl.ds(2 * pair + 1, 1), :]
        low = lane < half
        hit = iota((W, W), 0) == jnp.where(
            low, jnp.broadcast_to(first, (W, W)), jnp.broadcast_to(second, (W, W))
        ).astype(jnp.int32)
        sel_a[pair, :W, :] = one_hot(hit & low)
        sel_a[pair, W:, :] = one_hot(hit & (lane >= half))
        return carry

    lax.fori_loop(0, npair, pair_selector, 0)

    same = one_hot(iota((nq, nq), 0) == iota((nq, nq), 1))
    crossing = dot_nt(same, cross_ref[...].astype(F32).astype(BF)).astype(jnp.int32)
    crossing = (
        shift_down(crossing, nchunk) * W
        + (crossing & 1) * half
        + (shift_down(crossing, 2) & (nz - 1)) * na
    )
    for r in range(na):
        column = jnp.broadcast_to(crossing[:, r : r + 1] + r, (nq, nq * na))
        sel_out[pl.ds(r * nq, nq), :] = one_hot(column == iota((nq, nq * na), 1))

    def first_selection(slot):
        picked = dot_nt(sel_b[...], st[slot]).astype(BF)
        for c in range(2):
            mine = st[slot, pl.ds(pl.multiple_of(c * W + nb * grp, nb), nb), :]
            sb[slot, c] = dot(mine, my_a)
            for q in range(nq):
                halfway[q // 2, slot, c, :, pl.ds((q % 2) * W, W)] = picked[
                    q * nb : (q + 1) * nb, c * W : (c + 1) * W
                ]

    def own_chip(step, carry):
        @pl.when(step > 0)
        def _():
            st_copy(0, near, near).wait_recv()

        first_selection(step * near)
        return carry

    def same_core(step, carry):
        st_copy(0, step, near).wait_recv()
        st_copy(step, near + step, near).start()
        return carry

    def peers(step, carry):
        first_selection(step)
        return carry

    def forwarded(step, carry):
        st_copy(0, step, near).wait_recv()
        first_selection(step)
        return carry

    lax.fori_loop(0, CORES, own_chip, 0)
    lax.fori_loop(1, near, same_core, 0)
    lax.fori_loop(1, near, peers, 0)
    for slot in range(1, near):
        lr_copy(lr.at[0], slot, near).wait_recv()
        lr_copy(lr.at[slot], near + slot, near).start()
    lax.fori_loop(near + 1, CORES * near, forwarded, 0)

    for slot in range(near, CORES * near):
        lr_copy(lr.at[0], slot, near).wait_recv()

    nw = len(plane) + 1
    four = W // (nw * PARTS)
    depth = four * PARTS

    def t_copy(dz, chunk):
        cols = pl.ds(pl.multiple_of(chunk * W, W), W)
        return pltpu.make_async_remote_copy(
            src_ref=tsend.at[(zz + dz) % nz, :, cols],
            dst_ref=trecv.at[dz, :, cols],
            send_sem=t_send.at[dz, chunk],
            recv_sem=t_recv.at[dz, chunk],
            device_id=z_peer(dz),
            device_id_type=MESH,
        )

    same_q = shift_down(iota((W, W), 0) & (depth - 1), PARTS) - shift_down(lane, half)

    def measure_chunk(chunk, carry):
        totals = []
        for sub in range(nz):
            pair = chunk * nz + sub
            partner = dot(halfway[pair].reshape(nw * 2 * nb, 2 * W), sel_a[pair])
            t_re = jnp.zeros((nb, W), F32)
            t_im = jnp.zeros((nb, W), F32)
            for w in range(nw):
                s_re = sb[w, 0]
                s_im = sb[w, 1]
                p_re = partner[2 * nb * w : 2 * nb * w + nb]
                p_im = partner[2 * nb * w + nb : 2 * nb * (w + 1)]
                t_re = t_re + (s_re * p_re - s_im * p_im)
                t_im = t_im + (s_re * p_im + s_im * p_re)
            pairs = four // 2
            if sub % pairs == 0:
                start = pl.multiple_of((chunk * (nz // pairs) + sub // pairs) * depth, depth)
                stacked = lr[:, pl.ds(start, depth), :].reshape(W, W).astype(F32)
                turned_back = stacked.T
                mine = jnp.where(core == 0, turned_back[:nb], turned_back[nb : 2 * nb])
                odd = (iota((nb, W), 1) & 1) == 1
                trailing = jnp.concatenate(
                    [
                        jnp.where(odd, -mine, mine),
                        jnp.where(odd, pltpu.roll(mine, 1, 1), pltpu.roll(mine, W - 1, 1)),
                    ],
                    0,
                ).astype(BF)
                leading = jnp.where(lane < half, pltpu.roll(stacked, half, 1), stacked)
                masked = jnp.concatenate(
                    [jnp.where(same_q == 2 * i, leading, 0.0) for i in range(pairs)], 1
                )
                exchange = dot(trailing, masked.astype(BF))
            at = sub % pairs * W
            totals.append(jnp.concatenate([t_re, t_im], 0) - exchange[:, at : at + W])
        spot = shift_down(iota((2 * nb, W), 1), na) & (nz - 1)
        cols = pl.ds(pl.multiple_of(chunk * W, W), W)
        for z in range(nz):
            moved = shifted(totals[0], -na * z)
            for sub in range(1, nz):
                moved = jnp.where(spot == sub, shifted(totals[sub], na * (sub - z)), moved)
            tsend[z, :, cols] = moved.astype(BF)
        for dz in range(1, nz):
            t_copy(dz, chunk).start()
        return carry

    chunks = nq // nchunk
    lax.fori_loop(0, chunks, measure_chunk, 0)

    total = dot_nt(tsend[zz], sel_out[...])
    for dz in range(1, nz):
        for chunk in range(chunks):
            t_copy(dz, chunk).wait_recv()
        total = total + dot_nt(trecv[dz], sel_out[...])
    out_ref[...] = total

    for slot in plane:
        st_copy(0, slot, near).wait_send()
        lr_copy(lr.at[0], slot, near).wait_send()
    for dz in range(1, nz):
        for chunk in range(chunks):
            t_copy(dz, chunk).wait_send()


def order_result(dense_ref, out_ref):
    parts, na, nq, nb = out_ref.shape
    for c in range(parts):
        out_ref[c] = dense_ref[c * nb : (c + 1) * nb, :].T.reshape(na, nq, nb)


def kernel_body(
    vertex_matrix, vertex_site, vertex_time, vertex_spin, free_green, plus_table, cross_table
):
    nblk = lax.axis_size("blk")
    ngroup = lax.axis_size("group")
    nv = vertex_matrix.shape[-1]
    nq = plus_table.shape[0]
    nz = nblk // INNER
    na = W // nblk
    nb = W // ngroup
    nw = INNER * ngroup
    npair = nq // 2
    chunks = nq // (W // na)
    vmem = pl.BlockSpec(memory_space=pltpu.VMEM)
    dma = pltpu.SemaphoreType.DMA
    out = pl.pallas_call(
        functools.partial(kernel, nblk, ngroup),
        out_shape=jax.ShapeDtypeStruct((2 * nb, na * nq), F32),
        in_specs=[pl.BlockSpec(memory_space=pltpu.HBM)] * 7,
        out_specs=vmem,
        scratch_shapes=[
            pltpu.VMEM(vertex_site.shape, jnp.int32),
            pltpu.VMEM(vertex_time.shape, jnp.int32),
            pltpu.VMEM(vertex_spin.shape, jnp.int32),
            pltpu.VMEM(free_green.shape, F32),
            pltpu.VMEM(plus_table.shape, jnp.int32),
            pltpu.VMEM(cross_table.shape, jnp.int32),
            pltpu.VMEM((nv, nv), BF),
            pltpu.VMEM((4 * W, nv), BF),
            pltpu.VMEM((nw, 2 * W, W), BF),
            pltpu.VMEM((nw, W, W), BF),
            pltpu.VMEM((nw // CORES, W, W), BF),
            pltpu.VMEM((nq * nb, W), BF),
            pltpu.VMEM((npair, 2 * W, W), BF),
            pltpu.VMEM((na * nq, nq * na), BF),
            pltpu.VMEM((nq, W), F32),
            pltpu.VMEM((nw, 2, nb, W), F32),
            pltpu.VMEM((npair, nw, 2, nb, 2 * W), BF),
            pltpu.VMEM((nz, 2 * nb, nq * na), BF),
            pltpu.VMEM((nz, 2 * nb, nq * na), BF),
            dma((6,)),
            dma,
            dma((nw,)),
            dma((nw,)),
            dma((nw,)),
            dma((nw,)),
            dma((nz, chunks)),
            dma((nz, chunks)),
        ],
        compiler_params=pltpu.CompilerParams(
            collective_id=0, has_side_effects=True, vmem_limit_bytes=VMEM_BYTES - 1024 * 1024
        ),
    )(
        vertex_site,
        vertex_time,
        vertex_spin,
        free_green,
        plus_table,
        cross_table,
        vertex_matrix[0],
    )
    return pl.pallas_call(
        order_result,
        out_shape=jax.ShapeDtypeStruct((2, na, nq, nb), F32),
        in_specs=[vmem],
        out_specs=vmem,
        compiler_params=pltpu.CompilerParams(vmem_limit_bytes=VMEM_BYTES - 1024 * 1024),
    )(out)


def fits(mesh):
    nblk, ngroup = mesh.shape["blk"], mesh.shape["group"]
    if nblk % INNER or W % nblk or W % ngroup:
        return False
    nz, na, nb = nblk // INNER, W // nblk, W // ngroup
    return nz == 4 and ngroup % CORES == 0 and 2 * nz * na == W and 4 * nb == W and na % 16 == 0 and nb % 16 == 0


def solution(mesh):
    in_specs = (
        P(("blk", "group"), None, None),
        P(("blk", "group"), None),
        P(("blk", "group"), None),
        P(("blk", "group"), None),
        P(),
        P(),
        P("blk", None),
    )
    out_specs = P(None, "blk", None, "group")

    def chosen(*args):
        matrix, plus = args[0], args[5]
        small = fits(mesh) and PARTS * plus.shape[0] == W and matrix.shape[-1] % 128 == 0
        return (kernel_body if small else plain_body)(*args)

    return jax.shard_map(chosen, mesh=mesh, in_specs=in_specs, out_specs=out_specs, check_vma=False)
```

```python
import functools
import math

import jax
import jax.numpy as jnp
from jax import lax
from jax.experimental import pallas as pl
from jax.experimental.pallas import tpu as pltpu
from jax.sharding import PartitionSpec as P

LX = 4
NW = 8
W = 128
NV = 1152
NT = 1024


def phases(site_ids, time_ids):
    points = jnp.arange(W, dtype=jnp.int32)
    moment = points // NW
    freq_index = points % NW
    kx_part = moment % LX
    ky_part = moment // LX
    rx_part = site_ids % LX
    ry_part = site_ids // LX
    winding = (2 * freq_index + 1)[:, None] * time_ids[None, :] + 2 * NT // LX * (
        kx_part[:, None] * rx_part[None, :] + ky_part[:, None] * ry_part[None, :]
    )
    winding = winding % (2 * NT)
    return winding.astype(jnp.float32) * (math.pi / NT)


def green_pair(matrix, site_ids, time_ids, spin_ids, free_green):
    angles = phases(site_ids, time_ids)
    cosine = jnp.cos(angles)
    sine_part = jnp.sin(angles)
    spin_up = (spin_ids == 0).astype(jnp.float32)[None, :]
    spin_down = (spin_ids == 1).astype(jnp.float32)[None, :]
    fourier_rows = jnp.concatenate(
        [cosine * spin_up, sine_part * spin_up, cosine * spin_down, sine_part * spin_down], 0
    ).astype(jnp.bfloat16)
    projected = jnp.dot(fourier_rows, matrix, preferred_element_type=jnp.float32).astype(
        jnp.bfloat16
    )
    norm_factor = 1.0 / math.sqrt(NV)
    real_free = free_green[0]
    imag_free = free_green[1]
    greens = []
    for spin_index in range(2):
        offset = 2 * W * spin_index
        cosine_rows = fourier_rows[offset : offset + W]
        sine_rows = fourier_rows[offset + W : offset + 2 * W]
        proj_real = projected[offset : offset + W]
        proj_imag = projected[offset + W : offset + 2 * W]
        left_block = jnp.concatenate(
            [
                jnp.concatenate([proj_real, proj_imag], 1),
                jnp.concatenate([proj_imag, -proj_real], 1),
            ],
            0,
        )
        right_block = jnp.concatenate([cosine_rows, sine_rows], 1)
        kernel = lax.dot_general(
            left_block, right_block, (((1,), (1,)), ((), ())), preferred_element_type=jnp.float32
        )
        kernel_real = kernel[:W]
        kernel_imag = kernel[W:]
        half_real = real_free[:, None] * kernel_real - imag_free[:, None] * kernel_imag
        half_imag = real_free[:, None] * kernel_imag + imag_free[:, None] * kernel_real
        green_real = (
            -(half_real * real_free[None, :] - half_imag * imag_free[None, :]) * norm_factor
        )
        green_imag = (
            -(half_real * imag_free[None, :] + half_imag * real_free[None, :]) * norm_factor
        )
        greens.append(jnp.stack([green_real, green_imag], 0))
    green_sum = (greens[0] + greens[1]).astype(jnp.bfloat16)
    return (green_sum, greens[0].astype(jnp.bfloat16), greens[1].astype(jnp.bfloat16))


def direct_terms(sums_piece, perm_row):
    column_ids = jnp.arange(sums_piece.shape[-1], dtype=jnp.int32)
    selector = (perm_row[:, None] == column_ids[None, :]).astype(jnp.bfloat16)
    halfway = jnp.einsum(
        "aj,kcbj->kcab", selector, sums_piece, preferred_element_type=jnp.float32
    ).astype(jnp.bfloat16)
    partner = jnp.einsum("kcaj,bj->kcab", halfway, selector, preferred_element_type=jnp.float32)
    local_copy = sums_piece.astype(jnp.float32)
    real_part = jnp.sum(local_copy[:, 0] * partner[:, 0] - local_copy[:, 1] * partner[:, 1], axis=0)
    imag_part = jnp.sum(local_copy[:, 0] * partner[:, 1] + local_copy[:, 1] * partner[:, 0], axis=0)
    return jnp.stack([real_part, imag_part], 0)


def copy_exchange(up_piece, down_piece, perm_row):
    column_ids = jnp.arange(up_piece.shape[-1], dtype=jnp.int32)
    spin_pieces = jnp.concatenate([up_piece, down_piece], 0)
    lead_values = spin_pieces[:, :, column_ids, perm_row]
    trail_values = spin_pieces[:, :, perm_row, column_ids]
    real_part = jnp.einsum(
        "ka,kb->ab", lead_values[:, 0], trail_values[:, 0], preferred_element_type=jnp.float32
    ) - jnp.einsum(
        "ka,kb->ab", lead_values[:, 1], trail_values[:, 1], preferred_element_type=jnp.float32
    )
    imag_part = jnp.einsum(
        "ka,kb->ab", lead_values[:, 0], trail_values[:, 1], preferred_element_type=jnp.float32
    ) + jnp.einsum(
        "ka,kb->ab", lead_values[:, 1], trail_values[:, 0], preferred_element_type=jnp.float32
    )
    return jnp.stack([real_part, imag_part], 0)


def plain_body(vertex_matrix, vertex_site, vertex_time, vertex_spin, free_green, plus_table, cross_table):
    green_sum, green_up, green_down = green_pair(
        vertex_matrix[0], vertex_site[0], vertex_time[0], vertex_spin[0], free_green
    )
    slices = plus_table.shape[0] // lax.axis_size("blk")
    owned_perms = lax.dynamic_slice_in_dim(plus_table, lax.axis_index("blk") * slices, slices, 0)
    sums_piece = lax.all_gather(green_sum[None], "blk", axis=0, tiled=True)
    up_piece = lax.all_gather(green_up[None], "blk", axis=0, tiled=True)
    down_piece = lax.all_gather(green_down[None], "blk", axis=0, tiled=True)

    def one_slice(perm_row):
        return direct_terms(sums_piece, perm_row) - copy_exchange(up_piece, down_piece, perm_row)

    transfer = jnp.swapaxes(lax.map(one_slice, owned_perms), 0, 1)
    shares = lax.psum_scatter(transfer, "group", scatter_dimension=3, tiled=True)
    regrouped = lax.all_to_all(shares, "blk", split_axis=2, concat_axis=1, tiled=True)
    row_ids = jnp.arange(regrouped.shape[2], dtype=jnp.int32)
    return regrouped[:, cross_table, row_ids[:, None], :]


BF = jnp.bfloat16
F32 = jnp.float32
MESH = pl.DeviceIdType.MESH
INNER = 2
CORES = 2
VMEM_BYTES = 64 * 1024 * 1024
PARTS = 4


def iota(shape, dim):
    return lax.broadcasted_iota(jnp.int32, shape, dim)


def shift_down(value, divisor):
    return value >> (divisor.bit_length() - 1)


def one_hot(condition):
    return jnp.where(condition, 1.0, 0.0).astype(BF)


def dot(left, right):
    return jnp.dot(left, right, preferred_element_type=F32)


def dot_nt(left, right):
    return lax.dot_general(left, right, (((1,), (1,)), ((), ())), preferred_element_type=F32)


def kernel(
    nblk,
    ngroup,
    site_hbm,
    time_hbm,
    spin_hbm,
    free_hbm,
    plus_hbm,
    cross_hbm,
    matrix_hbm,
    out_ref,
    site_ref,
    time_ref,
    spin_ref,
    free_ref,
    plus_ref,
    cross_ref,
    matrix,
    rows,
    st,
    lr,
    lr_send,
    sel_b,
    sel_a,
    sel_out,
    prow,
    sb,
    halfway,
    tsend,
    trecv,
    small_sem,
    matrix_sem,
    st_send,
    st_recv,
    lr_send_sem,
    lr_recv,
    t_send,
    t_recv,
):
    small = [
        pltpu.make_async_copy(source, target, small_sem.at[place])
        for place, (source, target) in enumerate(
            [
                (site_hbm, site_ref),
                (time_hbm, time_ref),
                (spin_hbm, spin_ref),
                (free_hbm, free_ref),
                (plus_hbm, plus_ref),
                (cross_hbm, cross_ref),
            ]
        )
    ]
    for copy in small:
        copy.start()
    matrix_copy = pltpu.make_async_copy(matrix_hbm, matrix, matrix_sem)
    matrix_copy.start()

    nz = nblk // INNER
    na = W // nblk
    nb = W // ngroup
    nq = plus_ref.shape[0]
    half = na * nz
    npair = nq // 2
    nchunk = W // na
    nv = site_ref.shape[1]
    blk = lax.axis_index("blk")
    grp = lax.axis_index("group")
    zz = blk // INNER
    yy = blk % INNER
    nx = ngroup // CORES
    xx = grp // CORES
    core = grp % CORES
    near = nx * INNER
    plane = list(range(1, CORES * near))

    def plane_peer(slot):
        dc, dy, dx = slot // near, slot // nx % INNER, slot % nx
        return (
            zz * INNER + (yy + dy) % INNER,
            (xx + dx) % nx * CORES + (core + dc) % CORES,
        )

    def z_peer(dz):
        return (((zz + dz) % nz) * INNER + yy, grp)

    barrier = pltpu.get_barrier_semaphore()
    for slot in plane:
        pl.semaphore_signal(barrier, inc=1, device_id=plane_peer(slot), device_id_type=MESH)
    for dz in range(1, nz):
        pl.semaphore_signal(barrier, inc=1, device_id=z_peer(dz), device_id_type=MESH)

    for copy in small:
        copy.wait()

    quarter = NT // 2
    site = jnp.broadcast_to(site_ref[...], (2 * NW, nv))
    rx = site & (LX - 1)
    ry = shift_down(site, LX)
    ids = iota((2 * NW, nv), 0)
    freq = ids & (NW - 1)
    upper = shift_down(ids, NW)
    winding = (2 * freq + 1) * time_ref[...]
    turns = shift_down(winding + quarter // 2, quarter)
    rest = (winding - turns * quarter).astype(F32) * (math.pi / NT)
    square = rest * rest
    cosine = 1.0 + square * (
        -1 / 2
        + square
        * (1 / 24 + square * (-1 / 720 + square * (1 / 40320 + square * (-1 / 3628800))))
    )
    sine = rest + rest * square * (
        -1 / 6 + square * (1 / 120 + square * (-1 / 5040 + square * (1 / 362880)))
    )
    cosine = cosine.astype(BF)
    sine = sine.astype(BF)

    def unit(amount):
        amount = amount & 3
        real = jnp.where(amount == 0, 1.0, jnp.where(amount == 2, -1.0, 0.0))
        imag = jnp.where(amount == 1, 1.0, jnp.where(amount == 3, -1.0, 0.0))
        return real.astype(BF), imag.astype(BF)

    def turn(value, by):
        return (value[0] * by[0] - value[1] * by[1], value[1] * by[0] + value[0] * by[1])

    spin = jnp.broadcast_to(spin_ref[...], (2 * NW, nv))
    up = one_hot(spin == 0)
    down = one_hot(spin == 1)
    across = [unit((kx + upper) * rx) for kx in range(0, LX, 2)]
    for ky in range(W // NW // LX):
        base = turn((cosine, sine), unit(turns + ky * ry))
        for place, by in enumerate(across):
            c_both, s_both = turn(base, by)
            at = (ky * LX + 2 * place) * NW
            rows[pl.ds(at, 2 * NW), :] = c_both * up
            rows[pl.ds(W + at, 2 * NW), :] = s_both * up
            rows[pl.ds(2 * W + at, 2 * NW), :] = c_both * down
            rows[pl.ds(3 * W + at, 2 * NW), :] = s_both * down

    matrix_copy.wait()
    projected = dot(rows[...], matrix[...]).astype(BF)
    kern = [
        dot_nt(projected[2 * W * s : 2 * W * (s + 1)], rows[2 * W * s : 2 * W * (s + 1), :])
        for s in range(2)
    ]

    ga_re = jnp.broadcast_to(free_ref[0:1, :], (W, W))
    ga_im = jnp.broadcast_to(free_ref[1:2, :], (W, W))
    gb_re, gb_im = ga_re, ga_im
    ga_re = ga_re.T
    ga_im = ga_im.T
    norm_factor = 1.0 / math.sqrt(NV)
    greens = []
    for s in range(2):
        k_re = kern[s][:W, :W] + kern[s][W:, W:]
        k_im = kern[s][W:, :W] - kern[s][:W, W:]
        h_re = ga_re * k_re - ga_im * k_im
        h_im = ga_re * k_im + ga_im * k_re
        greens.append(-(h_re * gb_re - h_im * gb_im) * norm_factor)
        greens.append(-(h_re * gb_im + h_im * gb_re) * norm_factor)
    turned = [g.T for g in greens]
    st[0, :W, :] = (turned[0] + turned[2]).astype(BF)
    st[0, W:, :] = (turned[1] + turned[3]).astype(BF)

    pl.semaphore_wait(barrier, len(plane) + nz - 1)

    def st_copy(source, slot, steps):
        return pltpu.make_async_remote_copy(
            src_ref=st.at[source],
            dst_ref=st.at[slot],
            send_sem=st_send.at[slot],
            recv_sem=st_recv.at[slot],
            device_id=plane_peer(steps),
            device_id_type=MESH,
        )

    def lr_copy(source, slot, steps):
        return pltpu.make_async_remote_copy(
            src_ref=source,
            dst_ref=lr.at[slot],
            send_sem=lr_send_sem.at[slot],
            recv_sem=lr_recv.at[slot],
            device_id=plane_peer(steps),
            device_id_type=MESH,
        )

    def lr_for(slot):
        dy, dx = slot // nx % INNER, slot % nx
        return lr_send.at[(yy + dy) % INNER * nx + (xx + dx) % nx]

    for slot in range(near - 1, 0, -1):
        st_copy(0, slot, slot).start()
    st_copy(0, near, near).start()

    greens = [g.astype(BF).astype(F32) for g in greens]
    turned = [g.astype(BF).astype(F32) for g in turned]
    plus = plus_ref[...].astype(F32)
    plus_turned = jnp.concatenate([plus, jnp.zeros((W - nq, W), F32)], 0).T
    expand = one_hot(shift_down(iota((W, W), 1), PARTS) == iota((W, W), 0))
    index = dot(plus_turned.astype(BF), expand).astype(jnp.int32)
    lane = iota((W, W), 1)
    part = lane & (PARTS - 1)

    def choose(values):
        picked = values[0]
        for g in range(1, PARTS):
            picked = jnp.where(part == g, values[g], picked)
        return picked

    lead = choose([jnp.take_along_axis(g, index, axis=1) for g in greens])
    trail = [jnp.take_along_axis(g, index, axis=1) for g in turned]
    trail = choose(trail).T
    order = [INNER * z + y for y in range(INNER) for z in range(nz)]
    lead = jnp.concatenate([lead[na * i : na * (i + 1)] for i in order], 0).T

    def shifted(value, by):
        by = by % W
        return value if by == 0 else pltpu.roll(value, by, 1)

    for x in range(nx):
        left = shifted(trail, -half * x)
        for y in range(INNER):
            joined = jnp.where(lane < half, left, shifted(lead, half - half * y))
            lr_send[y * nx + x] = joined.astype(BF)
    for slot in reversed(plane):
        lr_copy(lr_for(slot), slot, slot).start()
    lr[0] = lr_send[yy * nx + xx]

    plus_bf = plus.astype(BF)
    my_b = one_hot(iota((nb, W), 1) == iota((nb, W), 0) + nb * grp)
    plus_b = dot_nt(my_b, plus_bf).astype(jnp.int32)
    for q in range(nq):
        column = jnp.broadcast_to(plus_b[:, q : q + 1], (nb, W))
        sel_b[pl.ds(q * nb, nb), :] = one_hot(column == iota((nb, W), 1))
    place = shift_down(lane & (half - 1), na) * (na * INNER) + na * yy + (lane & (na - 1))
    my_a = one_hot(iota((W, W), 0) == place)
    prow[...] = dot(plus_bf, my_a)

    def pair_selector(pair, carry):
        first = prow[pl.ds(2 * pair, 1), :]
        second = prow[pl.ds(2 * pair + 1, 1), :]
        low = lane < half
        hit = iota((W, W), 0) == jnp.where(
            low, jnp.broadcast_to(first, (W, W)), jnp.broadcast_to(second, (W, W))
        ).astype(jnp.int32)
        sel_a[pair, :W, :] = one_hot(hit & low)
        sel_a[pair, W:, :] = one_hot(hit & (lane >= half))
        return carry

    lax.fori_loop(0, npair, pair_selector, 0)

    same = one_hot(iota((nq, nq), 0) == iota((nq, nq), 1))
    crossing = dot_nt(same, cross_ref[...].astype(F32).astype(BF)).astype(jnp.int32)
    crossing = (
        shift_down(crossing, nchunk) * W
        + (crossing & 1) * half
        + (shift_down(crossing, 2) & (nz - 1)) * na
    )
    for r in range(na):
        column = jnp.broadcast_to(crossing[:, r : r + 1] + r, (nq, nq * na))
        sel_out[pl.ds(r * nq, nq), :] = one_hot(column == iota((nq, nq * na), 1))

    def first_selection(slot):
        picked = dot_nt(sel_b[...], st[slot]).astype(BF)
        for c in range(2):
            mine = st[slot, pl.ds(pl.multiple_of(c * W + nb * grp, nb), nb), :]
            sb[slot, c] = dot(mine, my_a)
            for q in range(nq):
                halfway[q // 2, slot, c, :, pl.ds((q % 2) * W, W)] = picked[
                    q * nb : (q + 1) * nb, c * W : (c + 1) * W
                ]

    def own_chip(step, carry):
        @pl.when(step > 0)
        def _():
            st_copy(0, near, near).wait_recv()

        first_selection(step * near)
        return carry

    def same_core(step, carry):
        st_copy(0, step, near).wait_recv()
        st_copy(step, near + step, near).start()
        return carry

    def peers(step, carry):
        first_selection(step)
        return carry

    def forwarded(step, carry):
        st_copy(0, step, near).wait_recv()
        first_selection(step)
        return carry

    lax.fori_loop(0, CORES, own_chip, 0)
    lax.fori_loop(1, near, same_core, 0)
    lax.fori_loop(1, near, peers, 0)
    lax.fori_loop(near + 1, CORES * near, forwarded, 0)

    for slot in plane:
        lr_copy(lr.at[0], slot, near).wait_recv()

    nw = len(plane) + 1
    four = W // (nw * PARTS)
    depth = four * PARTS

    def t_copy(dz, chunk):
        cols = pl.ds(pl.multiple_of(chunk * W, W), W)
        return pltpu.make_async_remote_copy(
            src_ref=tsend.at[(zz + dz) % nz, :, cols],
            dst_ref=trecv.at[dz, :, cols],
            send_sem=t_send.at[dz, chunk],
            recv_sem=t_recv.at[dz, chunk],
            device_id=z_peer(dz),
            device_id_type=MESH,
        )

    same_q = shift_down(iota((W, W), 0) & (depth - 1), PARTS) - shift_down(lane, half)

    def measure_chunk(chunk, carry):
        totals = []
        for sub in range(nz):
            pair = chunk * nz + sub
            partner = dot(halfway[pair].reshape(nw * 2 * nb, 2 * W), sel_a[pair])
            t_re = jnp.zeros((nb, W), F32)
            t_im = jnp.zeros((nb, W), F32)
            for w in range(nw):
                s_re = sb[w, 0]
                s_im = sb[w, 1]
                p_re = partner[2 * nb * w : 2 * nb * w + nb]
                p_im = partner[2 * nb * w + nb : 2 * nb * (w + 1)]
                t_re = t_re + (s_re * p_re - s_im * p_im)
                t_im = t_im + (s_re * p_im + s_im * p_re)
            pairs = four // 2
            if sub % pairs == 0:
                start = pl.multiple_of((chunk * (nz // pairs) + sub // pairs) * depth, depth)
                stacked = lr[:, pl.ds(start, depth), :].reshape(W, W).astype(F32)
                turned_back = stacked.T
                mine = jnp.where(core == 0, turned_back[:nb], turned_back[nb : 2 * nb])
                odd = (iota((nb, W), 1) & 1) == 1
                trailing = jnp.concatenate(
                    [
                        jnp.where(odd, -mine, mine),
                        jnp.where(odd, pltpu.roll(mine, 1, 1), pltpu.roll(mine, W - 1, 1)),
                    ],
                    0,
                ).astype(BF)
                leading = jnp.where(lane < half, pltpu.roll(stacked, half, 1), stacked)
                masked = jnp.concatenate(
                    [jnp.where(same_q == 2 * i, leading, 0.0) for i in range(pairs)], 1
                )
                exchange = dot(trailing, masked.astype(BF))
            at = sub % pairs * W
            totals.append(jnp.concatenate([t_re, t_im], 0) - exchange[:, at : at + W])
        spot = shift_down(iota((2 * nb, W), 1), na) & (nz - 1)
        cols = pl.ds(pl.multiple_of(chunk * W, W), W)
        for z in range(nz):
            moved = shifted(totals[0], -na * z)
            for sub in range(1, nz):
                moved = jnp.where(spot == sub, shifted(totals[sub], na * (sub - z)), moved)
            tsend[z, :, cols] = moved.astype(BF)
        for dz in range(1, nz):
            t_copy(dz, chunk).start()
        return carry

    chunks = nq // nchunk
    lax.fori_loop(0, chunks, measure_chunk, 0)

    total = dot_nt(tsend[zz], sel_out[...])
    for dz in range(1, nz):
        for chunk in range(chunks):
            t_copy(dz, chunk).wait_recv()
        total = total + dot_nt(trecv[dz], sel_out[...])
    out_ref[...] = total

    for slot in plane:
        st_copy(0, slot, near).wait_send()
        lr_copy(lr.at[0], slot, near).wait_send()
    for dz in range(1, nz):
        for chunk in range(chunks):
            t_copy(dz, chunk).wait_send()


def order_result(dense_ref, out_ref):
    parts, na, nq, nb = out_ref.shape
    for c in range(parts):
        out_ref[c] = dense_ref[c * nb : (c + 1) * nb, :].T.reshape(na, nq, nb)


def kernel_body(
    vertex_matrix, vertex_site, vertex_time, vertex_spin, free_green, plus_table, cross_table
):
    nblk = lax.axis_size("blk")
    ngroup = lax.axis_size("group")
    nv = vertex_matrix.shape[-1]
    nq = plus_table.shape[0]
    nz = nblk // INNER
    na = W // nblk
    nb = W // ngroup
    nw = INNER * ngroup
    npair = nq // 2
    chunks = nq // (W // na)
    vmem = pl.BlockSpec(memory_space=pltpu.VMEM)
    dma = pltpu.SemaphoreType.DMA
    out = pl.pallas_call(
        functools.partial(kernel, nblk, ngroup),
        out_shape=jax.ShapeDtypeStruct((2 * nb, na * nq), F32),
        in_specs=[pl.BlockSpec(memory_space=pltpu.HBM)] * 7,
        out_specs=vmem,
        scratch_shapes=[
            pltpu.VMEM(vertex_site.shape, jnp.int32),
            pltpu.VMEM(vertex_time.shape, jnp.int32),
            pltpu.VMEM(vertex_spin.shape, jnp.int32),
            pltpu.VMEM(free_green.shape, F32),
            pltpu.VMEM(plus_table.shape, jnp.int32),
            pltpu.VMEM(cross_table.shape, jnp.int32),
            pltpu.VMEM((nv, nv), BF),
            pltpu.VMEM((4 * W, nv), BF),
            pltpu.VMEM((nw, 2 * W, W), BF),
            pltpu.VMEM((nw, W, W), BF),
            pltpu.VMEM((nw // CORES, W, W), BF),
            pltpu.VMEM((nq * nb, W), BF),
            pltpu.VMEM((npair, 2 * W, W), BF),
            pltpu.VMEM((na * nq, nq * na), BF),
            pltpu.VMEM((nq, W), F32),
            pltpu.VMEM((nw, 2, nb, W), F32),
            pltpu.VMEM((npair, nw, 2, nb, 2 * W), BF),
            pltpu.VMEM((nz, 2 * nb, nq * na), BF),
            pltpu.VMEM((nz, 2 * nb, nq * na), BF),
            dma((6,)),
            dma,
            dma((nw,)),
            dma((nw,)),
            dma((nw,)),
            dma((nw,)),
            dma((nz, chunks)),
            dma((nz, chunks)),
        ],
        compiler_params=pltpu.CompilerParams(
            collective_id=0, has_side_effects=True, vmem_limit_bytes=VMEM_BYTES - 1024 * 1024
        ),
    )(
        vertex_site,
        vertex_time,
        vertex_spin,
        free_green,
        plus_table,
        cross_table,
        vertex_matrix[0],
    )
    return pl.pallas_call(
        order_result,
        out_shape=jax.ShapeDtypeStruct((2, na, nq, nb), F32),
        in_specs=[vmem],
        out_specs=vmem,
        compiler_params=pltpu.CompilerParams(vmem_limit_bytes=VMEM_BYTES - 1024 * 1024),
    )(out)


def fits(mesh):
    nblk, ngroup = mesh.shape["blk"], mesh.shape["group"]
    if nblk % INNER or W % nblk or W % ngroup:
        return False
    nz, na, nb = nblk // INNER, W // nblk, W // ngroup
    return nz == 4 and ngroup % CORES == 0 and 2 * nz * na == W and 4 * nb == W and na % 16 == 0 and nb % 16 == 0


def solution(mesh):
    in_specs = (
        P(("blk", "group"), None, None),
        P(("blk", "group"), None),
        P(("blk", "group"), None),
        P(("blk", "group"), None),
        P(),
        P(),
        P("blk", None),
    )
    out_specs = P(None, "blk", None, "group")

    def chosen(*args):
        matrix, plus = args[0], args[5]
        small = fits(mesh) and PARTS * plus.shape[0] == W and matrix.shape[-1] % 128 == 0
        return (kernel_body if small else plain_body)(*args)

    return jax.shard_map(chosen, mesh=mesh, in_specs=in_specs, out_specs=out_specs, check_vma=False)
```
